256 devices in a mesh: slab: 16 (over y, x), tile: 16 (over z, core).
Axes of the slice: x: 4, y: 4, z: 8, core: 2. Of those that a mesh axis runs over, the one named last changes fastest.
Arguments:
- sensitivity: float32 [64, 256, 1024], P('slab', 'tile'), may hold values from -32 to 32, as said below
- filtered_density: float32 [64, 256, 1024], P('slab', 'tile'), may hold values from 0 to 1
- passive_blocks: int32 [32, 128, 512], P('slab', 'tile'), may hold values 0 or 1
- history_steps: float32 [4, 64, 256, 1024], P(None, 'slab', 'tile'), may hold values from -40 to 40
- history_changes: float32 [4, 64, 256, 1024], P(None, 'slab', 'tile'), may hold values from -200 to 200
Outputs:
- direction: float32 [64, 256, 1024], P('slab', 'tile')
The draws below stay inside these ranges and needn't reach their ends.
Inputs may be any that keep to these rules, and one draw needn't show every extreme that they name: `sensitivity`: adjoint sensitivities.
All inputs are finite; a program needn't handle non-finite values. No bound on the sum of `passive_blocks` on one device may be relied on, other than what follows from the above.
Results may differ from the reference program's by a relative error of at most 0.0001.
Values sent between devices are 32-bit elements; how exact they have to be, the bound alone decides.
No kernel may reach another device: no remote copies, remote signals or barrier semaphores. Data moves between devices by JAX's collectives and lax.ppermute only.
A program may use at most 64 MiB of HBM per device.

```python
import math
import jax
import jax.numpy as jnp

NX = 1024
SWEEPS = 3
MEM = 4
NZ = 64
NY = 256


def smooth_modes(key):
    folded = jax.random.fold_in(key, 5)
    wave_key, phase_key = jax.random.split(folded, 2)
    waves = jax.random.randint(wave_key, (MEM, 3), 1, 3).astype(jnp.float32)
    phases = jax.random.uniform(phase_key, (MEM, 3), jnp.float32, 0.0, 1.0)
    depth_frac = jnp.arange(NZ, dtype=jnp.float32) / NZ
    row_frac = jnp.arange(NY, dtype=jnp.float32) / NY
    col_frac = jnp.arange(NX, dtype=jnp.float32) / NX
    two_pi = 2.0 * math.pi
    along_depth = jnp.cos(two_pi * (waves[:, 0:1] * depth_frac[None, :] + phases[:, 0:1]))
    along_rows = jnp.cos(two_pi * (waves[:, 1:2] * row_frac[None, :] + phases[:, 1:2]))
    along_cols = jnp.cos(two_pi * (waves[:, 2:3] * col_frac[None, :] + phases[:, 2:3]))
    return along_depth[:, :, None, None] * along_rows[:, None, :, None] * along_cols[:, None, None, :]


def history_pair(key):
    modes = smooth_modes(key)
    folded = jax.random.fold_in(key, 11)
    first = jax.random.fold_in(folded, 0)
    second = jax.random.fold_in(folded, 1)
    third = jax.random.fold_in(folded, 2)
    fifth = jax.random.fold_in(folded, 4)
    sixth = jax.random.fold_in(folded, 5)
    shape = (MEM, NZ, NY, NX)
    depth_frac = jnp.arange(NZ, dtype=jnp.float32) / NZ
    profile = jnp.exp(math.log(10.0) * depth_frac)[None, :, None, None]
    rough = jnp.clip(jax.random.normal(first, shape, jnp.float32), -4.0, 4.0)
    noise = jnp.clip(jax.random.normal(third, shape, jnp.float32), -4.0, 4.0)
    rowscale = jnp.ones((1, 1, NY, 1), jnp.float32)
    factor = jnp.exp(jax.random.uniform(second, shape, jnp.float32, -math.log(2.0), math.log(2.0)))
    ladder = jnp.exp(math.log(2.0) * (1.0 - 2.0 * jnp.arange(MEM, dtype=jnp.float32) / (MEM - 1)))
    order = jax.random.permutation(fifth, MEM)
    jitter = jnp.exp(jax.random.uniform(sixth, (MEM,), jnp.float32, -math.log(1.25), math.log(1.25)))
    member_scale = (ladder[order] * jitter)[:, None, None, None]
    steps = profile * rowscale * (modes + 0.6 * rough)
    changes = member_scale * factor * steps + 0.5 * noise * profile
    return (steps, changes)


def draw_history_steps(key, part):
    return history_pair(key)[0]


def draw_history_changes(key, part):
    return history_pair(key)[1]


def draw_sensitivity(key, part):
    modes = smooth_modes(key)
    folded = jax.random.fold_in(key, 23)
    first, second, third = jax.random.split(folded, 3)
    signs = (2 * jax.random.randint(first, (MEM,), 0, 2) - 1).astype(jnp.float32)
    weights = signs * jax.random.uniform(second, (MEM,), jnp.float32, 0.5, 1.5)
    smooth = weights[0] * modes[0]
    for member in range(1, MEM):
        smooth = smooth + weights[member] * modes[member]
    noise = jnp.clip(jax.random.normal(third, (NZ, NY, NX), jnp.float32), -4.0, 4.0)
    return 4.0 * smooth + 2.0 * noise


def plant(result, own_key, low, top_value):
    spot = [jax.random.randint(jax.random.fold_in(own_key, axis), (), 0, length) for axis, length in enumerate(result.shape)]
    longest = result.shape.index(max(result.shape))
    beside = spot[:longest] + [(spot[longest] + 1) % result.shape[longest]] + spot[longest + 1:]
    return result.at[tuple(spot)].set(low).at[tuple(beside)].set(top_value)


def levels(rng, shape, cuts, low, largest):
    def one(dim, shards_of):
        steps = jax.random.uniform(jax.random.fold_in(jax.random.fold_in(rng, 6), dim), (shards_of,), jnp.float32, low / len(cuts), largest / len(cuts))
        return jnp.repeat(jnp.exp(steps), shape[dim] // shards_of).reshape((-1,) + (1,) * (len(shape) - dim - 1))

    loudness = one(*cuts[0])
    for cut in cuts[1:]:
        loudness = loudness * one(*cut)
    return loudness


def setup_inputs(seed: int = 0) -> dict:
    arg_keys = jax.random.split(jax.random.key(seed), 6)
    sensitivity = draw_sensitivity(jax.random.fold_in(arg_keys[5], 71), 0)
    filtered_density = jnp.clip(1.0 * jax.random.uniform(arg_keys[1], (NZ, NY, NX), jnp.float32) ** levels(arg_keys[1], (NZ, NY, NX), ((0, 16), (1, 16)), -0.2, 0.2), 0.0, 1.0)
    passive_blocks = plant((jax.random.randint(arg_keys[2], (NZ // 2, NY // 2, NX // 2), 0, 4) < 1).astype(jnp.int32), jax.random.fold_in(arg_keys[2], 1), 0, 1)
    history_steps = draw_history_steps(jax.random.fold_in(arg_keys[5], 71), 0)
    history_changes = draw_history_changes(jax.random.fold_in(arg_keys[5], 71), 0)
    return dict(sensitivity=sensitivity, filtered_density=filtered_density, passive_blocks=passive_blocks, history_steps=history_steps, history_changes=history_changes)


radius_square = 4.0
sharpness = 8.0
threshold = 0.5


def expand_blocks(blocks):
    depth_n, rows_n, cols_n = blocks.shape
    spread = jnp.broadcast_to(blocks[:, None, :, None, :, None], (depth_n, 2, rows_n, 2, cols_n, 2))
    return spread.reshape(2 * depth_n, 2 * rows_n, 2 * cols_n)


def neighbour_sum(field):
    padded = jnp.pad(field, 1)
    total = padded[2:, 1:-1, 1:-1] + padded[:-2, 1:-1, 1:-1]
    total = total + padded[1:-1, 2:, 1:-1] + padded[1:-1, :-2, 1:-1]
    total = total + padded[1:-1, 1:-1, 2:] + padded[1:-1, 1:-1, :-2]
    return total


def reference(sensitivity, filtered_density, passive_blocks, history_steps, history_changes):
    denominator = jnp.tanh(sharpness * threshold) + jnp.tanh(sharpness * (1.0 - threshold))
    slope = sharpness * (1.0 - jnp.tanh(sharpness * (filtered_density - threshold)) ** 2) / denominator
    weighted = sensitivity * slope
    diagonal_value = 1.0 + 6.0 * radius_square
    iterate = weighted / diagonal_value
    for sweep_index in range(SWEEPS):
        iterate = (weighted + radius_square * neighbour_sum(iterate)) / diagonal_value
    passive = expand_blocks(passive_blocks).astype(jnp.float32)
    gradient = iterate * (1.0 - passive)
    curv = [jnp.sum(history_steps[member] * history_changes[member]) for member in range(MEM)]
    newest_yy = jnp.sum(history_changes[MEM - 1] * history_changes[MEM - 1])
    reduced = gradient
    alphas = [None] * MEM
    for member in reversed(range(MEM)):
        alphas[member] = jnp.sum(history_steps[member] * reduced) / curv[member]
        reduced = reduced - alphas[member] * history_changes[member]
    scaled = (curv[MEM - 1] / newest_yy) * reduced
    for member in range(MEM):
        betas = jnp.sum(history_changes[member] * scaled) / curv[member]
        scaled = scaled + (alphas[member] - betas) * history_steps[member]
    return -scaled
```

```python
import jax
import jax.numpy as jnp
from jax import lax
from jax.experimental import pallas as pl
from jax.experimental.pallas import tpu as pltpu
from jax.sharding import PartitionSpec as P

SWEEPS = 3
MEM = 4

radius_square = 4.0
sharpness = 8.0
threshold = 0.5
diagonal_value = 1.0 + 6.0 * radius_square
coupling = radius_square / diagonal_value

F32 = jnp.float32
LANES = 128
PAIRS = [(i, j) for i in range(MEM) for j in range(i, MEM)]
SY = {pair: n for n, pair in enumerate(PAIRS)}
YY = {pair: len(PAIRS) + n for n, pair in enumerate(PAIRS)}
SG = [2 * len(PAIRS) + n for n in range(MEM)]
YG = [2 * len(PAIRS) + MEM + n for n in range(MEM)]
SUMS = 32
ROWS_SENT = 24

VMEM = pl.BlockSpec(memory_space=pltpu.VMEM)


def kernel_params(mib):
    return pltpu.CompilerParams(vmem_limit_bytes=mib * 1024 * 1024)


def weight_kernel(sens_ref, dens_ref, u_ref, odd_ref, even_ref):
    slab_odd = lax.rem(lax.axis_index("slab"), 2)
    denominator = jnp.tanh(F32(sharpness * threshold)) + jnp.tanh(
        F32(sharpness * (1.0 - threshold))
    )
    for z in range(sens_ref.shape[0]):
        bend = jnp.tanh(sharpness * (dens_ref[z] - threshold))
        slope = sharpness * (1.0 - bend * bend) / denominator
        u_ref[z] = sens_ref[z] * slope / diagonal_value
    odd_ref[...] = u_ref[pl.ds(slab_odd, SWEEPS)]
    even_ref[...] = u_ref[pl.ds(1 - slab_odd, SWEEPS)]


def gram_kernel(steps_ref, changes_ref, passive_ref, sums_ref, keep_ref):
    depth, rows, cols = steps_ref.shape[1:]
    blocks = rows // 8

    def step(index, sums):
        z, block = index // blocks, lax.rem(index, blocks)
        row = pl.ds(pl.multiple_of(block * 8, 8), 8)
        sums = list(sums)
        for col in range(0, cols, LANES):
            lane = pl.ds(col, LANES)
            s = [steps_ref[i, z, row, lane] for i in range(MEM)]
            y = [changes_ref[i, z, row, lane] for i in range(MEM)]
            for i, j in PAIRS:
                sums[SY[i, j]] += s[i] * y[j]
                sums[YY[i, j]] += y[i] * y[j]
        return tuple(sums)

    zero = jnp.zeros((8, LANES), F32)
    sums = lax.fori_loop(0, depth * blocks, step, (zero,) * (2 * len(PAIRS)))
    for n, value in enumerate(sums):
        sums_ref[n : n + 1, :] = jnp.sum(value, axis=0, keepdims=True)

    def doubling(shape, dim):
        place = lax.broadcasted_iota(jnp.int32, shape, dim) // 2
        matches = place == lax.broadcasted_iota(jnp.int32, shape, 1 - dim)
        return matches.astype(F32).astype(jnp.bfloat16)

    half_rows = passive_ref.shape[1]
    twice_rows = doubling((2 * half_rows, half_rows), 0)
    twice_cols = doubling((LANES, 2 * LANES), 1)
    for z in range(passive_ref.shape[0]):
        blocks = passive_ref[z].astype(F32).astype(jnp.bfloat16)
        blocks = jnp.dot(twice_rows, blocks, preferred_element_type=F32).astype(jnp.bfloat16)
        for col in range(0, passive_ref.shape[2], LANES):
            wide = jnp.dot(
                blocks[:, col : col + LANES], twice_cols, preferred_element_type=F32
            )
            keep_ref[z, :, 2 * col : 2 * col + 2 * LANES] = 1.0 - wide


def pack_kernel(u_ref, odd_ref, even_ref, row_odd_ref, row_even_ref):
    depth, rows = u_ref.shape[:2]
    slab_odd = lax.rem(lax.axis_index("slab"), 2)
    tile_odd = lax.rem(lax.axis_index("tile"), 2)

    def pack(low_ref, high_ref, out_ref, top):
        for z in range(depth):
            start = rows - 3 if top else 0
            out_ref[3 * z : 3 * z + 3, :] = u_ref[z, start : start + 3, :]
        start = rows - 2 if top else 0
        out_ref[12:14, :] = low_ref[2, start : start + 2, :]
        out_ref[14:16, :] = high_ref[0, start : start + 2, :]
        start = rows - 1 if top else 0
        out_ref[16:17, :] = low_ref[1, start : start + 1, :]
        out_ref[17:18, :] = high_ref[1, start : start + 1, :]
        out_ref[18:24, :] = jnp.zeros((6, out_ref.shape[1]), F32)

    for parity in range(2):
        for top in range(2):

            @pl.when((slab_odd == parity) & (tile_odd == top))
            def _():
                low_ref, high_ref = (even_ref, odd_ref) if parity else (odd_ref, even_ref)
                pack(low_ref, high_ref, row_odd_ref, top == 1)
                pack(low_ref, high_ref, row_even_ref, top == 0)


def sweep_kernel(
    u_ref,
    odd_ref,
    even_ref,
    row_odd_ref,
    row_even_ref,
    keep_ref,
    steps_ref,
    changes_ref,
    sums_ref,
    grad_ref,
    send_ref,
    start_ref,
    one_ref,
    two_ref,
    total_ref,
):
    depth, rows, cols = u_ref.shape
    slab, tile = lax.axis_index("slab"), lax.axis_index("tile")
    slab_odd, tile_odd = lax.rem(slab, 2), lax.rem(tile, 2)
    inside = {
        "low_z": (slab > 0).astype(F32),
        "high_z": (slab < lax.axis_size("slab") - 1).astype(F32),
        "low_y": (tile > 0).astype(F32),
        "high_y": (tile < lax.axis_size("tile") - 1).astype(F32),
    }

    for z in range(depth):
        start_ref[3 + z, 8 : 8 + rows, :] = u_ref[z]

    def layers(low_ref, high_ref):
        for z in range(3):
            start_ref[z, 8 : 8 + rows, :] = low_ref[z] * inside["low_z"]
            start_ref[7 + z, 8 : 8 + rows, :] = high_ref[z] * inside["high_z"]

    def edge(from_ref, first, count, z, factor, high):
        to = 8 + rows if high else 8 - count
        start_ref[z, to : to + count, :] = from_ref[first : first + count, :] * factor

    def beside(from_ref, high):
        factor = inside["high_y" if high else "low_y"]
        for z in range(depth):
            edge(from_ref, 3 * z, 3, 3 + z, factor, high)
        low_factor, high_factor = factor * inside["low_z"], factor * inside["high_z"]
        edge(from_ref, 12, 2, 2, low_factor, high)
        edge(from_ref, 14, 2, 7, high_factor, high)
        edge(from_ref, 16, 1, 1, low_factor, high)
        edge(from_ref, 17, 1, 8, high_factor, high)

    for parity in range(2):

        @pl.when(slab_odd == parity)
        def _():
            layers(*((even_ref, odd_ref) if parity else (odd_ref, even_ref)))

        @pl.when(tile_odd == parity)
        def _():
            beside(row_odd_ref, parity == 1)
            beside(row_even_ref, parity == 0)

    column = lax.broadcasted_iota(jnp.int32, (8, cols), 1)
    first, last = column == 0, column == cols - 1

    def relax(from_ref, z, row):
        here = from_ref[z, row : row + 8, :]
        around = from_ref[z - 1, row : row + 8, :] + from_ref[z + 1, row : row + 8, :]
        if row == 0:
            below = pltpu.roll(here, 1, 0)
        else:
            below = from_ref[z, row - 1 : row + 7, :]
        if row == rows + 8:
            above = pltpu.roll(here, 7, 0)
        else:
            above = from_ref[z, row + 1 : row + 9, :]
        around += below + above
        around += jnp.where(first, 0.0, pltpu.roll(here, 1, 1))
        around += jnp.where(last, 0.0, pltpu.roll(here, cols - 1, 1))
        return start_ref[z, row : row + 8, :] + coupling * around

    def outside(z, row):
        factor = None
        if z < 3:
            factor = inside["low_z"]
        if z > 6:
            factor = inside["high_z"]
        edge_factor = inside["low_y"] if row < 8 else inside["high_y"] if row >= 8 + rows else None
        if factor is None or edge_factor is None:
            return edge_factor if factor is None else factor
        return factor * edge_factor

    def sweep(from_ref, to_ref, reach):
        for z in range(3 - reach, 7 + reach):
            beyond = max(3 - z, z - 6, 0)
            wide = reach - beyond > 0
            for row in range(0 if wide else 8, 8 + rows + (8 if wide else 0), 8):
                value = relax(from_ref, z, row)
                factor = outside(z, row)
                to_ref[z, row : row + 8, :] = value if factor is None else value * factor

    sweep(start_ref, one_ref, 2)
    sweep(one_ref, two_ref, 1)

    sums = [jnp.zeros((8, LANES), F32) for _ in range(2 * MEM)]
    for z in range(depth):
        for row in range(0, rows, 8):
            value = relax(two_ref, 3 + z, 8 + row) * keep_ref[z // 2, row : row + 8, :]
            grad_ref[z, row : row + 8, :] = value
            for col in range(0, cols, LANES):
                piece = value[:, col : col + LANES]
                for i in range(MEM):
                    sums[i] += steps_ref[i, z, row : row + 8, col : col + LANES] * piece
                    sums[MEM + i] += changes_ref[i, z, row : row + 8, col : col + LANES] * piece
    done = 2 * len(PAIRS)
    total_ref[0:done, :] = sums_ref[0:done, :]
    for n, value in enumerate(sums):
        total_ref[done + n : done + n + 1, :] = jnp.sum(value, axis=0, keepdims=True)
    total_ref[done + 2 * MEM :, :] = jnp.zeros((SUMS - done - 2 * MEM, LANES), F32)
    totals = jnp.sum(total_ref[...], axis=1, keepdims=True)
    diagonal = lax.broadcasted_iota(jnp.int32, (SUMS, LANES), 0) == lax.broadcasted_iota(
        jnp.int32, (SUMS, LANES), 1
    )
    line = jnp.sum(jnp.where(diagonal, totals, 0.0), axis=0, keepdims=True)
    send_ref[...] = jnp.broadcast_to(line, send_ref.shape)


def combine_kernel(all_ref, grad_ref, steps_ref, changes_ref, out_ref):
    depth, rows, cols = grad_ref.shape
    line = jnp.sum(all_ref[...], axis=0, keepdims=True)

    def entry(n):
        return jnp.broadcast_to(line[:, n : n + 1], (8, LANES))

    sy = {pair: entry(n) for pair, n in SY.items()}
    yy = {pair: entry(n) for pair, n in YY.items()}
    inverse = [1.0 / sy[i, i] for i in range(MEM)]
    alphas = [None] * MEM
    for i in reversed(range(MEM)):
        product = entry(SG[i])
        for j in range(i + 1, MEM):
            product -= alphas[j] * sy[i, j]
        alphas[i] = product * inverse[i]
    scale = sy[MEM - 1, MEM - 1] / yy[MEM - 1, MEM - 1]
    weights = [None] * MEM
    for i in range(MEM):
        product = entry(YG[i])
        for j in range(MEM):
            product -= alphas[j] * yy[min(i, j), max(i, j)]
        product *= scale
        for j in range(i):
            product += weights[j] * sy[j, i]
        weights[i] = alphas[i] - product * inverse[i]
    on_changes = [scale * alphas[i] for i in range(MEM)]
    for z in range(depth):
        for row in range(0, rows, 8):
            for col in range(0, cols, LANES):
                lane = slice(col, col + LANES)
                value = -scale * grad_ref[z, row : row + 8, lane]
                for i in range(MEM):
                    value += on_changes[i] * changes_ref[i, z, row : row + 8, lane]
                    value -= weights[i] * steps_ref[i, z, row : row + 8, lane]
                out_ref[z, row : row + 8, lane] = value


def swaps(count):
    even = [(i, i ^ 1) for i in range(count)]
    odd = [(i, (i + 1) % count if i % 2 else (i - 1) % count) for i in range(count)]
    return odd, even


def per_device(sensitivity, filtered_density, passive_blocks, history_steps, history_changes):
    shape = sensitivity.shape
    depth, rows, cols = shape
    like = jax.ShapeDtypeStruct
    layers = like((SWEEPS, rows, cols), F32)
    devices = lax.axis_size("slab") * lax.axis_size("tile")

    u, send_odd, send_even = pl.pallas_call(
        weight_kernel,
        out_shape=(like(shape, F32), layers, layers),
        in_specs=[VMEM] * 2,
        out_specs=[VMEM] * 3,
        compiler_params=kernel_params(8),
        name="weights",
    )(sensitivity, filtered_density)

    odd, even = swaps(lax.axis_size("slab"))
    got_odd = lax.ppermute(send_odd, "slab", odd)
    got_even = lax.ppermute(send_even, "slab", even)

    sums, keep = pl.pallas_call(
        gram_kernel,
        out_shape=(like((SUMS, LANES), F32), like((depth // 2, rows, cols), F32)),
        in_specs=[VMEM] * 3,
        out_specs=[VMEM] * 2,
        compiler_params=kernel_params(8),
        cost_estimate=pl.CostEstimate(flops=8_000_000, bytes_accessed=2_300_000, transcendentals=0),
        name="gram",
    )(history_steps, history_changes, passive_blocks)

    edges = like((ROWS_SENT, cols), F32)
    row_odd, row_even = pl.pallas_call(
        pack_kernel,
        out_shape=(edges, edges),
        in_specs=[VMEM] * 3,
        out_specs=[VMEM] * 2,
        compiler_params=kernel_params(8),
        name="edges",
    )(u, got_odd, got_even)
    odd, even = swaps(lax.axis_size("tile"))
    row_odd = lax.ppermute(row_odd, "tile", odd)
    row_even = lax.ppermute(row_even, "tile", even)

    padded = pltpu.VMEM((depth + 6, rows + 16, cols), F32)
    gradient, line = pl.pallas_call(
        sweep_kernel,
        out_shape=(like(shape, F32), like((devices, LANES), F32)),
        in_specs=[VMEM] * 9,
        out_specs=[VMEM] * 2,
        scratch_shapes=[padded, padded, padded, pltpu.VMEM((SUMS, LANES), F32)],
        compiler_params=kernel_params(16),
        name="sweeps",
    )(u, got_odd, got_even, row_odd, row_even, keep, history_steps, history_changes, sums)

    lines = lax.all_to_all(line, ("slab", "tile"), 0, 0, tiled=True)

    return pl.pallas_call(
        combine_kernel,
        out_shape=like(shape, F32),
        in_specs=[VMEM] * 4,
        out_specs=VMEM,
        compiler_params=kernel_params(8),
        name="combine",
    )(lines, gradient, history_steps, history_changes)


def solution(mesh):
    in_specs = (
        P("slab", "tile", None),
        P("slab", "tile", None),
        P("slab", "tile", None),
        P(None, "slab", "tile", None),
        P(None, "slab", "tile", None),
    )
    out_specs = P("slab", "tile", None)
    return jax.shard_map(
        per_device, mesh=mesh, in_specs=in_specs, out_specs=out_specs, check_vma=False
    )
```

```python
import jax
import jax.numpy as jnp
from jax import lax
from jax.experimental import pallas as pl
from jax.experimental.pallas import tpu as pltpu
from jax.sharding import PartitionSpec as P

SWEEPS = 3
MEM = 4

radius_square = 4.0
sharpness = 8.0
threshold = 0.5
diagonal_value = 1.0 + 6.0 * radius_square
coupling = radius_square / diagonal_value

F32 = jnp.float32
LANES = 128
PAIRS = [(i, j) for i in range(MEM) for j in range(i, MEM)]
SY = {pair: n for n, pair in enumerate(PAIRS)}
YY = {pair: len(PAIRS) + n for n, pair in enumerate(PAIRS)}
SG = [2 * len(PAIRS) + n for n in range(MEM)]
YG = [2 * len(PAIRS) + MEM + n for n in range(MEM)]
SUMS = 32
ROWS_SENT = 16

VMEM = pl.BlockSpec(memory_space=pltpu.VMEM)
HBM = pl.BlockSpec(memory_space=pltpu.HBM)


def kernel_params(mib):
    return pltpu.CompilerParams(vmem_limit_bytes=mib * 1024 * 1024)


def weight_kernel(
    sens_hbm,
    dens_hbm,
    u_ref,
    row_odd_ref,
    row_even_ref,
    odd_ref,
    even_ref,
    sens_ref,
    dens_ref,
    arrived,
):
    depth, rows, cols = u_ref.shape
    slab_odd = lax.rem(lax.axis_index("slab"), 2)
    tile_odd = lax.rem(lax.axis_index("tile"), 2)
    copies = [
        [
            pltpu.make_async_copy(from_ref.at[z], to_ref.at[z], arrived.at[n, z])
            for n, (from_ref, to_ref) in enumerate(((sens_hbm, sens_ref), (dens_hbm, dens_ref)))
        ]
        for z in range(depth)
    ]
    for pair in copies:
        for copy in pair:
            copy.start()
    denominator = jnp.tanh(F32(sharpness * threshold)) + jnp.tanh(
        F32(sharpness * (1.0 - threshold))
    )
    for z in range(depth):
        for copy in copies[z]:
            copy.wait()
        bend = jnp.tanh(sharpness * (dens_ref[z] - threshold))
        slope = sharpness * (1.0 - bend * bend) / denominator
        u_ref[z] = sens_ref[z] * slope / diagonal_value

    odd_ref[...] = u_ref[pl.ds(slab_odd, SWEEPS)]
    even_ref[...] = u_ref[pl.ds(1 - slab_odd, SWEEPS)]

    def edge_rows(to_ref, start):
        for z in range(depth):
            to_ref[3 * z : 3 * z + 3, :] = u_ref[z, start : start + 3, :]
        to_ref[3 * depth :, :] = jnp.zeros((to_ref.shape[0] - 3 * depth, cols), F32)

    for parity in range(2):

        @pl.when(tile_odd == parity)
        def _():
            edge_rows(row_odd_ref, rows - 3 if parity else 0)
            edge_rows(row_even_ref, 0 if parity else rows - 3)


def gram_kernel(
    steps_hbm,
    changes_hbm,
    passive_hbm,
    sums_ref,
    keep_ref,
    steps_ref,
    changes_ref,
    passive_ref,
    arrived,
    passive_arrived,
):
    depth, rows, cols = steps_ref.shape[1:]
    passive_copy = pltpu.make_async_copy(passive_hbm, passive_ref, passive_arrived)
    copies = [
        [
            pltpu.make_async_copy(from_ref.at[:, z], to_ref.at[:, z], arrived.at[n, z])
            for n, (from_ref, to_ref) in enumerate(
                ((steps_hbm, steps_ref), (changes_hbm, changes_ref))
            )
        ]
        for z in range(depth)
    ]
    passive_copy.start()
    for pair in copies:
        for copy in pair:
            copy.start()

    def doubling(shape, dim):
        place = lax.broadcasted_iota(jnp.int32, shape, dim) // 2
        matches = place == lax.broadcasted_iota(jnp.int32, shape, 1 - dim)
        return matches.astype(F32).astype(jnp.bfloat16)

    passive_copy.wait()
    half_rows = passive_ref.shape[1]
    twice_rows = doubling((2 * half_rows, half_rows), 0)
    twice_cols = doubling((LANES, 2 * LANES), 1)
    for z in range(passive_ref.shape[0]):
        blocks = passive_ref[z].astype(F32).astype(jnp.bfloat16)
        blocks = jnp.dot(twice_rows, blocks, preferred_element_type=F32).astype(jnp.bfloat16)
        for col in range(0, passive_ref.shape[2], LANES):
            wide = jnp.dot(
                blocks[:, col : col + LANES], twice_cols, preferred_element_type=F32
            )
            keep_ref[z, :, 2 * col : 2 * col + 2 * LANES] = 1.0 - wide

    sums = (jnp.zeros((8, LANES), F32),) * (2 * len(PAIRS))
    for z in range(depth):
        for copy in copies[z]:
            copy.wait()

        def step(block, sums):
            row = pl.ds(pl.multiple_of(block * 8, 8), 8)
            sums = list(sums)
            for col in range(0, cols, LANES):
                lane = pl.ds(col, LANES)
                s = [steps_ref[i, z, row, lane] for i in range(MEM)]
                y = [changes_ref[i, z, row, lane] for i in range(MEM)]
                for i, j in PAIRS:
                    sums[SY[i, j]] += s[i] * y[j]
                    sums[YY[i, j]] += y[i] * y[j]
            return tuple(sums)

        sums = lax.fori_loop(0, rows // 8, step, sums)
    for n, value in enumerate(sums):
        sums_ref[n : n + 1, :] = jnp.sum(value, axis=0, keepdims=True)


def corner_kernel(row_odd_ref, row_even_ref, rim_odd_ref, rim_even_ref):
    cols = rim_odd_ref.shape[1]
    depth = 4
    slab_odd = lax.rem(lax.axis_index("slab"), 2)
    tile_odd = lax.rem(lax.axis_index("tile"), 2)

    def pack(low_ref, high_ref, out_ref, top):
        near, second = (3 * (depth - 1), 3 * (depth - 2)) if top else (0, 3)
        out_ref[0:2, :] = low_ref[near + 1 : near + 3, :]
        out_ref[2:4, :] = high_ref[near : near + 2, :]
        out_ref[4:5, :] = low_ref[second + 2 : second + 3, :]
        out_ref[5:6, :] = high_ref[second : second + 1, :]
        out_ref[6:8, :] = jnp.zeros((2, cols), F32)

    for parity in range(2):
        for top in range(2):

            @pl.when((tile_odd == parity) & (slab_odd == top))
            def _():
                beside = (row_even_ref, row_odd_ref) if parity else (row_odd_ref, row_even_ref)
                pack(*beside, rim_odd_ref, top == 1)
                pack(*beside, rim_even_ref, top == 0)


def sweep_kernel(
    u_ref,
    odd_ref,
    even_ref,
    row_odd_ref,
    row_even_ref,
    rim_odd_ref,
    rim_even_ref,
    keep_ref,
    steps_ref,
    changes_ref,
    sums_ref,
    grad_ref,
    send_ref,
    start_ref,
    one_ref,
    two_ref,
    total_ref,
):
    depth, rows, cols = u_ref.shape
    slab, tile = lax.axis_index("slab"), lax.axis_index("tile")
    slab_odd, tile_odd = lax.rem(slab, 2), lax.rem(tile, 2)
    inside = {
        "low_z": (slab > 0).astype(F32),
        "high_z": (slab < lax.axis_size("slab") - 1).astype(F32),
        "low_y": (tile > 0).astype(F32),
        "high_y": (tile < lax.axis_size("tile") - 1).astype(F32),
    }

    for z in range(depth):
        start_ref[3 + z, 8 : 8 + rows, :] = u_ref[z]

    def edge(from_ref, first, count, z, factor, high):
        to = 8 + rows if high else 8 - count
        start_ref[z, to : to + count, :] = from_ref[first : first + count, :] * factor

    def below_and_above(from_ref, rim_ref, high):
        factor = inside["high_z" if high else "low_z"]
        for z in range(3):
            start_ref[7 * high + z, 8 : 8 + rows, :] = from_ref[z] * factor
        near, second = (7, 8) if high else (2, 1)
        low_factor, high_factor = factor * inside["low_y"], factor * inside["high_y"]
        edge(rim_ref, 0, 2, near, low_factor, False)
        edge(rim_ref, 2, 2, near, high_factor, True)
        edge(rim_ref, 4, 1, second, low_factor, False)
        edge(rim_ref, 5, 1, second, high_factor, True)

    def beside(from_ref, high):
        for z in range(depth):
            edge(from_ref, 3 * z, 3, 3 + z, inside["high_y" if high else "low_y"], high)

    for parity in range(2):

        @pl.when(slab_odd == parity)
        def _():
            below_and_above(odd_ref, rim_odd_ref, parity == 1)
            below_and_above(even_ref, rim_even_ref, parity == 0)

        @pl.when(tile_odd == parity)
        def _():
            beside(row_odd_ref, parity == 1)
            beside(row_even_ref, parity == 0)

    column = lax.broadcasted_iota(jnp.int32, (8, cols), 1)
    first, last = column == 0, column == cols - 1

    def relax(from_ref, z, row):
        here = from_ref[z, row : row + 8, :]
        around = from_ref[z - 1, row : row + 8, :] + from_ref[z + 1, row : row + 8, :]
        if row == 0:
            below = pltpu.roll(here, 1, 0)
        else:
            below = from_ref[z, row - 1 : row + 7, :]
        if row == rows + 8:
            above = pltpu.roll(here, 7, 0)
        else:
            above = from_ref[z, row + 1 : row + 9, :]
        around += below + above
        around += jnp.where(first, 0.0, pltpu.roll(here, 1, 1))
        around += jnp.where(last, 0.0, pltpu.roll(here, cols - 1, 1))
        return start_ref[z, row : row + 8, :] + coupling * around

    def outside(z, row):
        factor = None
        if z < 3:
            factor = inside["low_z"]
        if z > 6:
            factor = inside["high_z"]
        edge_factor = inside["low_y"] if row < 8 else inside["high_y"] if row >= 8 + rows else None
        if factor is None or edge_factor is None:
            return edge_factor if factor is None else factor
        return factor * edge_factor

    def sweep(from_ref, to_ref, reach):
        for z in range(3 - reach, 7 + reach):
            beyond = max(3 - z, z - 6, 0)
            wide = reach - beyond > 0
            for row in range(0 if wide else 8, 8 + rows + (8 if wide else 0), 8):
                value = relax(from_ref, z, row)
                factor = outside(z, row)
                to_ref[z, row : row + 8, :] = value if factor is None else value * factor

    sweep(start_ref, one_ref, 2)
    sweep(one_ref, two_ref, 1)

    sums = [jnp.zeros((8, LANES), F32) for _ in range(2 * MEM)]
    for z in range(depth):
        for row in range(0, rows, 8):
            value = relax(two_ref, 3 + z, 8 + row) * keep_ref[z // 2, row : row + 8, :]
            grad_ref[z, row : row + 8, :] = value
            for col in range(0, cols, LANES):
                piece = value[:, col : col + LANES]
                for i in range(MEM):
                    sums[i] += steps_ref[i, z, row : row + 8, col : col + LANES] * piece
                    sums[MEM + i] += changes_ref[i, z, row : row + 8, col : col + LANES] * piece
    done = 2 * len(PAIRS)
    total_ref[0:done, :] = sums_ref[0:done, :]
    for n, value in enumerate(sums):
        total_ref[done + n : done + n + 1, :] = jnp.sum(value, axis=0, keepdims=True)
    total_ref[done + 2 * MEM :, :] = jnp.zeros((SUMS - done - 2 * MEM, LANES), F32)
    totals = jnp.sum(total_ref[...], axis=1, keepdims=True)
    diagonal = lax.broadcasted_iota(jnp.int32, (SUMS, LANES), 0) == lax.broadcasted_iota(
        jnp.int32, (SUMS, LANES), 1
    )
    line = jnp.sum(jnp.where(diagonal, totals, 0.0), axis=0, keepdims=True)
    send_ref[...] = jnp.broadcast_to(line, send_ref.shape)


def combine_kernel(all_ref, grad_ref, steps_ref, changes_ref, out_hbm, out_ref, left):
    depth, rows, cols = grad_ref.shape
    line = jnp.sum(all_ref[...], axis=0, keepdims=True)

    def entry(n):
        return jnp.broadcast_to(line[:, n : n + 1], (8, LANES))

    sy = {pair: entry(n) for pair, n in SY.items()}
    yy = {pair: entry(n) for pair, n in YY.items()}
    inverse = [1.0 / sy[i, i] for i in range(MEM)]
    alphas = [None] * MEM
    for i in reversed(range(MEM)):
        product = entry(SG[i])
        for j in range(i + 1, MEM):
            product -= alphas[j] * sy[i, j]
        alphas[i] = product * inverse[i]
    scale = sy[MEM - 1, MEM - 1] / yy[MEM - 1, MEM - 1]
    weights = [None] * MEM
    for i in range(MEM):
        product = entry(YG[i])
        for j in range(MEM):
            product -= alphas[j] * yy[min(i, j), max(i, j)]
        product *= scale
        for j in range(i):
            product += weights[j] * sy[j, i]
        weights[i] = alphas[i] - product * inverse[i]
    on_changes = [scale * alphas[i] for i in range(MEM)]
    copies = [
        pltpu.make_async_copy(out_ref.at[z], out_hbm.at[z], left.at[z]) for z in range(depth)
    ]
    for z in range(depth):
        for row in range(0, rows, 8):
            for col in range(0, cols, LANES):
                lane = slice(col, col + LANES)
                value = -scale * grad_ref[z, row : row + 8, lane]
                for i in range(MEM):
                    value += on_changes[i] * changes_ref[i, z, row : row + 8, lane]
                    value -= weights[i] * steps_ref[i, z, row : row + 8, lane]
                out_ref[z, row : row + 8, lane] = value
        copies[z].start()
    for copy in copies:
        copy.wait()


def in_hbm(array):
    return pltpu.with_memory_space_constraint(array, pltpu.HBM)


def swaps(count):
    even = [(i, i ^ 1) for i in range(count)]
    odd = [(i, (i + 1) % count if i % 2 else (i - 1) % count) for i in range(count)]
    return odd, even


def per_device(sensitivity, filtered_density, passive_blocks, history_steps, history_changes):
    shape = sensitivity.shape
    depth, rows, cols = shape
    like = jax.ShapeDtypeStruct
    layers, rim, edges = (
        like(size, F32) for size in ((SWEEPS, rows, cols), (8, cols), (ROWS_SENT, cols))
    )
    devices = lax.axis_size("slab") * lax.axis_size("tile")

    u, row_odd, row_even, odd, even = pl.pallas_call(
        weight_kernel,
        out_shape=(like(shape, F32), edges, edges, layers, layers),
        in_specs=[HBM] * 2,
        out_specs=[VMEM] * 5,
        scratch_shapes=[
            pltpu.VMEM(shape, F32),
            pltpu.VMEM(shape, F32),
            pltpu.SemaphoreType.DMA((2, depth)),
        ],
        compiler_params=kernel_params(8),
        name="weights",
    )(in_hbm(sensitivity), in_hbm(filtered_density))

    slab_odd, slab_even = swaps(lax.axis_size("slab"))
    tile_odd, tile_even = swaps(lax.axis_size("tile"))
    odd = lax.ppermute(odd, "slab", slab_odd)
    even = lax.ppermute(even, "slab", slab_even)
    row_odd = lax.ppermute(row_odd, "tile", tile_odd)
    row_even = lax.ppermute(row_even, "tile", tile_even)

    rim_odd, rim_even = pl.pallas_call(
        corner_kernel,
        out_shape=(rim, rim),
        in_specs=[VMEM] * 2,
        out_specs=[VMEM] * 2,
        compiler_params=kernel_params(8),
        name="corners",
    )(row_odd, row_even)
    rim_odd = lax.ppermute(rim_odd, "slab", slab_odd)
    rim_even = lax.ppermute(rim_even, "slab", slab_even)

    history = like(history_steps.shape, F32)
    sums, keep, steps, changes = pl.pallas_call(
        gram_kernel,
        out_shape=(
            like((SUMS, LANES), F32),
            like((depth // 2, rows, cols), F32),
            history,
            history,
        ),
        in_specs=[HBM] * 3,
        out_specs=[VMEM] * 4,
        scratch_shapes=[
            pltpu.VMEM(passive_blocks.shape, jnp.int32),
            pltpu.SemaphoreType.DMA((2, depth)),
            pltpu.SemaphoreType.DMA,
        ],
        compiler_params=kernel_params(8),
        cost_estimate=pl.CostEstimate(flops=8_000_000, bytes_accessed=4_300_000, transcendentals=0),
        name="gram",
    )(in_hbm(history_steps), in_hbm(history_changes), in_hbm(passive_blocks))

    padded = pltpu.VMEM((depth + 6, rows + 16, cols), F32)
    gradient, line = pl.pallas_call(
        sweep_kernel,
        out_shape=(like(shape, F32), like((devices, LANES), F32)),
        in_specs=[VMEM] * 11,
        out_specs=[VMEM] * 2,
        scratch_shapes=[padded, padded, padded, pltpu.VMEM((SUMS, LANES), F32)],
        compiler_params=kernel_params(16),
        name="sweeps",
    )(u, odd, even, row_odd, row_even, rim_odd, rim_even, keep, steps, changes, sums)

    lines = lax.all_to_all(line, ("slab", "tile"), 0, 0, tiled=True)

    return pl.pallas_call(
        combine_kernel,
        out_shape=like(shape, F32),
        in_specs=[VMEM] * 4,
        out_specs=HBM,
        scratch_shapes=[pltpu.VMEM(shape, F32), pltpu.SemaphoreType.DMA((depth,))],
        compiler_params=kernel_params(8),
        name="combine",
    )(lines, gradient, steps, changes)


def solution(mesh):
    in_specs = (
        P("slab", "tile", None),
        P("slab", "tile", None),
        P("slab", "tile", None),
        P(None, "slab", "tile", None),
        P(None, "slab", "tile", None),
    )
    out_specs = P("slab", "tile", None)
    return jax.shard_map(
        per_device, mesh=mesh, in_specs=in_specs, out_specs=out_specs, check_vma=False
    )
```

```python
import jax
import jax.numpy as jnp
from jax import lax
from jax.experimental import pallas as pl
from jax.experimental.pallas import tpu as pltpu
from jax.sharding import PartitionSpec as P

SWEEPS = 3
MEM = 4

radius_square = 4.0
sharpness = 8.0
threshold = 0.5
diagonal_value = 1.0 + 6.0 * radius_square
coupling = radius_square / diagonal_value

F32 = jnp.float32
LANES = 128
PAIRS = [(i, j) for i in range(MEM) for j in range(i, MEM)]
SY = {pair: n for n, pair in enumerate(PAIRS)}
YY = {pair: len(PAIRS) + n for n, pair in enumerate(PAIRS)}
SG = [2 * len(PAIRS) + n for n in range(MEM)]
YG = [2 * len(PAIRS) + MEM + n for n in range(MEM)]
SUMS = 32
ROWS_SENT = 16

VMEM = pl.BlockSpec(memory_space=pltpu.VMEM)
HBM = pl.BlockSpec(memory_space=pltpu.HBM)


def kernel_params(mib):
    return pltpu.CompilerParams(vmem_limit_bytes=mib * 1024 * 1024)


def weight_kernel(
    sens_hbm,
    dens_hbm,
    u_ref,
    row_odd_ref,
    row_even_ref,
    odd_ref,
    even_ref,
    sens_ref,
    dens_ref,
    arrived,
):
    depth, rows, cols = u_ref.shape
    slab_odd = lax.rem(lax.axis_index("slab"), 2)
    tile_odd = lax.rem(lax.axis_index("tile"), 2)
    copies = [
        [
            pltpu.make_async_copy(from_ref.at[z], to_ref.at[z], arrived.at[n, z])
            for n, (from_ref, to_ref) in enumerate(((sens_hbm, sens_ref), (dens_hbm, dens_ref)))
        ]
        for z in range(depth)
    ]
    for pair in copies:
        for copy in pair:
            copy.start()
    denominator = jnp.tanh(F32(sharpness * threshold)) + jnp.tanh(
        F32(sharpness * (1.0 - threshold))
    )
    for z in range(depth):
        for copy in copies[z]:
            copy.wait()
        bend = jnp.tanh(sharpness * (dens_ref[z] - threshold))
        slope = sharpness * (1.0 - bend * bend) / denominator
        u_ref[z] = sens_ref[z] * slope / diagonal_value

    odd_ref[...] = u_ref[pl.ds(slab_odd, SWEEPS)]
    even_ref[...] = u_ref[pl.ds(1 - slab_odd, SWEEPS)]

    def edge_rows(to_ref, start):
        for z in range(depth):
            to_ref[3 * z : 3 * z + 3, :] = u_ref[z, start : start + 3, :]
        to_ref[3 * depth :, :] = jnp.zeros((to_ref.shape[0] - 3 * depth, cols), F32)

    for parity in range(2):

        @pl.when(tile_odd == parity)
        def _():
            edge_rows(row_odd_ref, rows - 3 if parity else 0)
            edge_rows(row_even_ref, 0 if parity else rows - 3)


def gram_kernel(
    steps_hbm,
    changes_hbm,
    passive_hbm,
    sums_ref,
    keep_ref,
    steps_ref,
    changes_ref,
    passive_ref,
    arrived,
    passive_arrived,
):
    depth, rows, cols = steps_ref.shape[1:]
    passive_copy = pltpu.make_async_copy(passive_hbm, passive_ref, passive_arrived)
    copies = [
        [
            pltpu.make_async_copy(from_ref.at[:, z], to_ref.at[:, z], arrived.at[n, z])
            for n, (from_ref, to_ref) in enumerate(
                ((steps_hbm, steps_ref), (changes_hbm, changes_ref))
            )
        ]
        for z in range(depth)
    ]
    passive_copy.start()
    for pair in copies:
        for copy in pair:
            copy.start()

    def doubling(shape, dim):
        place = lax.broadcasted_iota(jnp.int32, shape, dim) // 2
        matches = place == lax.broadcasted_iota(jnp.int32, shape, 1 - dim)
        return matches.astype(F32).astype(jnp.bfloat16)

    passive_copy.wait()
    half_rows = passive_ref.shape[1]
    twice_rows = doubling((2 * half_rows, half_rows), 0)
    twice_cols = doubling((LANES, 2 * LANES), 1)
    for z in range(passive_ref.shape[0]):
        blocks = passive_ref[z].astype(F32).astype(jnp.bfloat16)
        blocks = jnp.dot(twice_rows, blocks, preferred_element_type=F32).astype(jnp.bfloat16)
        for col in range(0, passive_ref.shape[2], LANES):
            wide = jnp.dot(
                blocks[:, col : col + LANES], twice_cols, preferred_element_type=F32
            )
            keep_ref[z, :, 2 * col : 2 * col + 2 * LANES] = 1.0 - wide

    sums = (jnp.zeros((8, LANES), F32),) * (2 * len(PAIRS))
    for z in range(depth):
        for copy in copies[z]:
            copy.wait()

        def step(block, sums):
            row = pl.ds(pl.multiple_of(block * 8, 8), 8)
            sums = list(sums)
            for col in range(0, cols, LANES):
                lane = pl.ds(col, LANES)
                s = [steps_ref[i, z, row, lane] for i in range(MEM)]
                y = [changes_ref[i, z, row, lane] for i in range(MEM)]
                for i, j in PAIRS:
                    sums[SY[i, j]] += s[i] * y[j]
                    sums[YY[i, j]] += y[i] * y[j]
            return tuple(sums)

        sums = lax.fori_loop(0, rows // 8, step, sums)
    for n, value in enumerate(sums):
        sums_ref[n : n + 1, :] = jnp.sum(value, axis=0, keepdims=True)


def corner_kernel(row_odd_ref, row_even_ref, sums_ref, rim_odd_ref, rim_even_ref):
    cols = rim_odd_ref.shape[1]
    depth = 4
    slab_odd = lax.rem(lax.axis_index("slab"), 2)
    tile_odd = lax.rem(lax.axis_index("tile"), 2)

    def pack(low_ref, high_ref, out_ref, top):
        near, second = (3 * (depth - 1), 3 * (depth - 2)) if top else (0, 3)
        out_ref[0:2, :] = low_ref[near + 1 : near + 3, :]
        out_ref[2:4, :] = high_ref[near : near + 2, :]
        out_ref[4:5, :] = low_ref[second + 2 : second + 3, :]
        out_ref[5:6, :] = high_ref[second : second + 1, :]
        out_ref[6:8, :] = jnp.zeros((2, cols), F32)

    for parity in range(2):
        for top in range(2):

            @pl.when((tile_odd == parity) & (slab_odd == top))
            def _():
                beside = (row_even_ref, row_odd_ref) if parity else (row_odd_ref, row_even_ref)
                pack(*beside, rim_odd_ref, top == 1)
                pack(*beside, rim_even_ref, top == 0)


def sweep_kernel(
    u_ref,
    odd_ref,
    even_ref,
    row_odd_ref,
    row_even_ref,
    rim_odd_ref,
    rim_even_ref,
    keep_ref,
    steps_ref,
    changes_ref,
    sums_ref,
    grad_ref,
    send_ref,
    start_ref,
    one_ref,
    two_ref,
    total_ref,
):
    depth, rows, cols = u_ref.shape
    slab, tile = lax.axis_index("slab"), lax.axis_index("tile")
    slab_odd, tile_odd = lax.rem(slab, 2), lax.rem(tile, 2)
    inside = {
        "low_z": (slab > 0).astype(F32),
        "high_z": (slab < lax.axis_size("slab") - 1).astype(F32),
        "low_y": (tile > 0).astype(F32),
        "high_y": (tile < lax.axis_size("tile") - 1).astype(F32),
    }

    for z in range(depth):
        start_ref[3 + z, 8 : 8 + rows, :] = u_ref[z]

    def edge(from_ref, first, count, z, factor, high):
        to = 8 + rows if high else 8 - count
        start_ref[z, to : to + count, :] = from_ref[first : first + count, :] * factor

    def below_and_above(from_ref, rim_ref, high):
        factor = inside["high_z" if high else "low_z"]
        for z in range(3):
            start_ref[7 * high + z, 8 : 8 + rows, :] = from_ref[z] * factor
        near, second = (7, 8) if high else (2, 1)
        low_factor, high_factor = factor * inside["low_y"], factor * inside["high_y"]
        edge(rim_ref, 0, 2, near, low_factor, False)
        edge(rim_ref, 2, 2, near, high_factor, True)
        edge(rim_ref, 4, 1, second, low_factor, False)
        edge(rim_ref, 5, 1, second, high_factor, True)

    def beside(from_ref, high):
        for z in range(depth):
            edge(from_ref, 3 * z, 3, 3 + z, inside["high_y" if high else "low_y"], high)

    for parity in range(2):

        @pl.when(slab_odd == parity)
        def _():
            below_and_above(odd_ref, rim_odd_ref, parity == 1)
            below_and_above(even_ref, rim_even_ref, parity == 0)

        @pl.when(tile_odd == parity)
        def _():
            beside(row_odd_ref, parity == 1)
            beside(row_even_ref, parity == 0)

    column = lax.broadcasted_iota(jnp.int32, (8, cols), 1)
    first, last = column == 0, column == cols - 1

    def relax(from_ref, z, row):
        here = from_ref[z, row : row + 8, :]
        around = from_ref[z - 1, row : row + 8, :] + from_ref[z + 1, row : row + 8, :]
        if row == 0:
            below = pltpu.roll(here, 1, 0)
        else:
            below = from_ref[z, row - 1 : row + 7, :]
        if row == rows + 8:
            above = pltpu.roll(here, 7, 0)
        else:
            above = from_ref[z, row + 1 : row + 9, :]
        around += below + above
        around += jnp.where(first, 0.0, pltpu.roll(here, 1, 1))
        around += jnp.where(last, 0.0, pltpu.roll(here, cols - 1, 1))
        return start_ref[z, row : row + 8, :] + coupling * around

    def outside(z, row):
        factor = None
        if z < 3:
            factor = inside["low_z"]
        if z > 6:
            factor = inside["high_z"]
        edge_factor = inside["low_y"] if row < 8 else inside["high_y"] if row >= 8 + rows else None
        if factor is None or edge_factor is None:
            return edge_factor if factor is None else factor
        return factor * edge_factor

    def sweep(from_ref, to_ref, reach):
        for z in range(3 - reach, 7 + reach):
            beyond = max(3 - z, z - 6, 0)
            wide = reach - beyond > 0
            for row in range(0 if wide else 8, 8 + rows + (8 if wide else 0), 8):
                value = relax(from_ref, z, row)
                factor = outside(z, row)
                to_ref[z, row : row + 8, :] = value if factor is None else value * factor

    sweep(start_ref, one_ref, 2)
    sweep(one_ref, two_ref, 1)

    sums = [jnp.zeros((8, LANES), F32) for _ in range(2 * MEM)]
    for z in range(depth):
        for row in range(0, rows, 8):
            value = relax(two_ref, 3 + z, 8 + row) * keep_ref[z // 2, row : row + 8, :]
            grad_ref[z, row : row + 8, :] = value
            for col in range(0, cols, LANES):
                piece = value[:, col : col + LANES]
                for i in range(MEM):
                    sums[i] += steps_ref[i, z, row : row + 8, col : col + LANES] * piece
                    sums[MEM + i] += changes_ref[i, z, row : row + 8, col : col + LANES] * piece
    done = 2 * len(PAIRS)
    total_ref[0:done, :] = sums_ref[0:done, :]
    for n, value in enumerate(sums):
        total_ref[done + n : done + n + 1, :] = jnp.sum(value, axis=0, keepdims=True)
    total_ref[done + 2 * MEM :, :] = jnp.zeros((SUMS - done - 2 * MEM, LANES), F32)
    totals = jnp.sum(total_ref[...], axis=1, keepdims=True)
    diagonal = lax.broadcasted_iota(jnp.int32, (SUMS, LANES), 0) == lax.broadcasted_iota(
        jnp.int32, (SUMS, LANES), 1
    )
    line = jnp.sum(jnp.where(diagonal, totals, 0.0), axis=0, keepdims=True)
    send_ref[...] = jnp.broadcast_to(line, send_ref.shape)


def combine_kernel(all_ref, grad_ref, steps_ref, changes_ref, out_hbm, out_ref, left):
    depth, rows, cols = grad_ref.shape
    line = jnp.sum(all_ref[...], axis=0, keepdims=True)

    def entry(n):
        return jnp.broadcast_to(line[:, n : n + 1], (8, LANES))

    sy = {pair: entry(n) for pair, n in SY.items()}
    yy = {pair: entry(n) for pair, n in YY.items()}
    inverse = [1.0 / sy[i, i] for i in range(MEM)]
    alphas = [None] * MEM
    for i in reversed(range(MEM)):
        product = entry(SG[i])
        for j in range(i + 1, MEM):
            product -= alphas[j] * sy[i, j]
        alphas[i] = product * inverse[i]
    scale = sy[MEM - 1, MEM - 1] / yy[MEM - 1, MEM - 1]
    weights = [None] * MEM
    for i in range(MEM):
        product = entry(YG[i])
        for j in range(MEM):
            product -= alphas[j] * yy[min(i, j), max(i, j)]
        product *= scale
        for j in range(i):
            product += weights[j] * sy[j, i]
        weights[i] = alphas[i] - product * inverse[i]
    on_changes = [scale * alphas[i] for i in range(MEM)]
    copies = [
        pltpu.make_async_copy(out_ref.at[z], out_hbm.at[z], left.at[z]) for z in range(depth)
    ]
    for z in range(depth):
        for row in range(0, rows, 8):
            for col in range(0, cols, LANES):
                lane = slice(col, col + LANES)
                value = -scale * grad_ref[z, row : row + 8, lane]
                for i in range(MEM):
                    value += on_changes[i] * changes_ref[i, z, row : row + 8, lane]
                    value -= weights[i] * steps_ref[i, z, row : row + 8, lane]
                out_ref[z, row : row + 8, lane] = value
        copies[z].start()
    for copy in copies:
        copy.wait()


def in_hbm(array):
    return pltpu.with_memory_space_constraint(array, pltpu.HBM)


def swaps(count):
    even = [(i, i ^ 1) for i in range(count)]
    odd = [(i, (i + 1) % count if i % 2 else (i - 1) % count) for i in range(count)]
    return odd, even


def per_device(sensitivity, filtered_density, passive_blocks, history_steps, history_changes):
    shape = sensitivity.shape
    depth, rows, cols = shape
    like = jax.ShapeDtypeStruct
    layers, rim, edges = (
        like(size, F32) for size in ((SWEEPS, rows, cols), (8, cols), (ROWS_SENT, cols))
    )
    devices = lax.axis_size("slab") * lax.axis_size("tile")

    u, row_odd, row_even, odd, even = pl.pallas_call(
        weight_kernel,
        out_shape=(like(shape, F32), edges, edges, layers, layers),
        in_specs=[HBM] * 2,
        out_specs=[VMEM] * 5,
        scratch_shapes=[
            pltpu.VMEM(shape, F32),
            pltpu.VMEM(shape, F32),
            pltpu.SemaphoreType.DMA((2, depth)),
        ],
        compiler_params=kernel_params(8),
        name="weights",
    )(in_hbm(sensitivity), in_hbm(filtered_density))

    slab_odd, slab_even = swaps(lax.axis_size("slab"))
    tile_odd, tile_even = swaps(lax.axis_size("tile"))
    row_odd = lax.ppermute(row_odd, "tile", tile_odd)
    row_even = lax.ppermute(row_even, "tile", tile_even)
    odd = lax.ppermute(odd, "slab", slab_odd)
    even = lax.ppermute(even, "slab", slab_even)

    history = like(history_steps.shape, F32)
    sums, keep, steps, changes = pl.pallas_call(
        gram_kernel,
        out_shape=(
            like((SUMS, LANES), F32),
            like((depth // 2, rows, cols), F32),
            history,
            history,
        ),
        in_specs=[HBM] * 3,
        out_specs=[VMEM] * 4,
        scratch_shapes=[
            pltpu.VMEM(passive_blocks.shape, jnp.int32),
            pltpu.SemaphoreType.DMA((2, depth)),
            pltpu.SemaphoreType.DMA,
        ],
        compiler_params=kernel_params(8),
        cost_estimate=pl.CostEstimate(flops=8_000_000_000, bytes_accessed=43_000_000, transcendentals=0),
        name="gram",
    )(in_hbm(history_steps), in_hbm(history_changes), in_hbm(passive_blocks))

    rim_odd, rim_even = pl.pallas_call(
        corner_kernel,
        out_shape=(rim, rim),
        in_specs=[VMEM] * 3,
        out_specs=[VMEM] * 2,
        compiler_params=kernel_params(8),
        name="corners",
    )(row_odd, row_even, sums)
    rim_odd = lax.ppermute(rim_odd, "slab", slab_odd)
    rim_even = lax.ppermute(rim_even, "slab", slab_even)

    padded = pltpu.VMEM((depth + 6, rows + 16, cols), F32)
    gradient, line = pl.pallas_call(
        sweep_kernel,
        out_shape=(like(shape, F32), like((devices, LANES), F32)),
        in_specs=[VMEM] * 11,
        out_specs=[VMEM] * 2,
        scratch_shapes=[padded, padded, padded, pltpu.VMEM((SUMS, LANES), F32)],
        compiler_params=kernel_params(16),
        name="sweeps",
    )(u, odd, even, row_odd, row_even, rim_odd, rim_even, keep, steps, changes, sums)

    lines = lax.all_to_all(line, ("slab", "tile"), 0, 0, tiled=True)

    return pl.pallas_call(
        combine_kernel,
        out_shape=like(shape, F32),
        in_specs=[VMEM] * 4,
        out_specs=HBM,
        scratch_shapes=[pltpu.VMEM(shape, F32), pltpu.SemaphoreType.DMA((depth,))],
        compiler_params=kernel_params(8),
        name="combine",
    )(lines, gradient, steps, changes)


def solution(mesh):
    in_specs = (
        P("slab", "tile", None),
        P("slab", "tile", None),
        P("slab", "tile", None),
        P(None, "slab", "tile", None),
        P(None, "slab", "tile", None),
    )
    out_specs = P("slab", "tile", None)
    return jax.shard_map(
        per_device, mesh=mesh, in_specs=in_specs, out_specs=out_specs, check_vma=False
    )
```

```python
import jax
import jax.numpy as jnp
from jax import lax
from jax.experimental import pallas as pl
from jax.experimental.pallas import tpu as pltpu
from jax.sharding import PartitionSpec as P

SWEEPS = 3
MEM = 4

radius_square = 4.0
sharpness = 8.0
threshold = 0.5
diagonal_value = 1.0 + 6.0 * radius_square
coupling = radius_square / diagonal_value

F32 = jnp.float32
LANES = 128
PAIRS = [(i, j) for i in range(MEM) for j in range(i, MEM)]
SY = {pair: n for n, pair in enumerate(PAIRS)}
YY = {pair: len(PAIRS) + n for n, pair in enumerate(PAIRS)}
SG = [2 * len(PAIRS) + n for n in range(MEM)]
YG = [2 * len(PAIRS) + MEM + n for n in range(MEM)]
SUMS = 32
ROWS_SENT = 24

VMEM = pl.BlockSpec(memory_space=pltpu.VMEM)
HBM = pl.BlockSpec(memory_space=pltpu.HBM)


def kernel_params(mib):
    return pltpu.CompilerParams(vmem_limit_bytes=mib * 1024 * 1024)


def weight_kernel(
    sens_hbm,
    dens_hbm,
    u_ref,
    rim_odd_ref,
    rim_even_ref,
    odd_ref,
    even_ref,
    sens_ref,
    dens_ref,
    arrived,
):
    depth, rows, cols = u_ref.shape
    slab_odd = lax.rem(lax.axis_index("slab"), 2)
    copies = [
        [
            pltpu.make_async_copy(from_ref.at[z], to_ref.at[z], arrived.at[n, z])
            for n, (from_ref, to_ref) in enumerate(((sens_hbm, sens_ref), (dens_hbm, dens_ref)))
        ]
        for z in range(depth)
    ]
    for pair in copies:
        for copy in pair:
            copy.start()
    denominator = jnp.tanh(F32(sharpness * threshold)) + jnp.tanh(
        F32(sharpness * (1.0 - threshold))
    )
    for z in range(depth):
        for copy in copies[z]:
            copy.wait()
        bend = jnp.tanh(sharpness * (dens_ref[z] - threshold))
        slope = sharpness * (1.0 - bend * bend) / denominator
        u_ref[z] = sens_ref[z] * slope / diagonal_value

    for rim_ref, layers_ref, top in (
        (rim_odd_ref, odd_ref, slab_odd),
        (rim_even_ref, even_ref, 1 - slab_odd),
    ):
        near, second = (depth - 1) * top, 1 + (depth - 3) * top
        rim_ref[0:2, :] = u_ref[near, 0:2, :]
        rim_ref[2:4, :] = u_ref[near, rows - 2 : rows, :]
        rim_ref[4:5, :] = u_ref[second, 0:1, :]
        rim_ref[5:6, :] = u_ref[second, rows - 1 : rows, :]
        rim_ref[6:8, :] = jnp.zeros((2, cols), F32)
        layers_ref[...] = u_ref[pl.ds(top, SWEEPS)]


def gram_kernel(
    steps_hbm,
    changes_hbm,
    passive_hbm,
    sums_ref,
    keep_ref,
    steps_ref,
    changes_ref,
    passive_ref,
    arrived,
    passive_arrived,
):
    depth, rows, cols = steps_ref.shape[1:]
    passive_copy = pltpu.make_async_copy(passive_hbm, passive_ref, passive_arrived)
    copies = [
        [
            pltpu.make_async_copy(from_ref.at[:, z], to_ref.at[:, z], arrived.at[n, z])
            for n, (from_ref, to_ref) in enumerate(
                ((steps_hbm, steps_ref), (changes_hbm, changes_ref))
            )
        ]
        for z in range(depth)
    ]
    passive_copy.start()
    for pair in copies:
        for copy in pair:
            copy.start()

    def doubling(shape, dim):
        place = lax.broadcasted_iota(jnp.int32, shape, dim) // 2
        matches = place == lax.broadcasted_iota(jnp.int32, shape, 1 - dim)
        return matches.astype(F32).astype(jnp.bfloat16)

    passive_copy.wait()
    half_rows = passive_ref.shape[1]
    twice_rows = doubling((2 * half_rows, half_rows), 0)
    twice_cols = doubling((LANES, 2 * LANES), 1)
    for z in range(passive_ref.shape[0]):
        blocks = passive_ref[z].astype(F32).astype(jnp.bfloat16)
        blocks = jnp.dot(twice_rows, blocks, preferred_element_type=F32).astype(jnp.bfloat16)
        for col in range(0, passive_ref.shape[2], LANES):
            wide = jnp.dot(
                blocks[:, col : col + LANES], twice_cols, preferred_element_type=F32
            )
            keep_ref[z, :, 2 * col : 2 * col + 2 * LANES] = 1.0 - wide

    sums = (jnp.zeros((8, LANES), F32),) * (2 * len(PAIRS))
    for z in range(depth):
        for copy in copies[z]:
            copy.wait()

        def step(block, sums):
            row = pl.ds(pl.multiple_of(block * 8, 8), 8)
            sums = list(sums)
            for col in range(0, cols, LANES):
                lane = pl.ds(col, LANES)
                s = [steps_ref[i, z, row, lane] for i in range(MEM)]
                y = [changes_ref[i, z, row, lane] for i in range(MEM)]
                for i, j in PAIRS:
                    sums[SY[i, j]] += s[i] * y[j]
                    sums[YY[i, j]] += y[i] * y[j]
            return tuple(sums)

        sums = lax.fori_loop(0, rows // 8, step, sums)
    for n, value in enumerate(sums):
        sums_ref[n : n + 1, :] = jnp.sum(value, axis=0, keepdims=True)


def pack_kernel(u_ref, odd_ref, even_ref, row_odd_ref, row_even_ref):
    depth, rows = u_ref.shape[:2]
    slab_odd = lax.rem(lax.axis_index("slab"), 2)
    tile_odd = lax.rem(lax.axis_index("tile"), 2)

    def pack(low_ref, high_ref, out_ref, top):
        for z in range(depth):
            start = rows - 3 if top else 0
            out_ref[3 * z : 3 * z + 3, :] = u_ref[z, start : start + 3, :]
        near, second = (2, 5) if top else (0, 4)
        out_ref[12:14, :] = low_ref[near : near + 2, :]
        out_ref[14:16, :] = high_ref[near : near + 2, :]
        out_ref[16:17, :] = low_ref[second : second + 1, :]
        out_ref[17:18, :] = high_ref[second : second + 1, :]
        out_ref[18:24, :] = jnp.zeros((6, out_ref.shape[1]), F32)

    for parity in range(2):
        for top in range(2):

            @pl.when((slab_odd == parity) & (tile_odd == top))
            def _():
                low_ref, high_ref = (even_ref, odd_ref) if parity else (odd_ref, even_ref)
                pack(low_ref, high_ref, row_odd_ref, top == 1)
                pack(low_ref, high_ref, row_even_ref, top == 0)


def sweep_kernel(
    u_ref,
    odd_ref,
    even_ref,
    row_odd_ref,
    row_even_ref,
    keep_ref,
    steps_ref,
    changes_ref,
    sums_ref,
    grad_ref,
    send_ref,
    start_ref,
    one_ref,
    two_ref,
    total_ref,
):
    depth, rows, cols = u_ref.shape
    slab, tile = lax.axis_index("slab"), lax.axis_index("tile")
    slab_odd, tile_odd = lax.rem(slab, 2), lax.rem(tile, 2)
    inside = {
        "low_z": (slab > 0).astype(F32),
        "high_z": (slab < lax.axis_size("slab") - 1).astype(F32),
        "low_y": (tile > 0).astype(F32),
        "high_y": (tile < lax.axis_size("tile") - 1).astype(F32),
    }

    for z in range(depth):
        start_ref[3 + z, 8 : 8 + rows, :] = u_ref[z]

    def layers(low_ref, high_ref):
        for z in range(3):
            start_ref[z, 8 : 8 + rows, :] = low_ref[z] * inside["low_z"]
            start_ref[7 + z, 8 : 8 + rows, :] = high_ref[z] * inside["high_z"]

    def edge(from_ref, first, count, z, factor, high):
        to = 8 + rows if high else 8 - count
        start_ref[z, to : to + count, :] = from_ref[first : first + count, :] * factor

    def beside(from_ref, high):
        factor = inside["high_y" if high else "low_y"]
        for z in range(depth):
            edge(from_ref, 3 * z, 3, 3 + z, factor, high)
        low_factor, high_factor = factor * inside["low_z"], factor * inside["high_z"]
        edge(from_ref, 12, 2, 2, low_factor, high)
        edge(from_ref, 14, 2, 7, high_factor, high)
        edge(from_ref, 16, 1, 1, low_factor, high)
        edge(from_ref, 17, 1, 8, high_factor, high)

    for parity in range(2):

        @pl.when(slab_odd == parity)
        def _():
            layers(*((even_ref, odd_ref) if parity else (odd_ref, even_ref)))

        @pl.when(tile_odd == parity)
        def _():
            beside(row_odd_ref, parity == 1)
            beside(row_even_ref, parity == 0)

    column = lax.broadcasted_iota(jnp.int32, (8, cols), 1)
    first, last = column == 0, column == cols - 1

    def relax(from_ref, z, row):
        here = from_ref[z, row : row + 8, :]
        around = from_ref[z - 1, row : row + 8, :] + from_ref[z + 1, row : row + 8, :]
        if row == 0:
            below = pltpu.roll(here, 1, 0)
        else:
            below = from_ref[z, row - 1 : row + 7, :]
        if row == rows + 8:
            above = pltpu.roll(here, 7, 0)
        else:
            above = from_ref[z, row + 1 : row + 9, :]
        around += below + above
        around += jnp.where(first, 0.0, pltpu.roll(here, 1, 1))
        around += jnp.where(last, 0.0, pltpu.roll(here, cols - 1, 1))
        return start_ref[z, row : row + 8, :] + coupling * around

    def outside(z, row):
        factor = None
        if z < 3:
            factor = inside["low_z"]
        if z > 6:
            factor = inside["high_z"]
        edge_factor = inside["low_y"] if row < 8 else inside["high_y"] if row >= 8 + rows else None
        if factor is None or edge_factor is None:
            return edge_factor if factor is None else factor
        return factor * edge_factor

    def sweep(from_ref, to_ref, reach):
        for z in range(3 - reach, 7 + reach):
            beyond = max(3 - z, z - 6, 0)
            wide = reach - beyond > 0
            for row in range(0 if wide else 8, 8 + rows + (8 if wide else 0), 8):
                value = relax(from_ref, z, row)
                factor = outside(z, row)
                to_ref[z, row : row + 8, :] = value if factor is None else value * factor

    sweep(start_ref, one_ref, 2)
    sweep(one_ref, two_ref, 1)

    sums = [jnp.zeros((8, LANES), F32) for _ in range(2 * MEM)]
    for z in range(depth):
        for row in range(0, rows, 8):
            value = relax(two_ref, 3 + z, 8 + row) * keep_ref[z // 2, row : row + 8, :]
            grad_ref[z, row : row + 8, :] = value
            for col in range(0, cols, LANES):
                piece = value[:, col : col + LANES]
                for i in range(MEM):
                    sums[i] += steps_ref[i, z, row : row + 8, col : col + LANES] * piece
                    sums[MEM + i] += changes_ref[i, z, row : row + 8, col : col + LANES] * piece
    done = 2 * len(PAIRS)
    total_ref[0:done, :] = sums_ref[0:done, :]
    for n, value in enumerate(sums):
        total_ref[done + n : done + n + 1, :] = jnp.sum(value, axis=0, keepdims=True)
    total_ref[done + 2 * MEM :, :] = jnp.zeros((SUMS - done - 2 * MEM, LANES), F32)
    totals = jnp.sum(total_ref[...], axis=1, keepdims=True)
    diagonal = lax.broadcasted_iota(jnp.int32, (SUMS, LANES), 0) == lax.broadcasted_iota(
        jnp.int32, (SUMS, LANES), 1
    )
    line = jnp.sum(jnp.where(diagonal, totals, 0.0), axis=0, keepdims=True)
    send_ref[...] = jnp.broadcast_to(line, send_ref.shape)


def combine_kernel(all_ref, grad_ref, steps_ref, changes_ref, out_hbm, out_ref, left):
    depth, rows, cols = grad_ref.shape
    line = jnp.sum(all_ref[...], axis=0, keepdims=True)

    def entry(n):
        return jnp.broadcast_to(line[:, n : n + 1], (8, LANES))

    sy = {pair: entry(n) for pair, n in SY.items()}
    yy = {pair: entry(n) for pair, n in YY.items()}
    inverse = [1.0 / sy[i, i] for i in range(MEM)]
    alphas = [None] * MEM
    for i in reversed(range(MEM)):
        product = entry(SG[i])
        for j in range(i + 1, MEM):
            product -= alphas[j] * sy[i, j]
        alphas[i] = product * inverse[i]
    scale = sy[MEM - 1, MEM - 1] / yy[MEM - 1, MEM - 1]
    weights = [None] * MEM
    for i in range(MEM):
        product = entry(YG[i])
        for j in range(MEM):
            product -= alphas[j] * yy[min(i, j), max(i, j)]
        product *= scale
        for j in range(i):
            product += weights[j] * sy[j, i]
        weights[i] = alphas[i] - product * inverse[i]
    on_changes = [scale * alphas[i] for i in range(MEM)]
    copies = [
        pltpu.make_async_copy(out_ref.at[z], out_hbm.at[z], left.at[z]) for z in range(depth)
    ]
    for z in range(depth):
        for row in range(0, rows, 8):
            for col in range(0, cols, LANES):
                lane = slice(col, col + LANES)
                value = -scale * grad_ref[z, row : row + 8, lane]
                for i in range(MEM):
                    value += on_changes[i] * changes_ref[i, z, row : row + 8, lane]
                    value -= weights[i] * steps_ref[i, z, row : row + 8, lane]
                out_ref[z, row : row + 8, lane] = value
        copies[z].start()
    for copy in copies:
        copy.wait()


def in_hbm(array):
    return pltpu.with_memory_space_constraint(array, pltpu.HBM)


def swaps(count):
    even = [(i, i ^ 1) for i in range(count)]
    odd = [(i, (i + 1) % count if i % 2 else (i - 1) % count) for i in range(count)]
    return odd, even


def per_device(sensitivity, filtered_density, passive_blocks, history_steps, history_changes):
    shape = sensitivity.shape
    depth, rows, cols = shape
    like = jax.ShapeDtypeStruct
    layers, rim, edges = (
        like(size, F32) for size in ((SWEEPS, rows, cols), (8, cols), (ROWS_SENT, cols))
    )
    devices = lax.axis_size("slab") * lax.axis_size("tile")

    u, rim_odd, rim_even, odd, even = pl.pallas_call(
        weight_kernel,
        out_shape=(like(shape, F32), rim, rim, layers, layers),
        in_specs=[HBM] * 2,
        out_specs=[VMEM] * 5,
        scratch_shapes=[
            pltpu.VMEM(shape, F32),
            pltpu.VMEM(shape, F32),
            pltpu.SemaphoreType.DMA((2, depth)),
        ],
        compiler_params=kernel_params(8),
        name="weights",
    )(in_hbm(sensitivity), in_hbm(filtered_density))

    odd_pairs, even_pairs = swaps(lax.axis_size("slab"))
    rim_odd = lax.ppermute(rim_odd, "slab", odd_pairs)
    rim_even = lax.ppermute(rim_even, "slab", even_pairs)
    odd = lax.ppermute(odd, "slab", odd_pairs)
    even = lax.ppermute(even, "slab", even_pairs)

    row_odd, row_even = pl.pallas_call(
        pack_kernel,
        out_shape=(edges, edges),
        in_specs=[VMEM] * 3,
        out_specs=[VMEM] * 2,
        compiler_params=kernel_params(8),
        name="edges",
    )(u, rim_odd, rim_even)
    odd_pairs, even_pairs = swaps(lax.axis_size("tile"))
    row_odd = lax.ppermute(row_odd, "tile", odd_pairs)
    row_even = lax.ppermute(row_even, "tile", even_pairs)

    history = like(history_steps.shape, F32)
    sums, keep, steps, changes = pl.pallas_call(
        gram_kernel,
        out_shape=(
            like((SUMS, LANES), F32),
            like((depth // 2, rows, cols), F32),
            history,
            history,
        ),
        in_specs=[HBM] * 3,
        out_specs=[VMEM] * 4,
        scratch_shapes=[
            pltpu.VMEM(passive_blocks.shape, jnp.int32),
            pltpu.SemaphoreType.DMA((2, depth)),
            pltpu.SemaphoreType.DMA,
        ],
        compiler_params=kernel_params(8),
        cost_estimate=pl.CostEstimate(flops=8_000_000_000, bytes_accessed=43_000_000, transcendentals=0),
        name="gram",
    )(in_hbm(history_steps), in_hbm(history_changes), in_hbm(passive_blocks))

    padded = pltpu.VMEM((depth + 6, rows + 16, cols), F32)
    gradient, line = pl.pallas_call(
        sweep_kernel,
        out_shape=(like(shape, F32), like((devices, LANES), F32)),
        in_specs=[VMEM] * 9,
        out_specs=[VMEM] * 2,
        scratch_shapes=[padded, padded, padded, pltpu.VMEM((SUMS, LANES), F32)],
        compiler_params=kernel_params(16),
        name="sweeps",
    )(u, odd, even, row_odd, row_even, keep, steps, changes, sums)

    lines = lax.all_to_all(line, ("slab", "tile"), 0, 0, tiled=True)

    return pl.pallas_call(
        combine_kernel,
        out_shape=like(shape, F32),
        in_specs=[VMEM] * 4,
        out_specs=HBM,
        scratch_shapes=[pltpu.VMEM(shape, F32), pltpu.SemaphoreType.DMA((depth,))],
        compiler_params=kernel_params(8),
        name="combine",
    )(lines, gradient, steps, changes)


def solution(mesh):
    in_specs = (
        P("slab", "tile", None),
        P("slab", "tile", None),
        P("slab", "tile", None),
        P(None, "slab", "tile", None),
        P(None, "slab", "tile", None),
    )
    out_specs = P("slab", "tile", None)
    return jax.shard_map(
        per_device, mesh=mesh, in_specs=in_specs, out_specs=out_specs, check_vma=False
    )
```

```python
import jax
import jax.numpy as jnp
from jax import lax
from jax.experimental import pallas as pl
from jax.experimental.pallas import tpu as pltpu
from jax.sharding import PartitionSpec as P

SWEEPS = 3
MEM = 4

radius_square = 4.0
sharpness = 8.0
threshold = 0.5
diagonal_value = 1.0 + 6.0 * radius_square
coupling = radius_square / diagonal_value

F32 = jnp.float32
LANES = 128
PAIRS = [(i, j) for i in range(MEM) for j in range(i, MEM)]
SY = {pair: n for n, pair in enumerate(PAIRS)}
YY = {pair: len(PAIRS) + n for n, pair in enumerate(PAIRS)}
SG = [2 * len(PAIRS) + n for n in range(MEM)]
YG = [2 * len(PAIRS) + MEM + n for n in range(MEM)]
SUMS = 32

VMEM = pl.BlockSpec(memory_space=pltpu.VMEM)
HBM = pl.BlockSpec(memory_space=pltpu.HBM)


def kernel_params(mib):
    return pltpu.CompilerParams(vmem_limit_bytes=mib * 1024 * 1024)


def weight_kernel(
    sens_hbm,
    dens_hbm,
    u_ref,
    rim_odd_ref,
    rim_even_ref,
    odd_ref,
    even_ref,
    sens_ref,
    dens_ref,
    arrived,
):
    depth, rows, cols = sens_ref.shape
    width = cols // LANES
    layer = rows * width
    slab_odd = lax.rem(lax.axis_index("slab"), 2)
    copies = [
        [
            pltpu.make_async_copy(from_ref.at[z], to_ref.at[z], arrived.at[n, z])
            for n, (from_ref, to_ref) in enumerate(((sens_hbm, sens_ref), (dens_hbm, dens_ref)))
        ]
        for z in range(depth)
    ]
    for pair in copies:
        for copy in pair:
            copy.start()
    denominator = jnp.tanh(F32(sharpness * threshold)) + jnp.tanh(
        F32(sharpness * (1.0 - threshold))
    )
    for z in range(depth):
        for copy in copies[z]:
            copy.wait()
        bend = jnp.tanh(sharpness * (dens_ref[z] - threshold))
        slope = sharpness * (1.0 - bend * bend) / denominator
        value = sens_ref[z] * slope / diagonal_value
        for row in range(0, rows, 8):
            for part in range(width):
                place = pl.ds(z * layer + row * width + part, 8, width)
                u_ref[place, :] = value[row : row + 8, part * LANES : (part + 1) * LANES]

    for rim_ref, layers_ref, top in (
        (rim_odd_ref, odd_ref, slab_odd),
        (rim_even_ref, even_ref, 1 - slab_odd),
    ):

        def put(first, count, z, row):
            place = pl.ds(pl.multiple_of(z * layer + row * width, 8), count * width)
            rim_ref[first * width : (first + count) * width, :] = u_ref[place, :]

        near, second = (depth - 1) * top, 1 + (depth - 3) * top
        put(0, 2, near, 0)
        put(2, 2, near, rows - 2)
        put(4, 1, second, 0)
        put(5, 1, second, rows - 1)
        layers_ref[...] = u_ref[pl.ds(pl.multiple_of(top * layer, 8), SWEEPS * layer), :]


def gram_kernel(
    steps_hbm,
    changes_hbm,
    passive_hbm,
    sums_ref,
    keep_ref,
    steps_ref,
    changes_ref,
    passive_ref,
    arrived,
    passive_arrived,
):
    depth, rows, cols = steps_ref.shape[1:]
    passive_copy = pltpu.make_async_copy(passive_hbm, passive_ref, passive_arrived)
    copies = [
        [
            pltpu.make_async_copy(from_ref.at[:, z], to_ref.at[:, z], arrived.at[n, z])
            for n, (from_ref, to_ref) in enumerate(
                ((steps_hbm, steps_ref), (changes_hbm, changes_ref))
            )
        ]
        for z in range(depth)
    ]
    passive_copy.start()
    for pair in copies:
        for copy in pair:
            copy.start()

    def doubling(shape, dim):
        place = lax.broadcasted_iota(jnp.int32, shape, dim) // 2
        matches = place == lax.broadcasted_iota(jnp.int32, shape, 1 - dim)
        return matches.astype(F32).astype(jnp.bfloat16)

    passive_copy.wait()
    half_rows = passive_ref.shape[1]
    twice_rows = doubling((2 * half_rows, half_rows), 0)
    twice_cols = doubling((LANES, 2 * LANES), 1)
    for z in range(passive_ref.shape[0]):
        blocks = passive_ref[z].astype(F32).astype(jnp.bfloat16)
        blocks = jnp.dot(twice_rows, blocks, preferred_element_type=F32).astype(jnp.bfloat16)
        for col in range(0, passive_ref.shape[2], LANES):
            wide = jnp.dot(
                blocks[:, col : col + LANES], twice_cols, preferred_element_type=F32
            )
            keep_ref[z, :, 2 * col : 2 * col + 2 * LANES] = 1.0 - wide

    sums = (jnp.zeros((8, LANES), F32),) * (2 * len(PAIRS))
    for z in range(depth):
        for copy in copies[z]:
            copy.wait()

        def step(block, sums):
            row = pl.ds(pl.multiple_of(block * 8, 8), 8)
            sums = list(sums)
            for col in range(0, cols, LANES):
                lane = pl.ds(col, LANES)
                s = [steps_ref[i, z, row, lane] for i in range(MEM)]
                y = [changes_ref[i, z, row, lane] for i in range(MEM)]
                for i, j in PAIRS:
                    sums[SY[i, j]] += s[i] * y[j]
                    sums[YY[i, j]] += y[i] * y[j]
            return tuple(sums)

        sums = lax.fori_loop(0, rows // 8, step, sums)
    for n, value in enumerate(sums):
        sums_ref[n : n + 1, :] = jnp.sum(value, axis=0, keepdims=True)


def pack_kernel(u_ref, odd_ref, even_ref, row_odd_ref, row_even_ref):
    depth, rows = u_ref.shape[:2]
    slab_odd = lax.rem(lax.axis_index("slab"), 2)
    tile_odd = lax.rem(lax.axis_index("tile"), 2)

    def pack(low_ref, high_ref, out_ref, top):
        start = rows - 3 if top else 0
        for z in range(depth):
            out_ref[3 * z : 3 * z + 3] = u_ref[z, start : start + 3]
        near, second = (2, 5) if top else (0, 4)
        out_ref[12:14] = low_ref[near : near + 2]
        out_ref[14:16] = high_ref[near : near + 2]
        out_ref[16] = low_ref[second]
        out_ref[17] = high_ref[second]

    for parity in range(2):
        for top in range(2):

            @pl.when((slab_odd == parity) & (tile_odd == top))
            def _():
                low_ref, high_ref = (even_ref, odd_ref) if parity else (odd_ref, even_ref)
                pack(low_ref, high_ref, row_odd_ref, top == 1)
                pack(low_ref, high_ref, row_even_ref, top == 0)


def sweep_kernel(
    u_ref,
    odd_ref,
    even_ref,
    row_odd_ref,
    row_even_ref,
    keep_ref,
    steps_ref,
    changes_ref,
    sums_ref,
    grad_ref,
    send_ref,
    start_ref,
    one_ref,
    two_ref,
    last_ref,
    total_ref,
):
    depth, rows, width = u_ref.shape[:3]
    slab, tile = lax.axis_index("slab"), lax.axis_index("tile")
    slab_odd, tile_odd = lax.rem(slab, 2), lax.rem(tile, 2)
    inside = {
        "low_z": (slab > 0).astype(F32),
        "high_z": (slab < lax.axis_size("slab") - 1).astype(F32),
        "low_y": (tile > 0).astype(F32),
        "high_y": (tile < lax.axis_size("tile") - 1).astype(F32),
    }

    start_ref[3 : 3 + depth, 3 : 3 + rows] = u_ref[...]

    def layers(low_ref, high_ref):
        start_ref[0:3, 3 : 3 + rows] = low_ref[...] * inside["low_z"]
        start_ref[3 + depth :, 3 : 3 + rows] = high_ref[...] * inside["high_z"]

    def edge(from_ref, first, count, z, factor, high):
        to = 3 + rows if high else 3 - count
        start_ref[z, to : to + count] = from_ref[first : first + count] * factor

    def beside(from_ref, high):
        factor = inside["high_y" if high else "low_y"]
        for z in range(depth):
            edge(from_ref, 3 * z, 3, 3 + z, factor, high)
        low_factor, high_factor = factor * inside["low_z"], factor * inside["high_z"]
        edge(from_ref, 12, 2, 2, low_factor, high)
        edge(from_ref, 14, 2, 3 + depth, high_factor, high)
        edge(from_ref, 16, 1, 1, low_factor, high)
        edge(from_ref, 17, 1, 4 + depth, high_factor, high)

    for parity in range(2):

        @pl.when(slab_odd == parity)
        def _():
            layers(*((even_ref, odd_ref) if parity else (odd_ref, even_ref)))

        @pl.when(tile_odd == parity)
        def _():
            beside(row_odd_ref, parity == 1)
            beside(row_even_ref, parity == 0)

    lane = lax.broadcasted_iota(jnp.int32, (width, LANES), 1)
    part = lax.broadcasted_iota(jnp.int32, (width, LANES), 0)
    lane_first, lane_last = lane == 0, lane == LANES - 1
    first, last = lane_first & (part == 0), lane_last & (part == width - 1)

    def relax(from_ref, z, y):
        here = from_ref[z, y]
        around = from_ref[z - 1, y] + from_ref[z + 1, y]
        around += from_ref[z, y - 1] + from_ref[z, y + 1]
        before, after = pltpu.roll(here, 1, 1), pltpu.roll(here, LANES - 1, 1)
        before = jnp.where(lane_first, pltpu.roll(before, 1, 0), before)
        after = jnp.where(lane_last, pltpu.roll(after, width - 1, 0), after)
        around += jnp.where(first, 0.0, before) + jnp.where(last, 0.0, after)
        return start_ref[z, y] + coupling * around

    def factors(z, y):
        if z < 3:
            yield inside["low_z"]
        if z >= 3 + depth:
            yield inside["high_z"]
        if y < 3:
            yield inside["low_y"]
        if y >= 3 + rows:
            yield inside["high_y"]

    def sweep(from_ref, to_ref, reach):
        for z in range(3 - reach, 3 + depth + reach):
            wide = reach - max(3 - z, z - 2 - depth, 0)
            for y in range(3 - wide, 3 + rows + wide):
                value = relax(from_ref, z, y)
                for factor in factors(z, y):
                    value *= factor
                to_ref[z, y] = value

    sweep(start_ref, one_ref, 2)
    sweep(one_ref, two_ref, 1)
    for z in range(depth):
        for y in range(rows):
            place = (z * rows + y) * width
            last_ref[place : place + width, :] = relax(two_ref, 3 + z, 3 + y)

    sums = [jnp.zeros((8, LANES), F32) for _ in range(2 * MEM)]
    for z in range(depth):
        for row in range(0, rows, 8):
            for part in range(width):
                block = slice(row, row + 8), slice(part * LANES, (part + 1) * LANES)
                value = last_ref[pl.ds((z * rows + row) * width + part, 8, width), :]
                value *= keep_ref[z // 2, *block]
                grad_ref[z, *block] = value
                for i in range(MEM):
                    sums[i] += steps_ref[i, z, *block] * value
                    sums[MEM + i] += changes_ref[i, z, *block] * value
    done = 2 * len(PAIRS)
    total_ref[0:done, :] = sums_ref[0:done, :]
    for n, value in enumerate(sums):
        total_ref[done + n : done + n + 1, :] = jnp.sum(value, axis=0, keepdims=True)
    total_ref[done + 2 * MEM :, :] = jnp.zeros((SUMS - done - 2 * MEM, LANES), F32)
    totals = jnp.sum(total_ref[...], axis=1, keepdims=True)
    diagonal = lax.broadcasted_iota(jnp.int32, (SUMS, LANES), 0) == lax.broadcasted_iota(
        jnp.int32, (SUMS, LANES), 1
    )
    line = jnp.sum(jnp.where(diagonal, totals, 0.0), axis=0, keepdims=True)
    send_ref[...] = jnp.broadcast_to(line, send_ref.shape)


def combine_kernel(all_ref, grad_ref, steps_ref, changes_ref, out_hbm, out_ref, left):
    depth, rows, cols = grad_ref.shape
    line = jnp.sum(all_ref[...], axis=0, keepdims=True)

    def entry(n):
        return jnp.broadcast_to(line[:, n : n + 1], (8, LANES))

    sy = {pair: entry(n) for pair, n in SY.items()}
    yy = {pair: entry(n) for pair, n in YY.items()}
    inverse = [1.0 / sy[i, i] for i in range(MEM)]
    alphas = [None] * MEM
    for i in reversed(range(MEM)):
        product = entry(SG[i])
        for j in range(i + 1, MEM):
            product -= alphas[j] * sy[i, j]
        alphas[i] = product * inverse[i]
    scale = sy[MEM - 1, MEM - 1] / yy[MEM - 1, MEM - 1]
    weights = [None] * MEM
    for i in range(MEM):
        product = entry(YG[i])
        for j in range(MEM):
            product -= alphas[j] * yy[min(i, j), max(i, j)]
        product *= scale
        for j in range(i):
            product += weights[j] * sy[j, i]
        weights[i] = alphas[i] - product * inverse[i]
    on_changes = [scale * alphas[i] for i in range(MEM)]
    copies = [
        pltpu.make_async_copy(out_ref.at[z], out_hbm.at[z], left.at[z]) for z in range(depth)
    ]
    for z in range(depth):
        for row in range(0, rows, 8):
            for col in range(0, cols, LANES):
                lane = slice(col, col + LANES)
                value = -scale * grad_ref[z, row : row + 8, lane]
                for i in range(MEM):
                    value += on_changes[i] * changes_ref[i, z, row : row + 8, lane]
                    value -= weights[i] * steps_ref[i, z, row : row + 8, lane]
                out_ref[z, row : row + 8, lane] = value
        copies[z].start()
    for copy in copies:
        copy.wait()


def in_hbm(array):
    return pltpu.with_memory_space_constraint(array, pltpu.HBM)


def swaps(count):
    even = [(i, i ^ 1) for i in range(count)]
    ends = {0: 0, count - 1: count - 1}
    odd = [(i, ends.get(i, i + 1 if i % 2 else i - 1)) for i in range(count)]
    return odd, even


def per_device(sensitivity, filtered_density, passive_blocks, history_steps, history_changes):
    shape = sensitivity.shape
    depth, rows, cols = shape
    like = jax.ShapeDtypeStruct
    width = cols // LANES
    lines, layers, rim = (
        like((count * width, LANES), F32) for count in (depth * rows, SWEEPS * rows, 6)
    )
    edges = like((3 * depth + 6, width, LANES), F32)
    devices = lax.axis_size("slab") * lax.axis_size("tile")

    u, rim_odd, rim_even, odd, even = pl.pallas_call(
        weight_kernel,
        out_shape=(lines, rim, rim, layers, layers),
        in_specs=[HBM] * 2,
        out_specs=[VMEM] * 5,
        scratch_shapes=[
            pltpu.VMEM(shape, F32),
            pltpu.VMEM(shape, F32),
            pltpu.SemaphoreType.DMA((2, depth)),
        ],
        compiler_params=kernel_params(8),
        name="weights",
    )(in_hbm(sensitivity), in_hbm(filtered_density))

    u = u.reshape(depth, rows, width, LANES)
    rim_odd, rim_even = (array.reshape(6, width, LANES) for array in (rim_odd, rim_even))
    odd, even = (array.reshape(SWEEPS, rows, width, LANES) for array in (odd, even))

    odd_pairs, even_pairs = swaps(lax.axis_size("slab"))
    rim_odd = lax.ppermute(rim_odd, "slab", odd_pairs)
    rim_even = lax.ppermute(rim_even, "slab", even_pairs)
    odd = lax.ppermute(odd, "slab", odd_pairs)
    even = lax.ppermute(even, "slab", even_pairs)

    row_odd, row_even = pl.pallas_call(
        pack_kernel,
        out_shape=(edges, edges),
        in_specs=[VMEM] * 3,
        out_specs=[VMEM] * 2,
        compiler_params=kernel_params(8),
        name="edges",
    )(u, rim_odd, rim_even)
    odd_pairs, even_pairs = swaps(lax.axis_size("tile"))
    row_odd = lax.ppermute(row_odd, "tile", odd_pairs)
    row_even = lax.ppermute(row_even, "tile", even_pairs)

    history = like(history_steps.shape, F32)
    sums, keep, steps, changes = pl.pallas_call(
        gram_kernel,
        out_shape=(
            like((SUMS, LANES), F32),
            like((depth // 2, rows, cols), F32),
            history,
            history,
        ),
        in_specs=[HBM] * 3,
        out_specs=[VMEM] * 4,
        scratch_shapes=[
            pltpu.VMEM(passive_blocks.shape, jnp.int32),
            pltpu.SemaphoreType.DMA((2, depth)),
            pltpu.SemaphoreType.DMA,
        ],
        compiler_params=kernel_params(8),
        cost_estimate=pl.CostEstimate(flops=8_000_000_000, bytes_accessed=43_000_000, transcendentals=0),
        name="gram",
    )(in_hbm(history_steps), in_hbm(history_changes), in_hbm(passive_blocks))

    padded = pltpu.VMEM((depth + 6, rows + 6, width, LANES), F32)
    gradient, line = pl.pallas_call(
        sweep_kernel,
        out_shape=(like(shape, F32), like((devices, LANES), F32)),
        in_specs=[VMEM] * 9,
        out_specs=[VMEM] * 2,
        scratch_shapes=[
            padded,
            padded,
            padded,
            pltpu.VMEM((depth * rows * width, LANES), F32),
            pltpu.VMEM((SUMS, LANES), F32),
        ],
        compiler_params=kernel_params(16),
        name="sweeps",
    )(u, odd, even, row_odd, row_even, keep, steps, changes, sums)

    received = lax.all_to_all(line, ("slab", "tile"), 0, 0, tiled=True)

    return pl.pallas_call(
        combine_kernel,
        out_shape=like(shape, F32),
        in_specs=[VMEM] * 4,
        out_specs=HBM,
        scratch_shapes=[pltpu.VMEM(shape, F32), pltpu.SemaphoreType.DMA((depth,))],
        compiler_params=kernel_params(8),
        name="combine",
    )(received, gradient, steps, changes)


def solution(mesh):
    in_specs = (
        P("slab", "tile", None),
        P("slab", "tile", None),
        P("slab", "tile", None),
        P(None, "slab", "tile", None),
        P(None, "slab", "tile", None),
    )
    out_specs = P("slab", "tile", None)
    return jax.shard_map(
        per_device, mesh=mesh, in_specs=in_specs, out_specs=out_specs, check_vma=False
    )
```

```python
import jax
import jax.numpy as jnp
from jax import lax
from jax.experimental import pallas as pl
from jax.experimental.pallas import tpu as pltpu
from jax.sharding import PartitionSpec as P

SWEEPS = 3
MEM = 4

radius_square = 4.0
sharpness = 8.0
threshold = 0.5
diagonal_value = 1.0 + 6.0 * radius_square
coupling = radius_square / diagonal_value

F32 = jnp.float32
LANES = 128
PAIRS = [(i, j) for i in range(MEM) for j in range(i, MEM)]
SY = {pair: n for n, pair in enumerate(PAIRS)}
YY = {pair: len(PAIRS) + n for n, pair in enumerate(PAIRS)}
SG = [2 * len(PAIRS) + n for n in range(MEM)]
YG = [2 * len(PAIRS) + MEM + n for n in range(MEM)]
SUMS = 32

VMEM = pl.BlockSpec(memory_space=pltpu.VMEM)
HBM = pl.BlockSpec(memory_space=pltpu.HBM)


def kernel_params(mib):
    return pltpu.CompilerParams(vmem_limit_bytes=mib * 1024 * 1024)


def weight_kernel(
    sens_hbm,
    dens_hbm,
    u_ref,
    rim_odd_ref,
    rim_even_ref,
    odd_ref,
    even_ref,
    sens_ref,
    dens_ref,
    arrived,
):
    depth, rows, cols = sens_ref.shape
    width = cols // LANES
    layer = rows * width
    slab_odd = lax.rem(lax.axis_index("slab"), 2)
    copies = [
        [
            pltpu.make_async_copy(from_ref.at[z], to_ref.at[z], arrived.at[n, z])
            for n, (from_ref, to_ref) in enumerate(((sens_hbm, sens_ref), (dens_hbm, dens_ref)))
        ]
        for z in range(depth)
    ]
    for pair in copies:
        for copy in pair:
            copy.start()
    denominator = jnp.tanh(F32(sharpness * threshold)) + jnp.tanh(
        F32(sharpness * (1.0 - threshold))
    )
    for z in range(depth):
        for copy in copies[z]:
            copy.wait()
        bend = jnp.tanh(sharpness * (dens_ref[z] - threshold))
        slope = sharpness * (1.0 - bend * bend) / denominator
        value = sens_ref[z] * slope / diagonal_value
        for row in range(0, rows, 8):
            for part in range(width):
                place = pl.ds(z * layer + row * width + part, 8, width)
                u_ref[place, :] = value[row : row + 8, part * LANES : (part + 1) * LANES]

    for rim_ref, layers_ref, top in (
        (rim_odd_ref, odd_ref, slab_odd),
        (rim_even_ref, even_ref, 1 - slab_odd),
    ):

        def put(first, count, z, row):
            place = pl.ds(pl.multiple_of(z * layer + row * width, 8), count * width)
            rim_ref[first * width : (first + count) * width, :] = u_ref[place, :]

        near, second = (depth - 1) * top, 1 + (depth - 3) * top
        put(0, 2, near, 0)
        put(2, 2, near, rows - 2)
        put(4, 1, second, 0)
        put(5, 1, second, rows - 1)
        layers_ref[...] = u_ref[pl.ds(pl.multiple_of(top * layer, 8), SWEEPS * layer), :]


def gram_kernel(
    steps_hbm,
    changes_hbm,
    passive_hbm,
    sums_ref,
    keep_ref,
    steps_ref,
    changes_ref,
    passive_ref,
    arrived,
    passive_arrived,
):
    depth, rows, cols = steps_ref.shape[1:]
    passive_copy = pltpu.make_async_copy(passive_hbm, passive_ref, passive_arrived)
    copies = [
        [
            pltpu.make_async_copy(from_ref.at[:, z], to_ref.at[:, z], arrived.at[n, z])
            for n, (from_ref, to_ref) in enumerate(
                ((steps_hbm, steps_ref), (changes_hbm, changes_ref))
            )
        ]
        for z in range(depth)
    ]
    passive_copy.start()
    for pair in copies:
        for copy in pair:
            copy.start()

    def doubling(shape, dim):
        place = lax.broadcasted_iota(jnp.int32, shape, dim) // 2
        matches = place == lax.broadcasted_iota(jnp.int32, shape, 1 - dim)
        return matches.astype(F32).astype(jnp.bfloat16)

    passive_copy.wait()
    half_rows = passive_ref.shape[1]
    twice_rows = doubling((2 * half_rows, half_rows), 0)
    twice_cols = doubling((LANES, 2 * LANES), 1)
    for z in range(passive_ref.shape[0]):
        blocks = passive_ref[z].astype(F32).astype(jnp.bfloat16)
        blocks = jnp.dot(twice_rows, blocks, preferred_element_type=F32).astype(jnp.bfloat16)
        for col in range(0, passive_ref.shape[2], LANES):
            wide = jnp.dot(
                blocks[:, col : col + LANES], twice_cols, preferred_element_type=F32
            )
            keep_ref[z, :, 2 * col : 2 * col + 2 * LANES] = 1.0 - wide

    sums = (jnp.zeros((8, LANES), F32),) * (2 * len(PAIRS))
    for z in range(depth):
        for copy in copies[z]:
            copy.wait()

        def step(block, sums):
            row = pl.ds(pl.multiple_of(block * 8, 8), 8)
            sums = list(sums)
            for col in range(0, cols, LANES):
                lane = pl.ds(col, LANES)
                s = [steps_ref[i, z, row, lane] for i in range(MEM)]
                y = [changes_ref[i, z, row, lane] for i in range(MEM)]
                for i, j in PAIRS:
                    sums[SY[i, j]] += s[i] * y[j]
                    sums[YY[i, j]] += y[i] * y[j]
            return tuple(sums)

        sums = lax.fori_loop(0, rows // 8, step, sums)
    for n, value in enumerate(sums):
        sums_ref[n : n + 1, :] = jnp.sum(value, axis=0, keepdims=True)


def pack_kernel(u_ref, odd_ref, even_ref, row_odd_ref, row_even_ref):
    depth, rows = u_ref.shape[:2]
    slab_odd = lax.rem(lax.axis_index("slab"), 2)
    tile_odd = lax.rem(lax.axis_index("tile"), 2)

    def pack(low_ref, high_ref, out_ref, top):
        start = rows - 3 if top else 0
        for z in range(depth):
            out_ref[3 * z : 3 * z + 3] = u_ref[z, start : start + 3]
        near, second = (2, 5) if top else (0, 4)
        out_ref[12:14] = low_ref[near : near + 2]
        out_ref[14:16] = high_ref[near : near + 2]
        out_ref[16] = low_ref[second]
        out_ref[17] = high_ref[second]

    for parity in range(2):
        for top in range(2):

            @pl.when((slab_odd == parity) & (tile_odd == top))
            def _():
                low_ref, high_ref = (even_ref, odd_ref) if parity else (odd_ref, even_ref)
                pack(low_ref, high_ref, row_odd_ref, top == 1)
                pack(low_ref, high_ref, row_even_ref, top == 0)


def sweep_kernel(
    u_ref,
    odd_ref,
    even_ref,
    row_odd_ref,
    row_even_ref,
    keep_ref,
    steps_ref,
    changes_ref,
    sums_ref,
    grad_ref,
    send_ref,
    start_ref,
    one_ref,
    two_ref,
    last_ref,
    total_ref,
):
    depth, rows, width = u_ref.shape[:3]
    slab, tile = lax.axis_index("slab"), lax.axis_index("tile")
    slab_odd, tile_odd = lax.rem(slab, 2), lax.rem(tile, 2)
    inside = {
        "low_z": (slab > 0).astype(F32),
        "high_z": (slab < lax.axis_size("slab") - 1).astype(F32),
        "low_y": (tile > 0).astype(F32),
        "high_y": (tile < lax.axis_size("tile") - 1).astype(F32),
    }

    start_ref[3 : 3 + depth, 3 : 3 + rows] = u_ref[...]

    def layers(low_ref, high_ref):
        start_ref[0:3, 3 : 3 + rows] = low_ref[...] * inside["low_z"]
        start_ref[3 + depth :, 3 : 3 + rows] = high_ref[...] * inside["high_z"]

    def edge(from_ref, first, count, z, factor, high):
        to = 3 + rows if high else 3 - count
        start_ref[z, to : to + count] = from_ref[first : first + count] * factor

    def beside(from_ref, high):
        factor = inside["high_y" if high else "low_y"]
        for z in range(depth):
            edge(from_ref, 3 * z, 3, 3 + z, factor, high)
        low_factor, high_factor = factor * inside["low_z"], factor * inside["high_z"]
        edge(from_ref, 12, 2, 2, low_factor, high)
        edge(from_ref, 14, 2, 3 + depth, high_factor, high)
        edge(from_ref, 16, 1, 1, low_factor, high)
        edge(from_ref, 17, 1, 4 + depth, high_factor, high)

    for parity in range(2):

        @pl.when(slab_odd == parity)
        def _():
            layers(*((even_ref, odd_ref) if parity else (odd_ref, even_ref)))

        @pl.when(tile_odd == parity)
        def _():
            beside(row_odd_ref, parity == 1)
            beside(row_even_ref, parity == 0)

    lane = lax.broadcasted_iota(jnp.int32, (width, LANES), 1)
    part = lax.broadcasted_iota(jnp.int32, (width, LANES), 0)
    lane_first, lane_last = lane == 0, lane == LANES - 1
    first, last = lane_first & (part == 0), lane_last & (part == width - 1)

    def relax(from_ref, z, y):
        here = from_ref[z, y]
        around = from_ref[z - 1, y] + from_ref[z + 1, y]
        around += from_ref[z, y - 1] + from_ref[z, y + 1]
        before, after = pltpu.roll(here, 1, 1), pltpu.roll(here, LANES - 1, 1)
        before = jnp.where(lane_first, pltpu.roll(before, 1, 0), before)
        after = jnp.where(lane_last, pltpu.roll(after, width - 1, 0), after)
        around += jnp.where(first, 0.0, before) + jnp.where(last, 0.0, after)
        return start_ref[z, y] + coupling * around

    def factors(z, y):
        if z < 3:
            yield inside["low_z"]
        if z >= 3 + depth:
            yield inside["high_z"]
        if y < 3:
            yield inside["low_y"]
        if y >= 3 + rows:
            yield inside["high_y"]

    def sweep(from_ref, to_ref, reach):
        for z in range(3 - reach, 3 + depth + reach):
            wide = reach - max(3 - z, z - 2 - depth, 0)
            for y in range(3 - wide, 3 + rows + wide):
                value = relax(from_ref, z, y)
                for factor in factors(z, y):
                    value *= factor
                to_ref[z, y] = value

    sweep(start_ref, one_ref, 2)
    sweep(one_ref, two_ref, 1)
    for z in range(depth):
        for y in range(rows):
            place = (z * rows + y) * width
            last_ref[place : place + width, :] = relax(two_ref, 3 + z, 3 + y)

    sums = [jnp.zeros((8, LANES), F32) for _ in range(2 * MEM)]
    for z in range(depth):
        for row in range(0, rows, 8):
            for part in range(width):
                block = slice(row, row + 8), slice(part * LANES, (part + 1) * LANES)
                value = last_ref[pl.ds((z * rows + row) * width + part, 8, width), :]
                value *= keep_ref[z // 2, *block]
                grad_ref[z, *block] = value
                for i in range(MEM):
                    sums[i] += steps_ref[i, z, *block] * value
                    sums[MEM + i] += changes_ref[i, z, *block] * value
    done = 2 * len(PAIRS)
    total_ref[0:done, :] = sums_ref[0:done, :]
    for n, value in enumerate(sums):
        total_ref[done + n : done + n + 1, :] = jnp.sum(value, axis=0, keepdims=True)
    total_ref[done + 2 * MEM :, :] = jnp.zeros((SUMS - done - 2 * MEM, LANES), F32)
    totals = jnp.sum(total_ref[...], axis=1, keepdims=True)
    diagonal = lax.broadcasted_iota(jnp.int32, (SUMS, LANES), 0) == lax.broadcasted_iota(
        jnp.int32, (SUMS, LANES), 1
    )
    line = jnp.sum(jnp.where(diagonal, totals, 0.0), axis=0, keepdims=True)
    send_ref[...] = jnp.broadcast_to(line, send_ref.shape)


def combine_kernel(all_ref, grad_ref, steps_ref, changes_ref, out_hbm, out_ref, left):
    depth, rows, cols = grad_ref.shape
    line = jnp.sum(all_ref[...], axis=0, keepdims=True)

    def entry(n):
        return jnp.broadcast_to(line[:, n : n + 1], (8, LANES))

    sy = {pair: entry(n) for pair, n in SY.items()}
    yy = {pair: entry(n) for pair, n in YY.items()}
    inverse = [1.0 / sy[i, i] for i in range(MEM)]
    alphas = [None] * MEM
    for i in reversed(range(MEM)):
        product = entry(SG[i])
        for j in range(i + 1, MEM):
            product -= alphas[j] * sy[i, j]
        alphas[i] = product * inverse[i]
    scale = sy[MEM - 1, MEM - 1] / yy[MEM - 1, MEM - 1]
    weights = [None] * MEM
    for i in range(MEM):
        product = entry(YG[i])
        for j in range(MEM):
            product -= alphas[j] * yy[min(i, j), max(i, j)]
        product *= scale
        for j in range(i):
            product += weights[j] * sy[j, i]
        weights[i] = alphas[i] - product * inverse[i]
    on_changes = [scale * alphas[i] for i in range(MEM)]
    copies = [
        pltpu.make_async_copy(out_ref.at[z], out_hbm.at[z], left.at[z]) for z in range(depth)
    ]
    for z in range(depth):
        for row in range(0, rows, 8):
            for col in range(0, cols, LANES):
                lane = slice(col, col + LANES)
                value = -scale * grad_ref[z, row : row + 8, lane]
                for i in range(MEM):
                    value += on_changes[i] * changes_ref[i, z, row : row + 8, lane]
                    value -= weights[i] * steps_ref[i, z, row : row + 8, lane]
                out_ref[z, row : row + 8, lane] = value
        copies[z].start()
    for copy in copies:
        copy.wait()


def in_hbm(array):
    return pltpu.with_memory_space_constraint(array, pltpu.HBM)


def swaps(count):
    even = [(i, i ^ 1) for i in range(count)]
    odd = [(i, (i + 1) % count if i % 2 else (i - 1) % count) for i in range(count)]
    return odd, even


def per_device(sensitivity, filtered_density, passive_blocks, history_steps, history_changes):
    shape = sensitivity.shape
    depth, rows, cols = shape
    like = jax.ShapeDtypeStruct
    width = cols // LANES
    lines, layers, rim = (
        like((count * width, LANES), F32) for count in (depth * rows, SWEEPS * rows, 6)
    )
    edges = like((3 * depth + 6, width, LANES), F32)
    devices = lax.axis_size("slab") * lax.axis_size("tile")

    u, rim_odd, rim_even, odd, even = pl.pallas_call(
        weight_kernel,
        out_shape=(lines, rim, rim, layers, layers),
        in_specs=[HBM] * 2,
        out_specs=[VMEM] * 5,
        scratch_shapes=[
            pltpu.VMEM(shape, F32),
            pltpu.VMEM(shape, F32),
            pltpu.SemaphoreType.DMA((2, depth)),
        ],
        compiler_params=kernel_params(8),
        name="weights",
    )(in_hbm(sensitivity), in_hbm(filtered_density))

    u = u.reshape(depth, rows, width, LANES)
    rim_odd, rim_even = (array.reshape(6, width, LANES) for array in (rim_odd, rim_even))
    odd, even = (array.reshape(SWEEPS, rows, width, LANES) for array in (odd, even))

    odd_pairs, even_pairs = swaps(lax.axis_size("slab"))
    rim_odd = lax.ppermute(rim_odd, "slab", odd_pairs)
    rim_even = lax.ppermute(rim_even, "slab", even_pairs)
    odd = lax.ppermute(odd, "slab", odd_pairs)
    even = lax.ppermute(even, "slab", even_pairs)

    row_odd, row_even = pl.pallas_call(
        pack_kernel,
        out_shape=(edges, edges),
        in_specs=[VMEM] * 3,
        out_specs=[VMEM] * 2,
        compiler_params=kernel_params(8),
        name="edges",
    )(u, rim_odd, rim_even)
    odd_pairs, even_pairs = swaps(lax.axis_size("tile"))
    row_odd = lax.ppermute(row_odd, "tile", odd_pairs)
    row_even = lax.ppermute(row_even, "tile", even_pairs)

    history = like(history_steps.shape, F32)
    sums, keep, steps, changes = pl.pallas_call(
        gram_kernel,
        out_shape=(
            like((SUMS, LANES), F32),
            like((depth // 2, rows, cols), F32),
            history,
            history,
        ),
        in_specs=[HBM] * 3,
        out_specs=[VMEM] * 4,
        scratch_shapes=[
            pltpu.VMEM(passive_blocks.shape, jnp.int32),
            pltpu.SemaphoreType.DMA((2, depth)),
            pltpu.SemaphoreType.DMA,
        ],
        compiler_params=kernel_params(8),
        cost_estimate=pl.CostEstimate(flops=8_000_000_000, bytes_accessed=43_000_000, transcendentals=0),
        name="gram",
    )(in_hbm(history_steps), in_hbm(history_changes), in_hbm(passive_blocks))

    padded = pltpu.VMEM((depth + 6, rows + 6, width, LANES), F32)
    gradient, line = pl.pallas_call(
        sweep_kernel,
        out_shape=(like(shape, F32), like((devices, LANES), F32)),
        in_specs=[VMEM] * 9,
        out_specs=[VMEM] * 2,
        scratch_shapes=[
            padded,
            padded,
            padded,
            pltpu.VMEM((depth * rows * width, LANES), F32),
            pltpu.VMEM((SUMS, LANES), F32),
        ],
        compiler_params=kernel_params(16),
        name="sweeps",
    )(u, odd, even, row_odd, row_even, keep, steps, changes, sums)

    received = lax.all_to_all(line, ("slab", "tile"), 0, 0, tiled=True)

    return pl.pallas_call(
        combine_kernel,
        out_shape=like(shape, F32),
        in_specs=[VMEM] * 4,
        out_specs=HBM,
        scratch_shapes=[pltpu.VMEM(shape, F32), pltpu.SemaphoreType.DMA((depth,))],
        compiler_params=kernel_params(8),
        name="combine",
    )(received, gradient, steps, changes)


def solution(mesh):
    in_specs = (
        P("slab", "tile", None),
        P("slab", "tile", None),
        P("slab", "tile", None),
        P(None, "slab", "tile", None),
        P(None, "slab", "tile", None),
    )
    out_specs = P("slab", "tile", None)
    return jax.shard_map(
        per_device, mesh=mesh, in_specs=in_specs, out_specs=out_specs, check_vma=False
    )
```

```python
import jax
import jax.numpy as jnp
from jax import lax
from jax.experimental import pallas as pl
from jax.experimental.pallas import tpu as pltpu
from jax.sharding import PartitionSpec as P

SWEEPS = 3
MEM = 4

radius_square = 4.0
sharpness = 8.0
threshold = 0.5
diagonal_value = 1.0 + 6.0 * radius_square
coupling = radius_square / diagonal_value

F32 = jnp.float32
MESH_AXES = ("slab", "tile")
LANES = 128
PAIRS = [(i, j) for i in range(MEM) for j in range(i, MEM)]
SY = {pair: n for n, pair in enumerate(PAIRS)}
YY = {pair: len(PAIRS) + n for n, pair in enumerate(PAIRS)}
SG = [2 * len(PAIRS) + n for n in range(MEM)]
YG = [2 * len(PAIRS) + MEM + n for n in range(MEM)]
SUMS = 32

VMEM = pl.BlockSpec(memory_space=pltpu.VMEM)
HBM = pl.BlockSpec(memory_space=pltpu.HBM)


def kernel_params(mib):
    return pltpu.CompilerParams(vmem_limit_bytes=mib * 1024 * 1024)


def weight_kernel(
    sens_hbm,
    dens_hbm,
    u_ref,
    rim_odd_ref,
    rim_even_ref,
    odd_ref,
    even_ref,
    sens_ref,
    dens_ref,
    arrived,
):
    depth, rows, cols = sens_ref.shape
    width = cols // LANES
    layer = rows * width
    slab_odd = lax.rem(lax.axis_index("slab"), 2)
    copies = [
        [
            pltpu.make_async_copy(from_ref.at[z], to_ref.at[z], arrived.at[n, z])
            for n, (from_ref, to_ref) in enumerate(((sens_hbm, sens_ref), (dens_hbm, dens_ref)))
        ]
        for z in range(depth)
    ]
    for pair in copies:
        for copy in pair:
            copy.start()
    denominator = jnp.tanh(F32(sharpness * threshold)) + jnp.tanh(
        F32(sharpness * (1.0 - threshold))
    )
    for z in range(depth):
        for copy in copies[z]:
            copy.wait()
        bend = jnp.tanh(sharpness * (dens_ref[z] - threshold))
        slope = sharpness * (1.0 - bend * bend) / denominator
        value = sens_ref[z] * slope / diagonal_value
        for row in range(0, rows, 8):
            for part in range(width):
                place = pl.ds(z * layer + row * width + part, 8, width)
                u_ref[place, :] = value[row : row + 8, part * LANES : (part + 1) * LANES]

    for rim_ref, layers_ref, top in (
        (rim_odd_ref, odd_ref, slab_odd),
        (rim_even_ref, even_ref, 1 - slab_odd),
    ):

        def put(first, count, z, row):
            place = pl.ds(pl.multiple_of(z * layer + row * width, 8), count * width)
            rim_ref[first * width : (first + count) * width, :] = u_ref[place, :]

        near, second = (depth - 1) * top, 1 + (depth - 3) * top
        put(0, 2, near, 0)
        put(2, 2, near, rows - 2)
        put(4, 1, second, 0)
        put(5, 1, second, rows - 1)
        layers_ref[...] = u_ref[pl.ds(pl.multiple_of(top * layer, 8), SWEEPS * layer), :]


def gram_kernel(
    steps_hbm,
    changes_hbm,
    passive_hbm,
    sums_ref,
    keep_ref,
    steps_ref,
    changes_ref,
    passive_ref,
    arrived,
    passive_arrived,
):
    depth, rows, cols = steps_ref.shape[1:]
    passive_copy = pltpu.make_async_copy(passive_hbm, passive_ref, passive_arrived)
    copies = [
        [
            pltpu.make_async_copy(from_ref.at[:, z], to_ref.at[:, z], arrived.at[n, z])
            for n, (from_ref, to_ref) in enumerate(
                ((steps_hbm, steps_ref), (changes_hbm, changes_ref))
            )
        ]
        for z in range(depth)
    ]
    passive_copy.start()
    for pair in copies:
        for copy in pair:
            copy.start()

    def doubling(shape, dim):
        place = lax.broadcasted_iota(jnp.int32, shape, dim) // 2
        matches = place == lax.broadcasted_iota(jnp.int32, shape, 1 - dim)
        return matches.astype(F32).astype(jnp.bfloat16)

    passive_copy.wait()
    half_rows = passive_ref.shape[1]
    twice_rows = doubling((2 * half_rows, half_rows), 0)
    twice_cols = doubling((LANES, 2 * LANES), 1)
    for z in range(passive_ref.shape[0]):
        blocks = passive_ref[z].astype(F32).astype(jnp.bfloat16)
        blocks = jnp.dot(twice_rows, blocks, preferred_element_type=F32).astype(jnp.bfloat16)
        for col in range(0, passive_ref.shape[2], LANES):
            wide = jnp.dot(
                blocks[:, col : col + LANES], twice_cols, preferred_element_type=F32
            )
            keep_ref[z, :, 2 * col : 2 * col + 2 * LANES] = 1.0 - wide

    sums = (jnp.zeros((8, LANES), F32),) * (2 * len(PAIRS))
    for z in range(depth):
        for copy in copies[z]:
            copy.wait()

        def step(block, sums):
            row = pl.ds(pl.multiple_of(block * 8, 8), 8)
            sums = list(sums)
            for col in range(0, cols, LANES):
                lane = pl.ds(col, LANES)
                s = [steps_ref[i, z, row, lane] for i in range(MEM)]
                y = [changes_ref[i, z, row, lane] for i in range(MEM)]
                for i, j in PAIRS:
                    sums[SY[i, j]] += s[i] * y[j]
                    sums[YY[i, j]] += y[i] * y[j]
            return tuple(sums)

        sums = lax.fori_loop(0, rows // 8, step, sums)
    for n, value in enumerate(sums):
        sums_ref[n : n + 1, :] = jnp.sum(value, axis=0, keepdims=True)


def pack_kernel(u_ref, odd_ref, even_ref, row_odd_ref, row_even_ref):
    depth, rows = u_ref.shape[:2]
    slab_odd = lax.rem(lax.axis_index("slab"), 2)
    tile_odd = lax.rem(lax.axis_index("tile"), 2)

    def pack(low_ref, high_ref, out_ref, top):
        start = rows - 3 if top else 0
        for z in range(depth):
            out_ref[3 * z : 3 * z + 3] = u_ref[z, start : start + 3]
        near, second = (2, 5) if top else (0, 4)
        out_ref[12:14] = low_ref[near : near + 2]
        out_ref[14:16] = high_ref[near : near + 2]
        out_ref[16] = low_ref[second]
        out_ref[17] = high_ref[second]

    for parity in range(2):
        for top in range(2):

            @pl.when((slab_odd == parity) & (tile_odd == top))
            def _():
                low_ref, high_ref = (even_ref, odd_ref) if parity else (odd_ref, even_ref)
                pack(low_ref, high_ref, row_odd_ref, top == 1)
                pack(low_ref, high_ref, row_even_ref, top == 0)


def sweep_kernel(
    u_ref,
    odd_ref,
    even_ref,
    row_odd_ref,
    row_even_ref,
    keep_ref,
    steps_ref,
    changes_ref,
    sums_ref,
    grad_ref,
    send_ref,
    start_ref,
    one_ref,
    two_ref,
    last_ref,
    total_ref,
):
    depth, rows, width = u_ref.shape[:3]
    slab, tile = lax.axis_index("slab"), lax.axis_index("tile")
    slab_odd, tile_odd = lax.rem(slab, 2), lax.rem(tile, 2)
    inside = {
        "low_z": (slab > 0).astype(F32),
        "high_z": (slab < lax.axis_size("slab") - 1).astype(F32),
        "low_y": (tile > 0).astype(F32),
        "high_y": (tile < lax.axis_size("tile") - 1).astype(F32),
    }

    start_ref[3 : 3 + depth, 3 : 3 + rows] = u_ref[...]

    def layers(low_ref, high_ref):
        start_ref[0:3, 3 : 3 + rows] = low_ref[...] * inside["low_z"]
        start_ref[3 + depth :, 3 : 3 + rows] = high_ref[...] * inside["high_z"]

    def edge(from_ref, first, count, z, factor, high):
        to = 3 + rows if high else 3 - count
        start_ref[z, to : to + count] = from_ref[first : first + count] * factor

    def beside(from_ref, high):
        factor = inside["high_y" if high else "low_y"]
        for z in range(depth):
            edge(from_ref, 3 * z, 3, 3 + z, factor, high)
        low_factor, high_factor = factor * inside["low_z"], factor * inside["high_z"]
        edge(from_ref, 12, 2, 2, low_factor, high)
        edge(from_ref, 14, 2, 3 + depth, high_factor, high)
        edge(from_ref, 16, 1, 1, low_factor, high)
        edge(from_ref, 17, 1, 4 + depth, high_factor, high)

    for parity in range(2):

        @pl.when(slab_odd == parity)
        def _():
            layers(*((even_ref, odd_ref) if parity else (odd_ref, even_ref)))

        @pl.when(tile_odd == parity)
        def _():
            beside(row_odd_ref, parity == 1)
            beside(row_even_ref, parity == 0)

    lane = lax.broadcasted_iota(jnp.int32, (width, LANES), 1)
    part = lax.broadcasted_iota(jnp.int32, (width, LANES), 0)
    lane_first, lane_last = lane == 0, lane == LANES - 1
    first, last = lane_first & (part == 0), lane_last & (part == width - 1)

    def relax(from_ref, z, y):
        here = from_ref[z, y]
        around = from_ref[z - 1, y] + from_ref[z + 1, y]
        around += from_ref[z, y - 1] + from_ref[z, y + 1]
        before, after = pltpu.roll(here, 1, 1), pltpu.roll(here, LANES - 1, 1)
        before = jnp.where(lane_first, pltpu.roll(before, 1, 0), before)
        after = jnp.where(lane_last, pltpu.roll(after, width - 1, 0), after)
        around += jnp.where(first, 0.0, before) + jnp.where(last, 0.0, after)
        return start_ref[z, y] + coupling * around

    def factors(z, y):
        if z < 3:
            yield inside["low_z"]
        if z >= 3 + depth:
            yield inside["high_z"]
        if y < 3:
            yield inside["low_y"]
        if y >= 3 + rows:
            yield inside["high_y"]

    def sweep(from_ref, to_ref, reach):
        for z in range(3 - reach, 3 + depth + reach):
            wide = reach - max(3 - z, z - 2 - depth, 0)
            for y in range(3 - wide, 3 + rows + wide):
                value = relax(from_ref, z, y)
                for factor in factors(z, y):
                    value *= factor
                to_ref[z, y] = value

    sweep(start_ref, one_ref, 2)
    sweep(one_ref, two_ref, 1)
    for z in range(depth):
        for y in range(rows):
            place = (z * rows + y) * width
            last_ref[place : place + width, :] = relax(two_ref, 3 + z, 3 + y)

    sums = [jnp.zeros((8, LANES), F32) for _ in range(2 * MEM)]
    for z in range(depth):
        for row in range(0, rows, 8):
            for part in range(width):
                block = slice(row, row + 8), slice(part * LANES, (part + 1) * LANES)
                value = last_ref[pl.ds((z * rows + row) * width + part, 8, width), :]
                value *= keep_ref[z // 2, *block]
                grad_ref[z, *block] = value
                for i in range(MEM):
                    sums[i] += steps_ref[i, z, *block] * value
                    sums[MEM + i] += changes_ref[i, z, *block] * value
    done = 2 * len(PAIRS)
    total_ref[0:done, :] = sums_ref[0:done, :]
    for n, value in enumerate(sums):
        total_ref[done + n : done + n + 1, :] = jnp.sum(value, axis=0, keepdims=True)
    total_ref[done + 2 * MEM :, :] = jnp.zeros((SUMS - done - 2 * MEM, LANES), F32)
    totals = jnp.sum(total_ref[...], axis=1, keepdims=True)
    diagonal = lax.broadcasted_iota(jnp.int32, (SUMS, LANES), 0) == lax.broadcasted_iota(
        jnp.int32, (SUMS, LANES), 1
    )
    line = jnp.sum(jnp.where(diagonal, totals, 0.0), axis=0, keepdims=True)
    send_ref[...] = jnp.broadcast_to(line, send_ref.shape)


def combine_kernel(all_ref, grad_ref, steps_ref, changes_ref, out_hbm, out_ref, left):
    depth, rows, cols = grad_ref.shape
    line = jnp.sum(all_ref[...], axis=0, keepdims=True)

    def entry(n):
        return jnp.broadcast_to(line[:, n : n + 1], (8, LANES))

    sy = {pair: entry(n) for pair, n in SY.items()}
    yy = {pair: entry(n) for pair, n in YY.items()}
    inverse = [1.0 / sy[i, i] for i in range(MEM)]
    alphas = [None] * MEM
    for i in reversed(range(MEM)):
        product = entry(SG[i])
        for j in range(i + 1, MEM):
            product -= alphas[j] * sy[i, j]
        alphas[i] = product * inverse[i]
    scale = sy[MEM - 1, MEM - 1] / yy[MEM - 1, MEM - 1]
    weights = [None] * MEM
    for i in range(MEM):
        product = entry(YG[i])
        for j in range(MEM):
            product -= alphas[j] * yy[min(i, j), max(i, j)]
        product *= scale
        for j in range(i):
            product += weights[j] * sy[j, i]
        weights[i] = alphas[i] - product * inverse[i]
    on_changes = [scale * alphas[i] for i in range(MEM)]
    copies = [
        pltpu.make_async_copy(out_ref.at[z], out_hbm.at[z], left.at[z]) for z in range(depth)
    ]
    for z in range(depth):
        for row in range(0, rows, 8):
            for col in range(0, cols, LANES):
                lane = slice(col, col + LANES)
                value = -scale * grad_ref[z, row : row + 8, lane]
                for i in range(MEM):
                    value += on_changes[i] * changes_ref[i, z, row : row + 8, lane]
                    value -= weights[i] * steps_ref[i, z, row : row + 8, lane]
                out_ref[z, row : row + 8, lane] = value
        copies[z].start()
    for copy in copies:
        copy.wait()


def in_hbm(array):
    return pltpu.with_memory_space_constraint(array, pltpu.HBM)


def swaps():
    slabs, tiles = lax.axis_size("slab"), lax.axis_size("tile")
    places = [(slab, tile) for slab in range(slabs) for tile in range(tiles)]
    spare = max(slabs // 4, 1)

    def pairs(partner):
        targets = [partner(*place) for place in places]
        return [(i, slab * tiles + tile) for i, (slab, tile) in enumerate(targets)]

    def slab_odd(slab, tile):
        beside = slab + 1 if slab % 2 else slab - 1
        return (beside, tile) if 0 <= beside < slabs else (slab, tile ^ 1)

    def tile_odd(slab, tile):
        beside = tile + 1 if tile % 2 else tile - 1
        return (slab, beside) if 0 <= beside < tiles else (slab ^ spare, tile)

    return (
        pairs(slab_odd),
        pairs(lambda slab, tile: (slab ^ 1, tile)),
        pairs(tile_odd),
        pairs(lambda slab, tile: (slab, tile ^ 1)),
    )


def per_device(sensitivity, filtered_density, passive_blocks, history_steps, history_changes):
    shape = sensitivity.shape
    depth, rows, cols = shape
    like = jax.ShapeDtypeStruct
    width = cols // LANES
    lines, layers, rim = (
        like((count * width, LANES), F32) for count in (depth * rows, SWEEPS * rows, 6)
    )
    edges = like((3 * depth + 6, width, LANES), F32)
    devices = lax.axis_size("slab") * lax.axis_size("tile")

    u, rim_odd, rim_even, odd, even = pl.pallas_call(
        weight_kernel,
        out_shape=(lines, rim, rim, layers, layers),
        in_specs=[HBM] * 2,
        out_specs=[VMEM] * 5,
        scratch_shapes=[
            pltpu.VMEM(shape, F32),
            pltpu.VMEM(shape, F32),
            pltpu.SemaphoreType.DMA((2, depth)),
        ],
        compiler_params=kernel_params(8),
        name="weights",
    )(in_hbm(sensitivity), in_hbm(filtered_density))

    u = u.reshape(depth, rows, width, LANES)
    rim_odd, rim_even = (array.reshape(6, width, LANES) for array in (rim_odd, rim_even))
    odd, even = (array.reshape(SWEEPS, rows, width, LANES) for array in (odd, even))

    slab_odd, slab_even, tile_odd, tile_even = swaps()
    rim_odd = lax.ppermute(rim_odd, MESH_AXES, slab_odd)
    rim_even = lax.ppermute(rim_even, MESH_AXES, slab_even)
    odd = lax.ppermute(odd, MESH_AXES, slab_odd)
    even = lax.ppermute(even, MESH_AXES, slab_even)

    row_odd, row_even = pl.pallas_call(
        pack_kernel,
        out_shape=(edges, edges),
        in_specs=[VMEM] * 3,
        out_specs=[VMEM] * 2,
        compiler_params=kernel_params(8),
        name="edges",
    )(u, rim_odd, rim_even)
    row_odd = lax.ppermute(row_odd, MESH_AXES, tile_odd)
    row_even = lax.ppermute(row_even, MESH_AXES, tile_even)

    history = like(history_steps.shape, F32)
    sums, keep, steps, changes = pl.pallas_call(
        gram_kernel,
        out_shape=(
            like((SUMS, LANES), F32),
            like((depth // 2, rows, cols), F32),
            history,
            history,
        ),
        in_specs=[HBM] * 3,
        out_specs=[VMEM] * 4,
        scratch_shapes=[
            pltpu.VMEM(passive_blocks.shape, jnp.int32),
            pltpu.SemaphoreType.DMA((2, depth)),
            pltpu.SemaphoreType.DMA,
        ],
        compiler_params=kernel_params(8),
        cost_estimate=pl.CostEstimate(flops=8_000_000_000, bytes_accessed=43_000_000, transcendentals=0),
        name="gram",
    )(in_hbm(history_steps), in_hbm(history_changes), in_hbm(passive_blocks))

    padded = pltpu.VMEM((depth + 6, rows + 6, width, LANES), F32)
    gradient, line = pl.pallas_call(
        sweep_kernel,
        out_shape=(like(shape, F32), like((devices, LANES), F32)),
        in_specs=[VMEM] * 9,
        out_specs=[VMEM] * 2,
        scratch_shapes=[
            padded,
            padded,
            padded,
            pltpu.VMEM((depth * rows * width, LANES), F32),
            pltpu.VMEM((SUMS, LANES), F32),
        ],
        compiler_params=kernel_params(16),
        name="sweeps",
    )(u, odd, even, row_odd, row_even, keep, steps, changes, sums)

    received = lax.all_to_all(line, MESH_AXES, 0, 0, tiled=True)

    return pl.pallas_call(
        combine_kernel,
        out_shape=like(shape, F32),
        in_specs=[VMEM] * 4,
        out_specs=HBM,
        scratch_shapes=[pltpu.VMEM(shape, F32), pltpu.SemaphoreType.DMA((depth,))],
        compiler_params=kernel_params(8),
        name="combine",
    )(received, gradient, steps, changes)


def solution(mesh):
    in_specs = (
        P("slab", "tile", None),
        P("slab", "tile", None),
        P("slab", "tile", None),
        P(None, "slab", "tile", None),
        P(None, "slab", "tile", None),
    )
    out_specs = P("slab", "tile", None)
    return jax.shard_map(
        per_device, mesh=mesh, in_specs=in_specs, out_specs=out_specs, check_vma=False
    )
```

```python
import jax
import jax.numpy as jnp
from jax import lax
from jax.experimental import pallas as pl
from jax.experimental.pallas import tpu as pltpu
from jax.sharding import PartitionSpec as P

SWEEPS = 3
MEM = 4

radius_square = 4.0
sharpness = 8.0
threshold = 0.5
diagonal_value = 1.0 + 6.0 * radius_square
coupling = radius_square / diagonal_value

F32 = jnp.float32
MESH_AXES = ("slab", "tile")
LANES = 128
PAIRS = [(i, j) for i in range(MEM) for j in range(i, MEM)]
SY = {pair: n for n, pair in enumerate(PAIRS)}
YY = {pair: len(PAIRS) + n for n, pair in enumerate(PAIRS)}
SG = [2 * len(PAIRS) + n for n in range(MEM)]
YG = [2 * len(PAIRS) + MEM + n for n in range(MEM)]
SUMS = 32

VMEM = pl.BlockSpec(memory_space=pltpu.VMEM)
HBM = pl.BlockSpec(memory_space=pltpu.HBM)


def kernel_params(mib):
    return pltpu.CompilerParams(vmem_limit_bytes=mib * 1024 * 1024)


def weight_kernel(
    sens_hbm,
    dens_hbm,
    u_ref,
    rim_odd_ref,
    rim_even_ref,
    odd_ref,
    even_ref,
    sens_ref,
    dens_ref,
    arrived,
):
    depth, rows, cols = sens_ref.shape
    width = cols // LANES
    layer = rows * width
    slab_odd = lax.rem(lax.axis_index("slab"), 2)
    copies = [
        [
            pltpu.make_async_copy(from_ref.at[z], to_ref.at[z], arrived.at[n, z])
            for n, (from_ref, to_ref) in enumerate(((sens_hbm, sens_ref), (dens_hbm, dens_ref)))
        ]
        for z in range(depth)
    ]
    for pair in copies:
        for copy in pair:
            copy.start()
    denominator = jnp.tanh(F32(sharpness * threshold)) + jnp.tanh(
        F32(sharpness * (1.0 - threshold))
    )
    for z in range(depth):
        for copy in copies[z]:
            copy.wait()
        bend = jnp.tanh(sharpness * (dens_ref[z] - threshold))
        slope = sharpness * (1.0 - bend * bend) / denominator
        value = sens_ref[z] * slope / diagonal_value
        for row in range(0, rows, 8):
            for part in range(width):
                place = pl.ds(z * layer + row * width + part, 8, width)
                u_ref[place, :] = value[row : row + 8, part * LANES : (part + 1) * LANES]

    for rim_ref, layers_ref, top in (
        (rim_odd_ref, odd_ref, slab_odd),
        (rim_even_ref, even_ref, 1 - slab_odd),
    ):

        def put(first, count, z, row):
            place = pl.ds(pl.multiple_of(z * layer + row * width, 8), count * width)
            rim_ref[first * width : (first + count) * width, :] = u_ref[place, :]

        near, second = (depth - 1) * top, 1 + (depth - 3) * top
        put(0, 2, near, 0)
        put(2, 2, near, rows - 2)
        put(4, 1, second, 0)
        put(5, 1, second, rows - 1)
        layers_ref[...] = u_ref[pl.ds(pl.multiple_of(top * layer, 8), SWEEPS * layer), :]


def gram_kernel(
    steps_hbm,
    changes_hbm,
    passive_hbm,
    sums_ref,
    keep_ref,
    steps_ref,
    changes_ref,
    passive_ref,
    arrived,
    passive_arrived,
):
    depth, rows, cols = steps_ref.shape[1:]
    passive_copy = pltpu.make_async_copy(passive_hbm, passive_ref, passive_arrived)
    copies = [
        [
            pltpu.make_async_copy(from_ref.at[:, z], to_ref.at[:, z], arrived.at[n, z])
            for n, (from_ref, to_ref) in enumerate(
                ((steps_hbm, steps_ref), (changes_hbm, changes_ref))
            )
        ]
        for z in range(depth)
    ]
    passive_copy.start()
    for pair in copies:
        for copy in pair:
            copy.start()

    def doubling(shape, dim):
        place = lax.broadcasted_iota(jnp.int32, shape, dim) // 2
        matches = place == lax.broadcasted_iota(jnp.int32, shape, 1 - dim)
        return matches.astype(F32).astype(jnp.bfloat16)

    passive_copy.wait()
    half_rows = passive_ref.shape[1]
    twice_rows = doubling((2 * half_rows, half_rows), 0)
    twice_cols = doubling((LANES, 2 * LANES), 1)
    for z in range(passive_ref.shape[0]):
        blocks = passive_ref[z].astype(F32).astype(jnp.bfloat16)
        blocks = jnp.dot(twice_rows, blocks, preferred_element_type=F32).astype(jnp.bfloat16)
        for col in range(0, passive_ref.shape[2], LANES):
            wide = jnp.dot(
                blocks[:, col : col + LANES], twice_cols, preferred_element_type=F32
            )
            keep_ref[z, :, 2 * col : 2 * col + 2 * LANES] = 1.0 - wide

    sums = (jnp.zeros((8, LANES), F32),) * (2 * len(PAIRS))
    for z in range(depth):
        for copy in copies[z]:
            copy.wait()

        def step(block, sums):
            row = pl.ds(pl.multiple_of(block * 8, 8), 8)
            sums = list(sums)
            for col in range(0, cols, LANES):
                lane = pl.ds(col, LANES)
                s = [steps_ref[i, z, row, lane] for i in range(MEM)]
                y = [changes_ref[i, z, row, lane] for i in range(MEM)]
                for i, j in PAIRS:
                    sums[SY[i, j]] += s[i] * y[j]
                    sums[YY[i, j]] += y[i] * y[j]
            return tuple(sums)

        sums = lax.fori_loop(0, rows // 8, step, sums)
    for n, value in enumerate(sums):
        sums_ref[n : n + 1, :] = jnp.sum(value, axis=0, keepdims=True)


def pack_kernel(u_ref, odd_ref, even_ref, row_odd_ref, row_even_ref):
    depth, rows = u_ref.shape[:2]
    slab_odd = lax.rem(lax.axis_index("slab"), 2)
    tile_odd = lax.rem(lax.axis_index("tile"), 2)

    def pack(low_ref, high_ref, out_ref, top):
        start = rows - 3 if top else 0
        for z in range(depth):
            out_ref[3 * z : 3 * z + 3] = u_ref[z, start : start + 3]
        near, second = (2, 5) if top else (0, 4)
        out_ref[12:14] = low_ref[near : near + 2]
        out_ref[14:16] = high_ref[near : near + 2]
        out_ref[16] = low_ref[second]
        out_ref[17] = high_ref[second]

    for parity in range(2):
        for top in range(2):

            @pl.when((slab_odd == parity) & (tile_odd == top))
            def _():
                low_ref, high_ref = (even_ref, odd_ref) if parity else (odd_ref, even_ref)
                pack(low_ref, high_ref, row_odd_ref, top == 1)
                pack(low_ref, high_ref, row_even_ref, top == 0)


def grid_ends():
    slab, tile = lax.axis_index("slab"), lax.axis_index("tile")
    return {
        "low_z": (slab > 0).astype(F32),
        "high_z": (slab < lax.axis_size("slab") - 1).astype(F32),
        "low_y": (tile > 0).astype(F32),
        "high_y": (tile < lax.axis_size("tile") - 1).astype(F32),
    }


def line_sweep(width, depth, rows, inside):
    lane = lax.broadcasted_iota(jnp.int32, (width, LANES), 1)
    group = lax.broadcasted_iota(jnp.int32, (width, LANES), 0)
    lane_first, lane_last = lane == 0, lane == LANES - 1
    first, last = lane_first & (group == 0), lane_last & (group == width - 1)

    def relax(start, field, z, y):
        here = field(z, y)
        around = field(z - 1, y) + field(z + 1, y)
        around += field(z, y - 1) + field(z, y + 1)
        before, after = pltpu.roll(here, 1, 1), pltpu.roll(here, LANES - 1, 1)
        before = jnp.where(lane_first, pltpu.roll(before, 1, 0), before)
        after = jnp.where(lane_last, pltpu.roll(after, width - 1, 0), after)
        around += jnp.where(first, 0.0, before) + jnp.where(last, 0.0, after)
        value = start(z, y) + coupling * around
        if z < 3:
            value *= inside["low_z"]
        if z >= 3 + depth:
            value *= inside["high_z"]
        if y < 3:
            value *= inside["low_y"]
        if y >= 3 + rows:
            value *= inside["high_y"]
        return value

    return relax


def inner_kernel(u_ref, odd_ref, even_ref, start_ref, one_ref, two_ref, last_ref):
    depth, rows, width = u_ref.shape[:3]
    slab_odd = lax.rem(lax.axis_index("slab"), 2)
    inside = grid_ends()
    start_ref[3 : 3 + depth] = u_ref[...]
    for parity in range(2):

        @pl.when(slab_odd == parity)
        def _():
            low_ref, high_ref = (even_ref, odd_ref) if parity else (odd_ref, even_ref)
            start_ref[0:3] = low_ref[...] * inside["low_z"]
            start_ref[3 + depth :] = high_ref[...] * inside["high_z"]

    relax = line_sweep(width, depth, rows, inside)

    def reader(ref):
        return lambda z, y: ref[z, y - 3]

    start, one, two = reader(start_ref), reader(one_ref), reader(two_ref)
    for z in range(1, 5 + depth):
        for y in range(4, 2 + rows):
            one_ref[z, y - 3] = relax(start, start, z, y)
    for z in range(2, 4 + depth):
        for y in range(5, 1 + rows):
            two_ref[z, y - 3] = relax(start, one, z, y)
    for z in range(3, 3 + depth):
        for y in range(6, rows):
            place = ((z - 3) * rows + y - 3) * width
            last_ref[place : place + width, :] = relax(start, two, z, y)


def outer_kernel(
    row_odd_ref,
    row_even_ref,
    inner_start_ref,
    inner_one_ref,
    inner_two_ref,
    inner_last_ref,
    keep_ref,
    steps_ref,
    changes_ref,
    sums_ref,
    grad_ref,
    send_ref,
    start_ref,
    one_ref,
    two_ref,
    last_ref,
    total_ref,
):
    depth, rows = grad_ref.shape[:2]
    width = start_ref.shape[2]
    tile_odd = lax.rem(lax.axis_index("tile"), 2)
    inside = grid_ends()

    def edge(from_ref, first, count, z, factor, high):
        to = 3 + rows if high else 3 - count
        start_ref[z, to : to + count] = from_ref[first : first + count] * factor

    def beside(from_ref, high):
        factor = inside["high_y" if high else "low_y"]
        for z in range(depth):
            edge(from_ref, 3 * z, 3, 3 + z, factor, high)
        low_factor, high_factor = factor * inside["low_z"], factor * inside["high_z"]
        edge(from_ref, 12, 2, 2, low_factor, high)
        edge(from_ref, 14, 2, 3 + depth, high_factor, high)
        edge(from_ref, 16, 1, 1, low_factor, high)
        edge(from_ref, 17, 1, 4 + depth, high_factor, high)

    for parity in range(2):

        @pl.when(tile_odd == parity)
        def _():
            beside(row_odd_ref, parity == 1)
            beside(row_even_ref, parity == 0)

    relax = line_sweep(width, depth, rows, inside)

    def reader(inner_ref, outer_ref, level):
        def read(z, y):
            inner = 3 + level <= y < 3 + rows - level
            return inner_ref[z, y - 3] if inner else outer_ref[z, y]

        return read

    start = reader(inner_start_ref, start_ref, 0)
    one = reader(inner_one_ref, one_ref, 1)
    two = reader(inner_two_ref, two_ref, 2)

    def edge_lines(level):
        reach = SWEEPS - level
        for z in range(3 - reach, 3 + depth + reach):
            wide = reach - max(3 - z, z - 2 - depth, 0)
            for y in range(3 - wide, 3 + rows + wide):
                if not 3 + level <= y < 3 + rows - level:
                    yield z, y

    for z, y in edge_lines(1):
        one_ref[z, y] = relax(start, start, z, y)
    for z, y in edge_lines(2):
        two_ref[z, y] = relax(start, one, z, y)
    for z in range(depth):
        place = slice((z * rows + 3) * width, (z * rows + rows - 3) * width)
        last_ref[place, :] = inner_last_ref[place, :]
    for z, y in edge_lines(3):
        place = ((z - 3) * rows + y - 3) * width
        last_ref[place : place + width, :] = relax(start, two, z, y)

    sums = [jnp.zeros((8, LANES), F32) for _ in range(2 * MEM)]
    for z in range(depth):
        for row in range(0, rows, 8):
            for part in range(width):
                block = slice(row, row + 8), slice(part * LANES, (part + 1) * LANES)
                value = last_ref[pl.ds((z * rows + row) * width + part, 8, width), :]
                value *= keep_ref[z // 2, *block]
                grad_ref[z, *block] = value
                for i in range(MEM):
                    sums[i] += steps_ref[i, z, *block] * value
                    sums[MEM + i] += changes_ref[i, z, *block] * value
    done = 2 * len(PAIRS)
    total_ref[0:done, :] = sums_ref[0:done, :]
    for n, value in enumerate(sums):
        total_ref[done + n : done + n + 1, :] = jnp.sum(value, axis=0, keepdims=True)
    total_ref[done + 2 * MEM :, :] = jnp.zeros((SUMS - done - 2 * MEM, LANES), F32)
    totals = jnp.sum(total_ref[...], axis=1, keepdims=True)
    diagonal = lax.broadcasted_iota(jnp.int32, (SUMS, LANES), 0) == lax.broadcasted_iota(
        jnp.int32, (SUMS, LANES), 1
    )
    line = jnp.sum(jnp.where(diagonal, totals, 0.0), axis=0, keepdims=True)
    send_ref[...] = jnp.broadcast_to(line, send_ref.shape)


def combine_kernel(all_ref, grad_ref, steps_ref, changes_ref, out_hbm, out_ref, left):
    depth, rows, cols = grad_ref.shape
    line = jnp.sum(all_ref[...], axis=0, keepdims=True)

    def entry(n):
        return jnp.broadcast_to(line[:, n : n + 1], (8, LANES))

    sy = {pair: entry(n) for pair, n in SY.items()}
    yy = {pair: entry(n) for pair, n in YY.items()}
    inverse = [1.0 / sy[i, i] for i in range(MEM)]
    alphas = [None] * MEM
    for i in reversed(range(MEM)):
        product = entry(SG[i])
        for j in range(i + 1, MEM):
            product -= alphas[j] * sy[i, j]
        alphas[i] = product * inverse[i]
    scale = sy[MEM - 1, MEM - 1] / yy[MEM - 1, MEM - 1]
    weights = [None] * MEM
    for i in range(MEM):
        product = entry(YG[i])
        for j in range(MEM):
            product -= alphas[j] * yy[min(i, j), max(i, j)]
        product *= scale
        for j in range(i):
            product += weights[j] * sy[j, i]
        weights[i] = alphas[i] - product * inverse[i]
    on_changes = [scale * alphas[i] for i in range(MEM)]
    copies = [
        pltpu.make_async_copy(out_ref.at[z], out_hbm.at[z], left.at[z]) for z in range(depth)
    ]
    for z in range(depth):
        for row in range(0, rows, 8):
            for col in range(0, cols, LANES):
                lane = slice(col, col + LANES)
                value = -scale * grad_ref[z, row : row + 8, lane]
                for i in range(MEM):
                    value += on_changes[i] * changes_ref[i, z, row : row + 8, lane]
                    value -= weights[i] * steps_ref[i, z, row : row + 8, lane]
                out_ref[z, row : row + 8, lane] = value
        copies[z].start()
    for copy in copies:
        copy.wait()


def in_hbm(array):
    return pltpu.with_memory_space_constraint(array, pltpu.HBM)


def swaps():
    slabs, tiles = lax.axis_size("slab"), lax.axis_size("tile")
    places = [(slab, tile) for slab in range(slabs) for tile in range(tiles)]
    spare = max(slabs // 4, 1)

    def pairs(partner):
        targets = [partner(*place) for place in places]
        return [(i, slab * tiles + tile) for i, (slab, tile) in enumerate(targets)]

    def slab_odd(slab, tile):
        beside = slab + 1 if slab % 2 else slab - 1
        return (beside, tile) if 0 <= beside < slabs else (slab, tile ^ 1)

    def tile_odd(slab, tile):
        beside = tile + 1 if tile % 2 else tile - 1
        return (slab, beside) if 0 <= beside < tiles else (slab ^ spare, tile)

    return (
        pairs(slab_odd),
        pairs(lambda slab, tile: (slab ^ 1, tile)),
        pairs(tile_odd),
        pairs(lambda slab, tile: (slab, tile ^ 1)),
    )


def per_device(sensitivity, filtered_density, passive_blocks, history_steps, history_changes):
    shape = sensitivity.shape
    depth, rows, cols = shape
    like = jax.ShapeDtypeStruct
    width = cols // LANES
    lines, layers, rim = (
        like((count * width, LANES), F32) for count in (depth * rows, SWEEPS * rows, 6)
    )
    edges = like((3 * depth + 6, width, LANES), F32)
    devices = lax.axis_size("slab") * lax.axis_size("tile")

    u, rim_odd, rim_even, odd, even = pl.pallas_call(
        weight_kernel,
        out_shape=(lines, rim, rim, layers, layers),
        in_specs=[HBM] * 2,
        out_specs=[VMEM] * 5,
        scratch_shapes=[
            pltpu.VMEM(shape, F32),
            pltpu.VMEM(shape, F32),
            pltpu.SemaphoreType.DMA((2, depth)),
        ],
        compiler_params=kernel_params(8),
        name="weights",
    )(in_hbm(sensitivity), in_hbm(filtered_density))

    u = u.reshape(depth, rows, width, LANES)
    rim_odd, rim_even = (array.reshape(6, width, LANES) for array in (rim_odd, rim_even))
    odd, even = (array.reshape(SWEEPS, rows, width, LANES) for array in (odd, even))

    slab_odd, slab_even, tile_odd, tile_even = swaps()
    rim_odd = lax.ppermute(rim_odd, MESH_AXES, slab_odd)
    rim_even = lax.ppermute(rim_even, MESH_AXES, slab_even)
    odd = lax.ppermute(odd, MESH_AXES, slab_odd)
    even = lax.ppermute(even, MESH_AXES, slab_even)

    row_odd, row_even = pl.pallas_call(
        pack_kernel,
        out_shape=(edges, edges),
        in_specs=[VMEM] * 3,
        out_specs=[VMEM] * 2,
        compiler_params=kernel_params(8),
        name="edges",
    )(u, rim_odd, rim_even)
    row_odd = lax.ppermute(row_odd, MESH_AXES, tile_odd)
    row_even = lax.ppermute(row_even, MESH_AXES, tile_even)

    history = like(history_steps.shape, F32)
    sums, keep, steps, changes = pl.pallas_call(
        gram_kernel,
        out_shape=(
            like((SUMS, LANES), F32),
            like((depth // 2, rows, cols), F32),
            history,
            history,
        ),
        in_specs=[HBM] * 3,
        out_specs=[VMEM] * 4,
        scratch_shapes=[
            pltpu.VMEM(passive_blocks.shape, jnp.int32),
            pltpu.SemaphoreType.DMA((2, depth)),
            pltpu.SemaphoreType.DMA,
        ],
        compiler_params=kernel_params(8),
        cost_estimate=pl.CostEstimate(flops=8_000_000_000, bytes_accessed=43_000_000, transcendentals=0),
        name="gram",
    )(in_hbm(history_steps), in_hbm(history_changes), in_hbm(passive_blocks))

    field = like((depth + 6, rows, width, LANES), F32)
    inner = pl.pallas_call(
        inner_kernel,
        out_shape=(field, field, field, lines),
        in_specs=[VMEM] * 3,
        out_specs=[VMEM] * 4,
        compiler_params=kernel_params(8),
        name="inner",
    )(u, odd, even)

    padded = pltpu.VMEM((depth + 6, rows + 6, width, LANES), F32)
    gradient, line = pl.pallas_call(
        outer_kernel,
        out_shape=(like(shape, F32), like((devices, LANES), F32)),
        in_specs=[VMEM] * 10,
        out_specs=[VMEM] * 2,
        scratch_shapes=[
            padded,
            padded,
            padded,
            pltpu.VMEM((depth * rows * width, LANES), F32),
            pltpu.VMEM((SUMS, LANES), F32),
        ],
        compiler_params=kernel_params(16),
        name="outer",
    )(row_odd, row_even, *inner, keep, steps, changes, sums)

    received = lax.all_to_all(line, MESH_AXES, 0, 0, tiled=True)

    return pl.pallas_call(
        combine_kernel,
        out_shape=like(shape, F32),
        in_specs=[VMEM] * 4,
        out_specs=HBM,
        scratch_shapes=[pltpu.VMEM(shape, F32), pltpu.SemaphoreType.DMA((depth,))],
        compiler_params=kernel_params(8),
        name="combine",
    )(received, gradient, steps, changes)


def solution(mesh):
    in_specs = (
        P("slab", "tile", None),
        P("slab", "tile", None),
        P("slab", "tile", None),
        P(None, "slab", "tile", None),
        P(None, "slab", "tile", None),
    )
    out_specs = P("slab", "tile", None)
    return jax.shard_map(
        per_device, mesh=mesh, in_specs=in_specs, out_specs=out_specs, check_vma=False
    )
```

```python
import jax
import jax.numpy as jnp
from jax import lax
from jax.experimental import pallas as pl
from jax.experimental.pallas import tpu as pltpu
from jax.sharding import PartitionSpec as P

SWEEPS = 3
MEM = 4

radius_square = 4.0
sharpness = 8.0
threshold = 0.5
diagonal_value = 1.0 + 6.0 * radius_square
coupling = radius_square / diagonal_value

F32 = jnp.float32
MESH_AXES = ("slab", "tile")
LANES = 128
PAIRS = [(i, j) for i in range(MEM) for j in range(i, MEM)]
SY = {pair: n for n, pair in enumerate(PAIRS)}
YY = {pair: len(PAIRS) + n for n, pair in enumerate(PAIRS)}
SG = [2 * len(PAIRS) + n for n in range(MEM)]
YG = [2 * len(PAIRS) + MEM + n for n in range(MEM)]
SUMS = 32

VMEM = pl.BlockSpec(memory_space=pltpu.VMEM)
HBM = pl.BlockSpec(memory_space=pltpu.HBM)


def kernel_params(mib):
    return pltpu.CompilerParams(vmem_limit_bytes=mib * 1024 * 1024)


def weight_kernel(
    sens_hbm,
    dens_hbm,
    u_ref,
    rim_odd_ref,
    rim_even_ref,
    odd_ref,
    even_ref,
    sens_ref,
    dens_ref,
    arrived,
):
    depth, rows, cols = sens_ref.shape
    width = cols // LANES
    layer = rows * width
    slab_odd = lax.rem(lax.axis_index("slab"), 2)
    copies = [
        [
            pltpu.make_async_copy(from_ref.at[z], to_ref.at[z], arrived.at[n, z])
            for n, (from_ref, to_ref) in enumerate(((sens_hbm, sens_ref), (dens_hbm, dens_ref)))
        ]
        for z in range(depth)
    ]
    for pair in copies:
        for copy in pair:
            copy.start()
    denominator = jnp.tanh(F32(sharpness * threshold)) + jnp.tanh(
        F32(sharpness * (1.0 - threshold))
    )
    for z in range(depth):
        for copy in copies[z]:
            copy.wait()
        bend = jnp.tanh(sharpness * (dens_ref[z] - threshold))
        slope = sharpness * (1.0 - bend * bend) / denominator
        value = sens_ref[z] * slope / diagonal_value
        for row in range(0, rows, 8):
            for part in range(width):
                place = pl.ds(z * layer + row * width + part, 8, width)
                u_ref[place, :] = value[row : row + 8, part * LANES : (part + 1) * LANES]

    for rim_ref, layers_ref, top in (
        (rim_odd_ref, odd_ref, slab_odd),
        (rim_even_ref, even_ref, 1 - slab_odd),
    ):

        def put(first, count, z, row):
            place = pl.ds(pl.multiple_of(z * layer + row * width, 8), count * width)
            rim_ref[first * width : (first + count) * width, :] = u_ref[place, :]

        near, second = (depth - 1) * top, 1 + (depth - 3) * top
        put(0, 2, near, 0)
        put(2, 2, near, rows - 2)
        put(4, 1, second, 0)
        put(5, 1, second, rows - 1)
        layers_ref[...] = u_ref[pl.ds(pl.multiple_of(top * layer, 8), SWEEPS * layer), :]


def gram_kernel(
    steps_hbm,
    changes_hbm,
    passive_hbm,
    sums_ref,
    keep_ref,
    steps_ref,
    changes_ref,
    passive_ref,
    arrived,
    passive_arrived,
):
    depth, rows, cols = steps_ref.shape[1:]
    passive_copy = pltpu.make_async_copy(passive_hbm, passive_ref, passive_arrived)
    copies = [
        [
            pltpu.make_async_copy(from_ref.at[:, z], to_ref.at[:, z], arrived.at[n, z])
            for n, (from_ref, to_ref) in enumerate(
                ((steps_hbm, steps_ref), (changes_hbm, changes_ref))
            )
        ]
        for z in range(depth)
    ]
    passive_copy.start()
    for pair in copies:
        for copy in pair:
            copy.start()

    def doubling(shape, dim):
        place = lax.broadcasted_iota(jnp.int32, shape, dim) // 2
        matches = place == lax.broadcasted_iota(jnp.int32, shape, 1 - dim)
        return matches.astype(F32).astype(jnp.bfloat16)

    passive_copy.wait()
    half_rows = passive_ref.shape[1]
    twice_rows = doubling((2 * half_rows, half_rows), 0)
    twice_cols = doubling((LANES, 2 * LANES), 1)
    for z in range(passive_ref.shape[0]):
        blocks = passive_ref[z].astype(F32).astype(jnp.bfloat16)
        blocks = jnp.dot(twice_rows, blocks, preferred_element_type=F32).astype(jnp.bfloat16)
        for col in range(0, passive_ref.shape[2], LANES):
            wide = jnp.dot(
                blocks[:, col : col + LANES], twice_cols, preferred_element_type=F32
            )
            keep_ref[z, :, 2 * col : 2 * col + 2 * LANES] = 1.0 - wide

    sums = (jnp.zeros((8, LANES), F32),) * (2 * len(PAIRS))
    for z in range(depth):
        for copy in copies[z]:
            copy.wait()

        def step(block, sums):
            row = pl.ds(pl.multiple_of(block * 8, 8), 8)
            sums = list(sums)
            for col in range(0, cols, LANES):
                lane = pl.ds(col, LANES)
                s = [steps_ref[i, z, row, lane] for i in range(MEM)]
                y = [changes_ref[i, z, row, lane] for i in range(MEM)]
                for i, j in PAIRS:
                    sums[SY[i, j]] += s[i] * y[j]
                    sums[YY[i, j]] += y[i] * y[j]
            return tuple(sums)

        sums = lax.fori_loop(0, rows // 8, step, sums)
    for n, value in enumerate(sums):
        sums_ref[n : n + 1, :] = jnp.sum(value, axis=0, keepdims=True)


def pack_kernel(u_ref, odd_ref, even_ref, row_odd_ref, row_even_ref):
    depth, rows = u_ref.shape[:2]
    slab_odd = lax.rem(lax.axis_index("slab"), 2)
    tile_odd = lax.rem(lax.axis_index("tile"), 2)

    def pack(low_ref, high_ref, out_ref, top):
        start = rows - 3 if top else 0
        for z in range(depth):
            out_ref[3 * z : 3 * z + 3] = u_ref[z, start : start + 3]
        near, second = (2, 5) if top else (0, 4)
        out_ref[12:14] = low_ref[near : near + 2]
        out_ref[14:16] = high_ref[near : near + 2]
        out_ref[16] = low_ref[second]
        out_ref[17] = high_ref[second]

    for parity in range(2):
        for top in range(2):

            @pl.when((slab_odd == parity) & (tile_odd == top))
            def _():
                low_ref, high_ref = (even_ref, odd_ref) if parity else (odd_ref, even_ref)
                pack(low_ref, high_ref, row_odd_ref, top == 1)
                pack(low_ref, high_ref, row_even_ref, top == 0)


def grid_ends():
    slab, tile = lax.axis_index("slab"), lax.axis_index("tile")
    return {
        "low_z": (slab > 0).astype(F32),
        "high_z": (slab < lax.axis_size("slab") - 1).astype(F32),
        "low_y": (tile > 0).astype(F32),
        "high_y": (tile < lax.axis_size("tile") - 1).astype(F32),
    }


def line_sweep(width, depth, rows, inside):
    lane = lax.broadcasted_iota(jnp.int32, (width, LANES), 1)
    group = lax.broadcasted_iota(jnp.int32, (width, LANES), 0)
    lane_first, lane_last = lane == 0, lane == LANES - 1
    first, last = lane_first & (group == 0), lane_last & (group == width - 1)

    def relax(start, field, z, y):
        here = field(z, y)
        around = field(z - 1, y) + field(z + 1, y)
        around += field(z, y - 1) + field(z, y + 1)
        before, after = pltpu.roll(here, 1, 1), pltpu.roll(here, LANES - 1, 1)
        before = jnp.where(lane_first, pltpu.roll(before, 1, 0), before)
        after = jnp.where(lane_last, pltpu.roll(after, width - 1, 0), after)
        around += jnp.where(first, 0.0, before) + jnp.where(last, 0.0, after)
        value = start(z, y) + coupling * around
        if z < 3:
            value *= inside["low_z"]
        if z >= 3 + depth:
            value *= inside["high_z"]
        if y < 3:
            value *= inside["low_y"]
        if y >= 3 + rows:
            value *= inside["high_y"]
        return value

    return relax


def inner_kernel(u_ref, odd_ref, even_ref, start_ref, one_ref, two_ref, last_ref):
    depth, rows, width = u_ref.shape[:3]
    slab_odd = lax.rem(lax.axis_index("slab"), 2)
    inside = grid_ends()
    start_ref[3 : 3 + depth] = u_ref[...]
    for parity in range(2):

        @pl.when(slab_odd == parity)
        def _():
            low_ref, high_ref = (even_ref, odd_ref) if parity else (odd_ref, even_ref)
            start_ref[0:3] = low_ref[...] * inside["low_z"]
            start_ref[3 + depth :] = high_ref[...] * inside["high_z"]

    relax = line_sweep(width, depth, rows, inside)

    def reader(ref):
        return lambda z, y: ref[z, y - 3]

    start, one, two = reader(start_ref), reader(one_ref), reader(two_ref)
    for z in range(1, 5 + depth):
        for y in range(4, 2 + rows):
            one_ref[z, y - 3] = relax(start, start, z, y)
    for z in range(2, 4 + depth):
        for y in range(5, 1 + rows):
            two_ref[z, y - 3] = relax(start, one, z, y)
    for z in range(3, 3 + depth):
        for y in range(6, rows):
            place = ((z - 3) * rows + y - 3) * width
            last_ref[place : place + width, :] = relax(start, two, z, y)


def outer_kernel(
    row_odd_ref,
    row_even_ref,
    inner_start_ref,
    inner_one_ref,
    inner_two_ref,
    inner_last_ref,
    keep_ref,
    steps_ref,
    changes_ref,
    sums_ref,
    grad_ref,
    send_ref,
    start_ref,
    one_ref,
    two_ref,
    last_ref,
    total_ref,
):
    depth, rows = grad_ref.shape[:2]
    width = start_ref.shape[2]
    tile_odd = lax.rem(lax.axis_index("tile"), 2)
    inside = grid_ends()

    def edge(from_ref, first, count, z, factor, high):
        to = 3 + rows if high else 3 - count
        start_ref[z, to : to + count] = from_ref[first : first + count] * factor

    def beside(from_ref, high):
        factor = inside["high_y" if high else "low_y"]
        for z in range(depth):
            edge(from_ref, 3 * z, 3, 3 + z, factor, high)
        low_factor, high_factor = factor * inside["low_z"], factor * inside["high_z"]
        edge(from_ref, 12, 2, 2, low_factor, high)
        edge(from_ref, 14, 2, 3 + depth, high_factor, high)
        edge(from_ref, 16, 1, 1, low_factor, high)
        edge(from_ref, 17, 1, 4 + depth, high_factor, high)

    for parity in range(2):

        @pl.when(tile_odd == parity)
        def _():
            beside(row_odd_ref, parity == 1)
            beside(row_even_ref, parity == 0)

    relax = line_sweep(width, depth, rows, inside)

    def reader(inner_ref, outer_ref, level):
        def read(z, y):
            inner = 3 + level <= y < 3 + rows - level
            return inner_ref[z, y - 3] if inner else outer_ref[z, y]

        return read

    start = reader(inner_start_ref, start_ref, 0)
    one = reader(inner_one_ref, one_ref, 1)
    two = reader(inner_two_ref, two_ref, 2)

    def edge_lines(level):
        reach = SWEEPS - level
        for z in range(3 - reach, 3 + depth + reach):
            wide = reach - max(3 - z, z - 2 - depth, 0)
            for y in range(3 - wide, 3 + rows + wide):
                if not 3 + level <= y < 3 + rows - level:
                    yield z, y

    for z, y in edge_lines(1):
        one_ref[z, y] = relax(start, start, z, y)
    for z, y in edge_lines(2):
        two_ref[z, y] = relax(start, one, z, y)
    for z in range(depth):
        place = slice((z * rows + 3) * width, (z * rows + rows - 3) * width)
        last_ref[place, :] = inner_last_ref[place, :]
    for z, y in edge_lines(3):
        place = ((z - 3) * rows + y - 3) * width
        last_ref[place : place + width, :] = relax(start, two, z, y)

    sums = [jnp.zeros((8, LANES), F32) for _ in range(2 * MEM)]
    for z in range(depth):
        for row in range(0, rows, 8):
            for part in range(width):
                block = slice(row, row + 8), slice(part * LANES, (part + 1) * LANES)
                value = last_ref[pl.ds((z * rows + row) * width + part, 8, width), :]
                value *= keep_ref[z // 2, *block]
                grad_ref[z, *block] = value
                for i in range(MEM):
                    sums[i] += steps_ref[i, z, *block] * value
                    sums[MEM + i] += changes_ref[i, z, *block] * value
    done = 2 * len(PAIRS)
    total_ref[0:done, :] = sums_ref[0:done, :]
    for n, value in enumerate(sums):
        total_ref[done + n : done + n + 1, :] = jnp.sum(value, axis=0, keepdims=True)
    total_ref[done + 2 * MEM :, :] = jnp.zeros((SUMS - done - 2 * MEM, LANES), F32)
    totals = jnp.sum(total_ref[...], axis=1, keepdims=True)
    diagonal = lax.broadcasted_iota(jnp.int32, (SUMS, LANES), 0) == lax.broadcasted_iota(
        jnp.int32, (SUMS, LANES), 1
    )
    line = jnp.sum(jnp.where(diagonal, totals, 0.0), axis=0, keepdims=True)
    send_ref[...] = jnp.broadcast_to(line, send_ref.shape)


def combine_kernel(all_ref, grad_ref, steps_ref, changes_ref, out_hbm, out_ref, left):
    depth, rows, cols = grad_ref.shape
    line = jnp.sum(all_ref[...], axis=0, keepdims=True)

    def entry(n):
        return jnp.broadcast_to(line[:, n : n + 1], (8, LANES))

    sy = {pair: entry(n) for pair, n in SY.items()}
    yy = {pair: entry(n) for pair, n in YY.items()}
    inverse = [1.0 / sy[i, i] for i in range(MEM)]
    alphas = [None] * MEM
    for i in reversed(range(MEM)):
        product = entry(SG[i])
        for j in range(i + 1, MEM):
            product -= alphas[j] * sy[i, j]
        alphas[i] = product * inverse[i]
    scale = sy[MEM - 1, MEM - 1] / yy[MEM - 1, MEM - 1]
    weights = [None] * MEM
    for i in range(MEM):
        product = entry(YG[i])
        for j in range(MEM):
            product -= alphas[j] * yy[min(i, j), max(i, j)]
        product *= scale
        for j in range(i):
            product += weights[j] * sy[j, i]
        weights[i] = alphas[i] - product * inverse[i]
    on_changes = [scale * alphas[i] for i in range(MEM)]
    copies = [
        pltpu.make_async_copy(out_ref.at[z], out_hbm.at[z], left.at[z]) for z in range(depth)
    ]
    for z in range(depth):
        for row in range(0, rows, 8):
            for col in range(0, cols, LANES):
                lane = slice(col, col + LANES)
                value = -scale * grad_ref[z, row : row + 8, lane]
                for i in range(MEM):
                    value += on_changes[i] * changes_ref[i, z, row : row + 8, lane]
                    value -= weights[i] * steps_ref[i, z, row : row + 8, lane]
                out_ref[z, row : row + 8, lane] = value
        copies[z].start()
    for copy in copies:
        copy.wait()


def in_hbm(array):
    return pltpu.with_memory_space_constraint(array, pltpu.HBM)


def swaps():
    slabs, tiles = lax.axis_size("slab"), lax.axis_size("tile")
    places = [(slab, tile) for slab in range(slabs) for tile in range(tiles)]
    spare = max(slabs // 4, 1)

    def pairs(partner):
        targets = [partner(*place) for place in places]
        return [(i, slab * tiles + tile) for i, (slab, tile) in enumerate(targets)]

    def slab_odd(slab, tile):
        beside = slab + 1 if slab % 2 else slab - 1
        return (beside, tile) if 0 <= beside < slabs else (slab, tile ^ 1)

    def tile_odd(slab, tile):
        beside = tile + 1 if tile % 2 else tile - 1
        return (slab, beside) if 0 <= beside < tiles else (slab ^ spare, tile)

    return (
        pairs(slab_odd),
        pairs(lambda slab, tile: (slab ^ 1, tile)),
        pairs(tile_odd),
        pairs(lambda slab, tile: (slab, tile ^ 1)),
    )


def per_device(sensitivity, filtered_density, passive_blocks, history_steps, history_changes):
    shape = sensitivity.shape
    depth, rows, cols = shape
    like = jax.ShapeDtypeStruct
    width = cols // LANES
    field_lines, layers, rim = (
        like((count * width, LANES), F32) for count in (depth * rows, SWEEPS * rows, 6)
    )
    edges = like((3 * depth + 6, width, LANES), F32)

    u, rim_odd, rim_even, odd, even = pl.pallas_call(
        weight_kernel,
        out_shape=(field_lines, rim, rim, layers, layers),
        in_specs=[HBM] * 2,
        out_specs=[VMEM] * 5,
        scratch_shapes=[
            pltpu.VMEM(shape, F32),
            pltpu.VMEM(shape, F32),
            pltpu.SemaphoreType.DMA((2, depth)),
        ],
        compiler_params=kernel_params(8),
        name="weights",
    )(in_hbm(sensitivity), in_hbm(filtered_density))

    u = u.reshape(depth, rows, width, LANES)
    rim_odd, rim_even = (array.reshape(6, width, LANES) for array in (rim_odd, rim_even))
    odd, even = (array.reshape(SWEEPS, rows, width, LANES) for array in (odd, even))

    slab_odd, slab_even, tile_odd, tile_even = swaps()
    rim_odd = lax.ppermute(rim_odd, MESH_AXES, slab_odd)
    rim_even = lax.ppermute(rim_even, MESH_AXES, slab_even)
    odd = lax.ppermute(odd, MESH_AXES, slab_odd)
    even = lax.ppermute(even, MESH_AXES, slab_even)

    row_odd, row_even = pl.pallas_call(
        pack_kernel,
        out_shape=(edges, edges),
        in_specs=[VMEM] * 3,
        out_specs=[VMEM] * 2,
        compiler_params=kernel_params(8),
        name="edges",
    )(u, rim_odd, rim_even)
    row_odd = lax.ppermute(row_odd, MESH_AXES, tile_odd)
    row_even = lax.ppermute(row_even, MESH_AXES, tile_even)

    history = like(history_steps.shape, F32)
    sums, keep, steps, changes = pl.pallas_call(
        gram_kernel,
        out_shape=(
            like((SUMS, LANES), F32),
            like((depth // 2, rows, cols), F32),
            history,
            history,
        ),
        in_specs=[HBM] * 3,
        out_specs=[VMEM] * 4,
        scratch_shapes=[
            pltpu.VMEM(passive_blocks.shape, jnp.int32),
            pltpu.SemaphoreType.DMA((2, depth)),
            pltpu.SemaphoreType.DMA,
        ],
        compiler_params=kernel_params(8),
        cost_estimate=pl.CostEstimate(flops=8_000_000_000, bytes_accessed=43_000_000, transcendentals=0),
        name="gram",
    )(in_hbm(history_steps), in_hbm(history_changes), in_hbm(passive_blocks))

    field = like((depth + 6, rows, width, LANES), F32)
    inner = pl.pallas_call(
        inner_kernel,
        out_shape=(field, field, field, field_lines),
        in_specs=[VMEM] * 3,
        out_specs=[VMEM] * 4,
        compiler_params=kernel_params(8),
        name="inner",
    )(u, odd, even)

    padded = pltpu.VMEM((depth + 6, rows + 6, width, LANES), F32)
    gradient, line = pl.pallas_call(
        outer_kernel,
        out_shape=(like(shape, F32), like((8, LANES), F32)),
        in_specs=[VMEM] * 10,
        out_specs=[VMEM] * 2,
        scratch_shapes=[
            padded,
            padded,
            padded,
            pltpu.VMEM((depth * rows * width, LANES), F32),
            pltpu.VMEM((SUMS, LANES), F32),
        ],
        compiler_params=kernel_params(16),
        name="outer",
    )(row_odd, row_even, *inner, keep, steps, changes, sums)

    slabs, tiles = lax.axis_size("slab"), lax.axis_size("tile")
    groups = [
        [slab * tiles + tile for tile in range(core, tiles, 2) for slab in range(slabs)]
        for core in range(2)
    ]
    line = line + lax.ppermute(line, MESH_AXES, tile_even)
    lines = jnp.broadcast_to(line[:1], (len(groups[0]), LANES))
    received = lax.all_to_all(lines, MESH_AXES, 0, 0, axis_index_groups=groups, tiled=True)

    return pl.pallas_call(
        combine_kernel,
        out_shape=like(shape, F32),
        in_specs=[VMEM] * 4,
        out_specs=HBM,
        scratch_shapes=[pltpu.VMEM(shape, F32), pltpu.SemaphoreType.DMA((depth,))],
        compiler_params=kernel_params(8),
        name="combine",
    )(received, gradient, steps, changes)


def solution(mesh):
    in_specs = (
        P("slab", "tile", None),
        P("slab", "tile", None),
        P("slab", "tile", None),
        P(None, "slab", "tile", None),
        P(None, "slab", "tile", None),
    )
    out_specs = P("slab", "tile", None)
    return jax.shard_map(
        per_device, mesh=mesh, in_specs=in_specs, out_specs=out_specs, check_vma=False
    )
```

```python
import jax
import jax.numpy as jnp
from jax import lax
from jax.experimental import pallas as pl
from jax.experimental.pallas import tpu as pltpu
from jax.sharding import PartitionSpec as P

SWEEPS = 3
MEM = 4

radius_square = 4.0
sharpness = 8.0
threshold = 0.5
diagonal_value = 1.0 + 6.0 * radius_square
coupling = radius_square / diagonal_value

F32 = jnp.float32
MESH_AXES = ("slab", "tile")
LANES = 128
PAIRS = [(i, j) for i in range(MEM) for j in range(i, MEM)]
SY = {pair: n for n, pair in enumerate(PAIRS)}
YY = {pair: len(PAIRS) + n for n, pair in enumerate(PAIRS)}
SG = [2 * len(PAIRS) + n for n in range(MEM)]
YG = [2 * len(PAIRS) + MEM + n for n in range(MEM)]
SUMS = 32

VMEM = pl.BlockSpec(memory_space=pltpu.VMEM)
HBM = pl.BlockSpec(memory_space=pltpu.HBM)


def kernel_params(mib):
    return pltpu.CompilerParams(vmem_limit_bytes=mib * 1024 * 1024)


def weight_kernel(
    sens_hbm,
    dens_hbm,
    u_ref,
    rim_odd_ref,
    rim_even_ref,
    far_ref,
    sens_ref,
    dens_ref,
    arrived,
):
    depth, rows, cols = sens_ref.shape
    width = cols // LANES
    layer = rows * width
    slab_odd = lax.rem(lax.axis_index("slab"), 2)
    copies = [
        [
            pltpu.make_async_copy(from_ref.at[z], to_ref.at[z], arrived.at[n, z])
            for n, (from_ref, to_ref) in enumerate(((sens_hbm, sens_ref), (dens_hbm, dens_ref)))
        ]
        for z in range(depth)
    ]
    for pair in copies:
        for copy in pair:
            copy.start()
    denominator = jnp.tanh(F32(sharpness * threshold)) + jnp.tanh(
        F32(sharpness * (1.0 - threshold))
    )
    for z in range(depth):
        for copy in copies[z]:
            copy.wait()
        bend = jnp.tanh(sharpness * (dens_ref[z] - threshold))
        slope = sharpness * (1.0 - bend * bend) / denominator
        value = sens_ref[z] * slope / diagonal_value
        for row in range(0, rows, 8):
            for part in range(width):
                place = pl.ds(z * layer + row * width + part, 8, width)
                u_ref[place, :] = value[row : row + 8, part * LANES : (part + 1) * LANES]

    for rim_ref, top in ((rim_odd_ref, slab_odd), (rim_even_ref, 1 - slab_odd)):

        def put(first, count, z, row):
            place = pl.ds(pl.multiple_of(z * layer + row * width, 8), count * width)
            rim_ref[first * width : (first + count) * width, :] = u_ref[place, :]

        near, second = (depth - 1) * top, 1 + (depth - 3) * top
        put(0, rows, near, 0)
        put(rows, 1, second, 0)
        put(rows + 1, 1, second, rows - 1)
    far_ref[...] = u_ref[layer : (depth - 1) * layer, :]


def gram_kernel(
    steps_hbm,
    changes_hbm,
    passive_hbm,
    sums_ref,
    keep_ref,
    steps_ref,
    changes_ref,
    passive_ref,
    arrived,
    passive_arrived,
):
    depth, rows, cols = steps_ref.shape[1:]
    passive_copy = pltpu.make_async_copy(passive_hbm, passive_ref, passive_arrived)
    copies = [
        [
            pltpu.make_async_copy(from_ref.at[:, z], to_ref.at[:, z], arrived.at[n, z])
            for n, (from_ref, to_ref) in enumerate(
                ((steps_hbm, steps_ref), (changes_hbm, changes_ref))
            )
        ]
        for z in range(depth)
    ]
    passive_copy.start()
    for pair in copies:
        for copy in pair:
            copy.start()

    def doubling(shape, dim):
        place = lax.broadcasted_iota(jnp.int32, shape, dim) // 2
        matches = place == lax.broadcasted_iota(jnp.int32, shape, 1 - dim)
        return matches.astype(F32).astype(jnp.bfloat16)

    passive_copy.wait()
    half_rows = passive_ref.shape[1]
    twice_rows = doubling((2 * half_rows, half_rows), 0)
    twice_cols = doubling((LANES, 2 * LANES), 1)
    for z in range(passive_ref.shape[0]):
        blocks = passive_ref[z].astype(F32).astype(jnp.bfloat16)
        blocks = jnp.dot(twice_rows, blocks, preferred_element_type=F32).astype(jnp.bfloat16)
        for col in range(0, passive_ref.shape[2], LANES):
            wide = jnp.dot(
                blocks[:, col : col + LANES], twice_cols, preferred_element_type=F32
            )
            keep_ref[z, :, 2 * col : 2 * col + 2 * LANES] = 1.0 - wide

    sums = (jnp.zeros((8, LANES), F32),) * (2 * len(PAIRS))
    for z in range(depth):
        for copy in copies[z]:
            copy.wait()

        def step(block, sums):
            row = pl.ds(pl.multiple_of(block * 8, 8), 8)
            sums = list(sums)
            for col in range(0, cols, LANES):
                lane = pl.ds(col, LANES)
                s = [steps_ref[i, z, row, lane] for i in range(MEM)]
                y = [changes_ref[i, z, row, lane] for i in range(MEM)]
                for i, j in PAIRS:
                    sums[SY[i, j]] += s[i] * y[j]
                    sums[YY[i, j]] += y[i] * y[j]
            return tuple(sums)

        sums = lax.fori_loop(0, rows // 8, step, sums)
    for n, value in enumerate(sums):
        sums_ref[n : n + 1, :] = jnp.sum(value, axis=0, keepdims=True)


def pack_kernel(u_ref, odd_ref, even_ref, row_odd_ref, row_even_ref):
    depth, rows = u_ref.shape[:2]
    slab_odd = lax.rem(lax.axis_index("slab"), 2)
    tile_odd = lax.rem(lax.axis_index("tile"), 2)

    def pack(low_ref, high_ref, out_ref, top):
        start = rows - 3 if top else 0
        for z in range(depth):
            out_ref[3 * z : 3 * z + 3] = u_ref[z, start : start + 3]
        near, second = (rows - 2, rows + 1) if top else (0, rows)
        out_ref[12:14] = low_ref[near : near + 2]
        out_ref[14:16] = high_ref[near : near + 2]
        out_ref[16] = low_ref[second]
        out_ref[17] = high_ref[second]

    for parity in range(2):
        for top in range(2):

            @pl.when((slab_odd == parity) & (tile_odd == top))
            def _():
                low_ref, high_ref = (even_ref, odd_ref) if parity else (odd_ref, even_ref)
                pack(low_ref, high_ref, row_odd_ref, top == 1)
                pack(low_ref, high_ref, row_even_ref, top == 0)


def grid_ends():
    slab, tile = lax.axis_index("slab"), lax.axis_index("tile")
    return {
        "low_z": (slab > 0).astype(F32),
        "high_z": (slab < lax.axis_size("slab") - 1).astype(F32),
        "low_y": (tile > 0).astype(F32),
        "high_y": (tile < lax.axis_size("tile") - 1).astype(F32),
    }


def line_sweep(width, depth, rows, inside):
    lane = lax.broadcasted_iota(jnp.int32, (width, LANES), 1)
    group = lax.broadcasted_iota(jnp.int32, (width, LANES), 0)
    lane_first, lane_last = lane == 0, lane == LANES - 1
    first, last = lane_first & (group == 0), lane_last & (group == width - 1)

    def relax(start, field, z, y):
        here = field(z, y)
        around = field(z - 1, y) + field(z + 1, y)
        around += field(z, y - 1) + field(z, y + 1)
        before, after = pltpu.roll(here, 1, 1), pltpu.roll(here, LANES - 1, 1)
        before = jnp.where(lane_first, pltpu.roll(before, 1, 0), before)
        after = jnp.where(lane_last, pltpu.roll(after, width - 1, 0), after)
        around += jnp.where(first, 0.0, before) + jnp.where(last, 0.0, after)
        value = start(z, y) + coupling * around
        if z < 3:
            value *= inside["low_z"]
        if z >= 3 + depth:
            value *= inside["high_z"]
        if y < 3:
            value *= inside["low_y"]
        if y >= 3 + rows:
            value *= inside["high_y"]
        return value

    return relax


def inner_kernel(
    u_ref, rim_odd_ref, rim_even_ref, even_ref, odd_ref, start_ref, one_ref, two_ref, last_ref
):
    depth, rows, width = u_ref.shape[:3]
    slab_odd = lax.rem(lax.axis_index("slab"), 2)
    inside = grid_ends()
    start_ref[3 : 3 + depth] = u_ref[...]
    for parity in range(2):

        @pl.when(slab_odd == parity)
        def _():
            pairs = (rim_odd_ref, odd_ref), (rim_even_ref, even_ref)
            (low_rim, low_far), (high_rim, high_far) = pairs[::-1] if parity else pairs
            start_ref[0:2] = low_far[...] * inside["low_z"]
            start_ref[2] = low_rim[0:rows] * inside["low_z"]
            start_ref[3 + depth] = high_rim[0:rows] * inside["high_z"]
            start_ref[4 + depth :] = high_far[...] * inside["high_z"]

    relax = line_sweep(width, depth, rows, inside)

    def reader(ref):
        return lambda z, y: ref[z, y - 3]

    start, one, two = reader(start_ref), reader(one_ref), reader(two_ref)
    for z in range(1, 5 + depth):
        for y in range(4, 2 + rows):
            one_ref[z, y - 3] = relax(start, start, z, y)
    for z in range(2, 4 + depth):
        for y in range(5, 1 + rows):
            two_ref[z, y - 3] = relax(start, one, z, y)
    for z in range(3, 3 + depth):
        for y in range(6, rows):
            place = ((z - 3) * rows + y - 3) * width
            last_ref[place : place + width, :] = relax(start, two, z, y)


def outer_kernel(
    row_odd_ref,
    row_even_ref,
    inner_start_ref,
    inner_one_ref,
    inner_two_ref,
    inner_last_ref,
    keep_ref,
    steps_ref,
    changes_ref,
    sums_ref,
    grad_ref,
    send_ref,
    start_ref,
    one_ref,
    two_ref,
    last_ref,
    total_ref,
):
    depth, rows = grad_ref.shape[:2]
    width = start_ref.shape[2]
    tile_odd = lax.rem(lax.axis_index("tile"), 2)
    inside = grid_ends()

    def edge(from_ref, first, count, z, factor, high):
        to = 3 + rows if high else 3 - count
        start_ref[z, to : to + count] = from_ref[first : first + count] * factor

    def beside(from_ref, high):
        factor = inside["high_y" if high else "low_y"]
        for z in range(depth):
            edge(from_ref, 3 * z, 3, 3 + z, factor, high)
        low_factor, high_factor = factor * inside["low_z"], factor * inside["high_z"]
        edge(from_ref, 12, 2, 2, low_factor, high)
        edge(from_ref, 14, 2, 3 + depth, high_factor, high)
        edge(from_ref, 16, 1, 1, low_factor, high)
        edge(from_ref, 17, 1, 4 + depth, high_factor, high)

    for parity in range(2):

        @pl.when(tile_odd == parity)
        def _():
            beside(row_odd_ref, parity == 1)
            beside(row_even_ref, parity == 0)

    relax = line_sweep(width, depth, rows, inside)

    def reader(inner_ref, outer_ref, level):
        def read(z, y):
            inner = 3 + level <= y < 3 + rows - level
            return inner_ref[z, y - 3] if inner else outer_ref[z, y]

        return read

    start = reader(inner_start_ref, start_ref, 0)
    one = reader(inner_one_ref, one_ref, 1)
    two = reader(inner_two_ref, two_ref, 2)

    def edge_lines(level):
        reach = SWEEPS - level
        for z in range(3 - reach, 3 + depth + reach):
            wide = reach - max(3 - z, z - 2 - depth, 0)
            for y in range(3 - wide, 3 + rows + wide):
                if not 3 + level <= y < 3 + rows - level:
                    yield z, y

    for z, y in edge_lines(1):
        one_ref[z, y] = relax(start, start, z, y)
    for z, y in edge_lines(2):
        two_ref[z, y] = relax(start, one, z, y)
    for z in range(depth):
        place = slice((z * rows + 3) * width, (z * rows + rows - 3) * width)
        last_ref[place, :] = inner_last_ref[place, :]
    for z, y in edge_lines(3):
        place = ((z - 3) * rows + y - 3) * width
        last_ref[place : place + width, :] = relax(start, two, z, y)

    sums = [jnp.zeros((8, LANES), F32) for _ in range(2 * MEM)]
    for z in range(depth):
        for row in range(0, rows, 8):
            for part in range(width):
                block = slice(row, row + 8), slice(part * LANES, (part + 1) * LANES)
                value = last_ref[pl.ds((z * rows + row) * width + part, 8, width), :]
                value *= keep_ref[z // 2, *block]
                grad_ref[z, *block] = value
                for i in range(MEM):
                    sums[i] += steps_ref[i, z, *block] * value
                    sums[MEM + i] += changes_ref[i, z, *block] * value
    done = 2 * len(PAIRS)
    total_ref[0:done, :] = sums_ref[0:done, :]
    for n, value in enumerate(sums):
        total_ref[done + n : done + n + 1, :] = jnp.sum(value, axis=0, keepdims=True)
    total_ref[done + 2 * MEM :, :] = jnp.zeros((SUMS - done - 2 * MEM, LANES), F32)
    totals = jnp.sum(total_ref[...], axis=1, keepdims=True)
    diagonal = lax.broadcasted_iota(jnp.int32, (SUMS, LANES), 0) == lax.broadcasted_iota(
        jnp.int32, (SUMS, LANES), 1
    )
    line = jnp.sum(jnp.where(diagonal, totals, 0.0), axis=0, keepdims=True)
    send_ref[...] = jnp.broadcast_to(line, send_ref.shape)


def combine_kernel(all_ref, grad_ref, steps_ref, changes_ref, out_hbm, out_ref, left):
    depth, rows, cols = grad_ref.shape
    line = jnp.sum(all_ref[...], axis=0, keepdims=True)

    def entry(n):
        return jnp.broadcast_to(line[:, n : n + 1], (8, LANES))

    sy = {pair: entry(n) for pair, n in SY.items()}
    yy = {pair: entry(n) for pair, n in YY.items()}
    inverse = [1.0 / sy[i, i] for i in range(MEM)]
    alphas = [None] * MEM
    for i in reversed(range(MEM)):
        product = entry(SG[i])
        for j in range(i + 1, MEM):
            product -= alphas[j] * sy[i, j]
        alphas[i] = product * inverse[i]
    scale = sy[MEM - 1, MEM - 1] / yy[MEM - 1, MEM - 1]
    weights = [None] * MEM
    for i in range(MEM):
        product = entry(YG[i])
        for j in range(MEM):
            product -= alphas[j] * yy[min(i, j), max(i, j)]
        product *= scale
        for j in range(i):
            product += weights[j] * sy[j, i]
        weights[i] = alphas[i] - product * inverse[i]
    on_changes = [scale * alphas[i] for i in range(MEM)]
    copies = [
        pltpu.make_async_copy(out_ref.at[z], out_hbm.at[z], left.at[z]) for z in range(depth)
    ]
    for z in range(depth):
        for row in range(0, rows, 8):
            for col in range(0, cols, LANES):
                lane = slice(col, col + LANES)
                value = -scale * grad_ref[z, row : row + 8, lane]
                for i in range(MEM):
                    value += on_changes[i] * changes_ref[i, z, row : row + 8, lane]
                    value -= weights[i] * steps_ref[i, z, row : row + 8, lane]
                out_ref[z, row : row + 8, lane] = value
        copies[z].start()
    for copy in copies:
        copy.wait()


def in_hbm(array):
    return pltpu.with_memory_space_constraint(array, pltpu.HBM)


def swaps():
    slabs, tiles = lax.axis_size("slab"), lax.axis_size("tile")
    places = [(slab, tile) for slab in range(slabs) for tile in range(tiles)]
    spare = max(slabs // 4, 1)

    def pairs(partner):
        targets = [partner(*place) for place in places]
        return [(i, slab * tiles + tile) for i, (slab, tile) in enumerate(targets)]

    def slab_odd(slab, tile):
        beside = slab + 1 if slab % 2 else slab - 1
        return (beside, tile) if 0 <= beside < slabs else (slab, tile ^ 1)

    def tile_odd(slab, tile):
        beside = tile + 1 if tile % 2 else tile - 1
        return (slab, beside) if 0 <= beside < tiles else (slab ^ spare, tile)

    return (
        pairs(slab_odd),
        pairs(lambda slab, tile: (slab ^ 1, tile)),
        pairs(tile_odd),
        pairs(lambda slab, tile: (slab, tile ^ 1)),
    )


def per_device(sensitivity, filtered_density, passive_blocks, history_steps, history_changes):
    shape = sensitivity.shape
    depth, rows, cols = shape
    like = jax.ShapeDtypeStruct
    width = cols // LANES
    lines, far, rim = (
        like((count * width, LANES), F32) for count in (depth * rows, 2 * rows, rows + 2)
    )
    edges = like((3 * depth + 6, width, LANES), F32)
    devices = lax.axis_size("slab") * lax.axis_size("tile")

    u, rim_odd, rim_even, far = pl.pallas_call(
        weight_kernel,
        out_shape=(lines, rim, rim, far),
        in_specs=[HBM] * 2,
        out_specs=[VMEM] * 4,
        scratch_shapes=[
            pltpu.VMEM(shape, F32),
            pltpu.VMEM(shape, F32),
            pltpu.SemaphoreType.DMA((2, depth)),
        ],
        compiler_params=kernel_params(8),
        name="weights",
    )(in_hbm(sensitivity), in_hbm(filtered_density))

    u = u.reshape(depth, rows, width, LANES)
    rim_odd, rim_even = (
        array.reshape(rows + 2, width, LANES) for array in (rim_odd, rim_even)
    )
    far = far.reshape(2, rows, width, LANES)

    slab_odd, slab_even, tile_odd, tile_even = swaps()
    rim_odd = lax.ppermute(rim_odd, MESH_AXES, slab_odd)
    rim_even = lax.ppermute(rim_even, MESH_AXES, slab_even)
    odd = lax.ppermute(far, MESH_AXES, slab_odd)
    even = lax.ppermute(far, MESH_AXES, slab_even)

    row_odd, row_even = pl.pallas_call(
        pack_kernel,
        out_shape=(edges, edges),
        in_specs=[VMEM] * 3,
        out_specs=[VMEM] * 2,
        compiler_params=kernel_params(8),
        name="edges",
    )(u, rim_odd, rim_even)
    row_odd = lax.ppermute(row_odd, MESH_AXES, tile_odd)
    row_even = lax.ppermute(row_even, MESH_AXES, tile_even)

    history = like(history_steps.shape, F32)
    sums, keep, steps, changes = pl.pallas_call(
        gram_kernel,
        out_shape=(
            like((SUMS, LANES), F32),
            like((depth // 2, rows, cols), F32),
            history,
            history,
        ),
        in_specs=[HBM] * 3,
        out_specs=[VMEM] * 4,
        scratch_shapes=[
            pltpu.VMEM(passive_blocks.shape, jnp.int32),
            pltpu.SemaphoreType.DMA((2, depth)),
            pltpu.SemaphoreType.DMA,
        ],
        compiler_params=kernel_params(8),
        cost_estimate=pl.CostEstimate(flops=8_000_000_000, bytes_accessed=43_000_000, transcendentals=0),
        name="gram",
    )(in_hbm(history_steps), in_hbm(history_changes), in_hbm(passive_blocks))

    field = like((depth + 6, rows, width, LANES), F32)
    inner = pl.pallas_call(
        inner_kernel,
        out_shape=(field, field, field, lines),
        in_specs=[VMEM] * 5,
        out_specs=[VMEM] * 4,
        compiler_params=kernel_params(8),
        name="inner",
    )(u, rim_odd, rim_even, even, odd)

    padded = pltpu.VMEM((depth + 6, rows + 6, width, LANES), F32)
    gradient, line = pl.pallas_call(
        outer_kernel,
        out_shape=(like(shape, F32), like((devices, LANES), F32)),
        in_specs=[VMEM] * 10,
        out_specs=[VMEM] * 2,
        scratch_shapes=[
            padded,
            padded,
            padded,
            pltpu.VMEM((depth * rows * width, LANES), F32),
            pltpu.VMEM((SUMS, LANES), F32),
        ],
        compiler_params=kernel_params(16),
        name="outer",
    )(row_odd, row_even, *inner, keep, steps, changes, sums)

    received = lax.all_to_all(line, MESH_AXES, 0, 0, tiled=True)

    return pl.pallas_call(
        combine_kernel,
        out_shape=like(shape, F32),
        in_specs=[VMEM] * 4,
        out_specs=HBM,
        scratch_shapes=[pltpu.VMEM(shape, F32), pltpu.SemaphoreType.DMA((depth,))],
        compiler_params=kernel_params(8),
        name="combine",
    )(received, gradient, steps, changes)


def solution(mesh):
    in_specs = (
        P("slab", "tile", None),
        P("slab", "tile", None),
        P("slab", "tile", None),
        P(None, "slab", "tile", None),
        P(None, "slab", "tile", None),
    )
    out_specs = P("slab", "tile", None)
    return jax.shard_map(
        per_device, mesh=mesh, in_specs=in_specs, out_specs=out_specs, check_vma=False
    )
```

```python
import jax
import jax.numpy as jnp
from jax import lax
from jax.experimental import pallas as pl
from jax.experimental.pallas import tpu as pltpu
from jax.sharding import PartitionSpec as P

SWEEPS = 3
MEM = 4

radius_square = 4.0
sharpness = 8.0
threshold = 0.5
diagonal_value = 1.0 + 6.0 * radius_square
coupling = radius_square / diagonal_value

F32 = jnp.float32
MESH_AXES = ("slab", "tile")
LANES = 128
PAIRS = [(i, j) for i in range(MEM) for j in range(i, MEM)]
SY = {pair: n for n, pair in enumerate(PAIRS)}
YY = {pair: len(PAIRS) + n for n, pair in enumerate(PAIRS)}
SG = [2 * len(PAIRS) + n for n in range(MEM)]
YG = [2 * len(PAIRS) + MEM + n for n in range(MEM)]
SUMS = 32

VMEM = pl.BlockSpec(memory_space=pltpu.VMEM)
HBM = pl.BlockSpec(memory_space=pltpu.HBM)


def kernel_params(mib):
    return pltpu.CompilerParams(vmem_limit_bytes=mib * 1024 * 1024)


def weight_kernel(
    sens_hbm,
    dens_hbm,
    u_ref,
    rim_odd_ref,
    rim_even_ref,
    far_ref,
    sens_ref,
    dens_ref,
    arrived,
):
    depth, rows, cols = sens_ref.shape
    width = cols // LANES
    layer = rows * width
    slab_odd = lax.rem(lax.axis_index("slab"), 2)
    copies = [
        [
            pltpu.make_async_copy(from_ref.at[z], to_ref.at[z], arrived.at[n, z])
            for n, (from_ref, to_ref) in enumerate(((sens_hbm, sens_ref), (dens_hbm, dens_ref)))
        ]
        for z in range(depth)
    ]
    for pair in copies:
        for copy in pair:
            copy.start()
    denominator = jnp.tanh(F32(sharpness * threshold)) + jnp.tanh(
        F32(sharpness * (1.0 - threshold))
    )
    for z in range(depth):
        for copy in copies[z]:
            copy.wait()
        bend = jnp.tanh(sharpness * (dens_ref[z] - threshold))
        slope = sharpness * (1.0 - bend * bend) / denominator
        value = sens_ref[z] * slope / diagonal_value
        for row in range(0, rows, 8):
            for part in range(width):
                place = pl.ds(z * layer + row * width + part, 8, width)
                u_ref[place, :] = value[row : row + 8, part * LANES : (part + 1) * LANES]

    for rim_ref, top in ((rim_odd_ref, slab_odd), (rim_even_ref, 1 - slab_odd)):

        def put(first, count, z, row):
            place = pl.ds(pl.multiple_of(z * layer + row * width, 8), count * width)
            rim_ref[first * width : (first + count) * width, :] = u_ref[place, :]

        near, second = (depth - 1) * top, 1 + (depth - 3) * top
        put(0, rows, near, 0)
        put(rows, 1, second, 0)
        put(rows + 1, 1, second, rows - 1)
    far_ref[...] = u_ref[layer : (depth - 1) * layer, :]


def gram_kernel(
    steps_hbm,
    changes_hbm,
    passive_hbm,
    sums_ref,
    keep_ref,
    steps_ref,
    changes_ref,
    passive_ref,
    arrived,
    passive_arrived,
):
    depth, rows, cols = steps_ref.shape[1:]
    passive_copy = pltpu.make_async_copy(passive_hbm, passive_ref, passive_arrived)
    copies = [
        [
            pltpu.make_async_copy(from_ref.at[:, z], to_ref.at[:, z], arrived.at[n, z])
            for n, (from_ref, to_ref) in enumerate(
                ((steps_hbm, steps_ref), (changes_hbm, changes_ref))
            )
        ]
        for z in range(depth)
    ]
    passive_copy.start()
    for pair in copies:
        for copy in pair:
            copy.start()

    def doubling(shape, dim):
        place = lax.broadcasted_iota(jnp.int32, shape, dim) // 2
        matches = place == lax.broadcasted_iota(jnp.int32, shape, 1 - dim)
        return matches.astype(F32).astype(jnp.bfloat16)

    passive_copy.wait()
    half_rows = passive_ref.shape[1]
    twice_rows = doubling((2 * half_rows, half_rows), 0)
    twice_cols = doubling((LANES, 2 * LANES), 1)
    for z in range(passive_ref.shape[0]):
        blocks = passive_ref[z].astype(F32).astype(jnp.bfloat16)
        blocks = jnp.dot(twice_rows, blocks, preferred_element_type=F32).astype(jnp.bfloat16)
        for col in range(0, passive_ref.shape[2], LANES):
            wide = jnp.dot(
                blocks[:, col : col + LANES], twice_cols, preferred_element_type=F32
            )
            keep_ref[z, :, 2 * col : 2 * col + 2 * LANES] = 1.0 - wide

    sums = (jnp.zeros((8, LANES), F32),) * (2 * len(PAIRS))
    for z in range(depth):
        for copy in copies[z]:
            copy.wait()

        def step(block, sums):
            row = pl.ds(pl.multiple_of(block * 8, 8), 8)
            sums = list(sums)
            for col in range(0, cols, LANES):
                lane = pl.ds(col, LANES)
                s = [steps_ref[i, z, row, lane] for i in range(MEM)]
                y = [changes_ref[i, z, row, lane] for i in range(MEM)]
                for i, j in PAIRS:
                    sums[SY[i, j]] += s[i] * y[j]
                    sums[YY[i, j]] += y[i] * y[j]
            return tuple(sums)

        sums = lax.fori_loop(0, rows // 8, step, sums)
    for n, value in enumerate(sums):
        sums_ref[n : n + 1, :] = jnp.sum(value, axis=0, keepdims=True)


def pack_kernel(u_ref, odd_ref, even_ref, row_odd_ref, row_even_ref):
    depth, rows = u_ref.shape[:2]
    slab_odd = lax.rem(lax.axis_index("slab"), 2)
    tile_odd = lax.rem(lax.axis_index("tile"), 2)

    def pack(low_ref, high_ref, out_ref, top):
        start = rows - 3 if top else 0
        for z in range(depth):
            out_ref[3 * z : 3 * z + 3] = u_ref[z, start : start + 3]
        near, second = (rows - 2, rows + 1) if top else (0, rows)
        out_ref[12:14] = low_ref[near : near + 2]
        out_ref[14:16] = high_ref[near : near + 2]
        out_ref[16] = low_ref[second]
        out_ref[17] = high_ref[second]

    for parity in range(2):
        for top in range(2):

            @pl.when((slab_odd == parity) & (tile_odd == top))
            def _():
                low_ref, high_ref = (even_ref, odd_ref) if parity else (odd_ref, even_ref)
                pack(low_ref, high_ref, row_odd_ref, top == 1)
                pack(low_ref, high_ref, row_even_ref, top == 0)


def grid_ends():
    slab, tile = lax.axis_index("slab"), lax.axis_index("tile")
    return {
        "low_z": (slab > 0).astype(F32),
        "high_z": (slab < lax.axis_size("slab") - 1).astype(F32),
        "low_y": (tile > 0).astype(F32),
        "high_y": (tile < lax.axis_size("tile") - 1).astype(F32),
    }


def line_sweep(width, depth, rows, inside):
    lane = lax.broadcasted_iota(jnp.int32, (width, LANES), 1)
    group = lax.broadcasted_iota(jnp.int32, (width, LANES), 0)
    lane_first, lane_last = lane == 0, lane == LANES - 1
    first, last = lane_first & (group == 0), lane_last & (group == width - 1)

    def relax(start, field, z, y):
        here = field(z, y)
        around = field(z - 1, y) + field(z + 1, y)
        around += field(z, y - 1) + field(z, y + 1)
        before, after = pltpu.roll(here, 1, 1), pltpu.roll(here, LANES - 1, 1)
        before = jnp.where(lane_first, pltpu.roll(before, 1, 0), before)
        after = jnp.where(lane_last, pltpu.roll(after, width - 1, 0), after)
        around += jnp.where(first, 0.0, before) + jnp.where(last, 0.0, after)
        value = start(z, y) + coupling * around
        if z < 3:
            value *= inside["low_z"]
        if z >= 3 + depth:
            value *= inside["high_z"]
        if y < 3:
            value *= inside["low_y"]
        if y >= 3 + rows:
            value *= inside["high_y"]
        return value

    return relax


def inner_kernel(
    u_ref, rim_odd_ref, rim_even_ref, odd_ref, even_ref, start_ref, one_ref, two_ref, last_ref
):
    depth, rows, width = u_ref.shape[:3]
    slab_odd = lax.rem(lax.axis_index("slab"), 2)
    inside = grid_ends()
    start_ref[3 : 3 + depth] = u_ref[...]
    for parity in range(2):

        @pl.when(slab_odd == parity)
        def _():
            pairs = (rim_odd_ref, odd_ref), (rim_even_ref, even_ref)
            (low_rim, low_far), (high_rim, high_far) = pairs[::-1] if parity else pairs
            start_ref[0:2] = low_far[...] * inside["low_z"]
            start_ref[2] = low_rim[0:rows] * inside["low_z"]
            start_ref[3 + depth] = high_rim[0:rows] * inside["high_z"]
            start_ref[4 + depth :] = high_far[...] * inside["high_z"]

    relax = line_sweep(width, depth, rows, inside)

    def reader(ref):
        return lambda z, y: ref[z, y - 3]

    start, one, two = reader(start_ref), reader(one_ref), reader(two_ref)
    for z in range(1, 5 + depth):
        for y in range(4, 2 + rows):
            one_ref[z, y - 3] = relax(start, start, z, y)
    for z in range(2, 4 + depth):
        for y in range(5, 1 + rows):
            two_ref[z, y - 3] = relax(start, one, z, y)
    for z in range(3, 3 + depth):
        for y in range(6, rows):
            place = ((z - 3) * rows + y - 3) * width
            last_ref[place : place + width, :] = relax(start, two, z, y)


def outer_kernel(
    row_odd_ref,
    row_even_ref,
    inner_start_ref,
    inner_one_ref,
    inner_two_ref,
    inner_last_ref,
    keep_ref,
    steps_ref,
    changes_ref,
    sums_ref,
    grad_ref,
    send_ref,
    start_ref,
    one_ref,
    two_ref,
    last_ref,
    total_ref,
):
    depth, rows = grad_ref.shape[:2]
    width = start_ref.shape[2]
    tile_odd = lax.rem(lax.axis_index("tile"), 2)
    inside = grid_ends()

    def edge(from_ref, first, count, z, factor, high):
        to = 3 + rows if high else 3 - count
        start_ref[z, to : to + count] = from_ref[first : first + count] * factor

    def beside(from_ref, high):
        factor = inside["high_y" if high else "low_y"]
        for z in range(depth):
            edge(from_ref, 3 * z, 3, 3 + z, factor, high)
        low_factor, high_factor = factor * inside["low_z"], factor * inside["high_z"]
        edge(from_ref, 12, 2, 2, low_factor, high)
        edge(from_ref, 14, 2, 3 + depth, high_factor, high)
        edge(from_ref, 16, 1, 1, low_factor, high)
        edge(from_ref, 17, 1, 4 + depth, high_factor, high)

    for parity in range(2):

        @pl.when(tile_odd == parity)
        def _():
            beside(row_odd_ref, parity == 1)
            beside(row_even_ref, parity == 0)

    relax = line_sweep(width, depth, rows, inside)

    def reader(inner_ref, outer_ref, level):
        def read(z, y):
            inner = 3 + level <= y < 3 + rows - level
            return inner_ref[z, y - 3] if inner else outer_ref[z, y]

        return read

    start = reader(inner_start_ref, start_ref, 0)
    one = reader(inner_one_ref, one_ref, 1)
    two = reader(inner_two_ref, two_ref, 2)

    def edge_lines(level):
        reach = SWEEPS - level
        for z in range(3 - reach, 3 + depth + reach):
            wide = reach - max(3 - z, z - 2 - depth, 0)
            for y in range(3 - wide, 3 + rows + wide):
                if not 3 + level <= y < 3 + rows - level:
                    yield z, y

    for z, y in edge_lines(1):
        one_ref[z, y] = relax(start, start, z, y)
    for z, y in edge_lines(2):
        two_ref[z, y] = relax(start, one, z, y)
    for z in range(depth):
        place = slice((z * rows + 3) * width, (z * rows + rows - 3) * width)
        last_ref[place, :] = inner_last_ref[place, :]
    for z, y in edge_lines(3):
        place = ((z - 3) * rows + y - 3) * width
        last_ref[place : place + width, :] = relax(start, two, z, y)

    sums = [jnp.zeros((8, LANES), F32) for _ in range(2 * MEM)]
    for z in range(depth):
        for row in range(0, rows, 8):
            for part in range(width):
                block = slice(row, row + 8), slice(part * LANES, (part + 1) * LANES)
                value = last_ref[pl.ds((z * rows + row) * width + part, 8, width), :]
                value *= keep_ref[z // 2, *block]
                grad_ref[z, *block] = value
                for i in range(MEM):
                    sums[i] += steps_ref[i, z, *block] * value
                    sums[MEM + i] += changes_ref[i, z, *block] * value
    done = 2 * len(PAIRS)
    total_ref[0:done, :] = sums_ref[0:done, :]
    for n, value in enumerate(sums):
        total_ref[done + n : done + n + 1, :] = jnp.sum(value, axis=0, keepdims=True)
    total_ref[done + 2 * MEM :, :] = jnp.zeros((SUMS - done - 2 * MEM, LANES), F32)
    totals = jnp.sum(total_ref[...], axis=1, keepdims=True)
    diagonal = lax.broadcasted_iota(jnp.int32, (SUMS, LANES), 0) == lax.broadcasted_iota(
        jnp.int32, (SUMS, LANES), 1
    )
    line = jnp.sum(jnp.where(diagonal, totals, 0.0), axis=0, keepdims=True)
    send_ref[...] = jnp.broadcast_to(line, send_ref.shape)


def combine_kernel(all_ref, grad_ref, steps_ref, changes_ref, out_hbm, out_ref, left):
    depth, rows, cols = grad_ref.shape
    line = jnp.sum(all_ref[...], axis=0, keepdims=True)

    def entry(n):
        return jnp.broadcast_to(line[:, n : n + 1], (8, LANES))

    sy = {pair: entry(n) for pair, n in SY.items()}
    yy = {pair: entry(n) for pair, n in YY.items()}
    inverse = [1.0 / sy[i, i] for i in range(MEM)]
    alphas = [None] * MEM
    for i in reversed(range(MEM)):
        product = entry(SG[i])
        for j in range(i + 1, MEM):
            product -= alphas[j] * sy[i, j]
        alphas[i] = product * inverse[i]
    scale = sy[MEM - 1, MEM - 1] / yy[MEM - 1, MEM - 1]
    weights = [None] * MEM
    for i in range(MEM):
        product = entry(YG[i])
        for j in range(MEM):
            product -= alphas[j] * yy[min(i, j), max(i, j)]
        product *= scale
        for j in range(i):
            product += weights[j] * sy[j, i]
        weights[i] = alphas[i] - product * inverse[i]
    on_changes = [scale * alphas[i] for i in range(MEM)]
    copies = [
        pltpu.make_async_copy(out_ref.at[z], out_hbm.at[z], left.at[z]) for z in range(depth)
    ]
    for z in range(depth):
        for row in range(0, rows, 8):
            for col in range(0, cols, LANES):
                lane = slice(col, col + LANES)
                value = -scale * grad_ref[z, row : row + 8, lane]
                for i in range(MEM):
                    value += on_changes[i] * changes_ref[i, z, row : row + 8, lane]
                    value -= weights[i] * steps_ref[i, z, row : row + 8, lane]
                out_ref[z, row : row + 8, lane] = value
        copies[z].start()
    for copy in copies:
        copy.wait()


def in_hbm(array):
    return pltpu.with_memory_space_constraint(array, pltpu.HBM)


def swaps():
    slabs, tiles = lax.axis_size("slab"), lax.axis_size("tile")
    places = [(slab, tile) for slab in range(slabs) for tile in range(tiles)]
    spare = max(slabs // 4, 1)

    def pairs(partner):
        targets = [partner(*place) for place in places]
        return [(i, slab * tiles + tile) for i, (slab, tile) in enumerate(targets)]

    def slab_odd(slab, tile):
        beside = slab + 1 if slab % 2 else slab - 1
        return (beside, tile) if 0 <= beside < slabs else (slab, tile ^ 1)

    def tile_odd(slab, tile):
        beside = tile + 1 if tile % 2 else tile - 1
        return (slab, beside) if 0 <= beside < tiles else (slab ^ spare, tile)

    return (
        pairs(slab_odd),
        pairs(lambda slab, tile: (slab ^ 1, tile)),
        pairs(tile_odd),
        pairs(lambda slab, tile: (slab, tile ^ 1)),
    )


def per_device(sensitivity, filtered_density, passive_blocks, history_steps, history_changes):
    shape = sensitivity.shape
    depth, rows, cols = shape
    like = jax.ShapeDtypeStruct
    width = cols // LANES
    lines, far, rim = (
        like((count * width, LANES), F32) for count in (depth * rows, 2 * rows, rows + 2)
    )
    edges = like((3 * depth + 6, width, LANES), F32)
    devices = lax.axis_size("slab") * lax.axis_size("tile")

    u, rim_odd, rim_even, far = pl.pallas_call(
        weight_kernel,
        out_shape=(lines, rim, rim, far),
        in_specs=[HBM] * 2,
        out_specs=[VMEM] * 4,
        scratch_shapes=[
            pltpu.VMEM(shape, F32),
            pltpu.VMEM(shape, F32),
            pltpu.SemaphoreType.DMA((2, depth)),
        ],
        compiler_params=kernel_params(8),
        name="weights",
    )(in_hbm(sensitivity), in_hbm(filtered_density))

    u = u.reshape(depth, rows, width, LANES)
    rim_odd, rim_even = (
        array.reshape(rows + 2, width, LANES) for array in (rim_odd, rim_even)
    )
    far = far.reshape(2, rows, width, LANES)

    slab_odd, slab_even, tile_odd, tile_even = swaps()
    rim_odd = lax.ppermute(rim_odd, MESH_AXES, slab_odd)
    rim_even = lax.ppermute(rim_even, MESH_AXES, slab_even)
    odd = lax.ppermute(far, MESH_AXES, slab_odd)
    even = lax.ppermute(far, MESH_AXES, slab_even)

    row_odd, row_even = pl.pallas_call(
        pack_kernel,
        out_shape=(edges, edges),
        in_specs=[VMEM] * 3,
        out_specs=[VMEM] * 2,
        compiler_params=kernel_params(8),
        name="edges",
    )(u, rim_odd, rim_even)
    row_odd = lax.ppermute(row_odd, MESH_AXES, tile_odd)
    row_even = lax.ppermute(row_even, MESH_AXES, tile_even)

    history = like(history_steps.shape, F32)
    sums, keep, steps, changes = pl.pallas_call(
        gram_kernel,
        out_shape=(
            like((SUMS, LANES), F32),
            like((depth // 2, rows, cols), F32),
            history,
            history,
        ),
        in_specs=[HBM] * 3,
        out_specs=[VMEM] * 4,
        scratch_shapes=[
            pltpu.VMEM(passive_blocks.shape, jnp.int32),
            pltpu.SemaphoreType.DMA((2, depth)),
            pltpu.SemaphoreType.DMA,
        ],
        compiler_params=kernel_params(8),
        cost_estimate=pl.CostEstimate(flops=8_000_000_000, bytes_accessed=43_000_000, transcendentals=0),
        name="gram",
    )(in_hbm(history_steps), in_hbm(history_changes), in_hbm(passive_blocks))

    field = like((depth + 6, rows, width, LANES), F32)
    inner = pl.pallas_call(
        inner_kernel,
        out_shape=(field, field, field, lines),
        in_specs=[VMEM] * 5,
        out_specs=[VMEM] * 4,
        compiler_params=kernel_params(8),
        name="inner",
    )(u, rim_odd, rim_even, odd, even)

    padded = pltpu.VMEM((depth + 6, rows + 6, width, LANES), F32)
    gradient, line = pl.pallas_call(
        outer_kernel,
        out_shape=(like(shape, F32), like((devices, LANES), F32)),
        in_specs=[VMEM] * 10,
        out_specs=[VMEM] * 2,
        scratch_shapes=[
            padded,
            padded,
            padded,
            pltpu.VMEM((depth * rows * width, LANES), F32),
            pltpu.VMEM((SUMS, LANES), F32),
        ],
        compiler_params=kernel_params(16),
        name="outer",
    )(row_odd, row_even, *inner, keep, steps, changes, sums)

    received = lax.all_to_all(line, MESH_AXES, 0, 0, tiled=True)

    return pl.pallas_call(
        combine_kernel,
        out_shape=like(shape, F32),
        in_specs=[VMEM] * 4,
        out_specs=HBM,
        scratch_shapes=[pltpu.VMEM(shape, F32), pltpu.SemaphoreType.DMA((depth,))],
        compiler_params=kernel_params(8),
        name="combine",
    )(received, gradient, steps, changes)


def solution(mesh):
    in_specs = (
        P("slab", "tile", None),
        P("slab", "tile", None),
        P("slab", "tile", None),
        P(None, "slab", "tile", None),
        P(None, "slab", "tile", None),
    )
    out_specs = P("slab", "tile", None)
    return jax.shard_map(
        per_device, mesh=mesh, in_specs=in_specs, out_specs=out_specs, check_vma=False
    )
```

```python
import jax
import jax.numpy as jnp
from jax import lax
from jax.experimental import pallas as pl
from jax.experimental.pallas import tpu as pltpu
from jax.sharding import PartitionSpec as P

SWEEPS = 3
MEM = 4

radius_square = 4.0
sharpness = 8.0
threshold = 0.5
diagonal_value = 1.0 + 6.0 * radius_square
coupling = radius_square / diagonal_value

F32 = jnp.float32
MESH_AXES = ("slab", "tile")
LANES = 128
PAIRS = [(i, j) for i in range(MEM) for j in range(i, MEM)]
SY = {pair: n for n, pair in enumerate(PAIRS)}
YY = {pair: len(PAIRS) + n for n, pair in enumerate(PAIRS)}
SG = [2 * len(PAIRS) + n for n in range(MEM)]
YG = [2 * len(PAIRS) + MEM + n for n in range(MEM)]
SUMS = 32

VMEM = pl.BlockSpec(memory_space=pltpu.VMEM)
HBM = pl.BlockSpec(memory_space=pltpu.HBM)


def kernel_params(mib):
    return pltpu.CompilerParams(vmem_limit_bytes=mib * 1024 * 1024)


def weight_kernel(
    sens_hbm,
    dens_hbm,
    u_ref,
    rim_odd_ref,
    rim_even_ref,
    odd_ref,
    even_ref,
    sens_ref,
    dens_ref,
    arrived,
):
    depth, rows, cols = sens_ref.shape
    width = cols // LANES
    layer = rows * width
    slab_odd = lax.rem(lax.axis_index("slab"), 2)
    copies = [
        [
            pltpu.make_async_copy(from_ref.at[z], to_ref.at[z], arrived.at[n, z])
            for n, (from_ref, to_ref) in enumerate(((sens_hbm, sens_ref), (dens_hbm, dens_ref)))
        ]
        for z in range(depth)
    ]
    for pair in copies:
        for copy in pair:
            copy.start()
    denominator = jnp.tanh(F32(sharpness * threshold)) + jnp.tanh(
        F32(sharpness * (1.0 - threshold))
    )
    for z in range(depth):
        for copy in copies[z]:
            copy.wait()
        bend = jnp.tanh(sharpness * (dens_ref[z] - threshold))
        slope = sharpness * (1.0 - bend * bend) / denominator
        value = sens_ref[z] * slope / diagonal_value
        for row in range(0, rows, 8):
            for part in range(width):
                place = pl.ds(z * layer + row * width + part, 8, width)
                u_ref[place, :] = value[row : row + 8, part * LANES : (part + 1) * LANES]

    for rim_ref, layers_ref, top in (
        (rim_odd_ref, odd_ref, slab_odd),
        (rim_even_ref, even_ref, 1 - slab_odd),
    ):

        def put(first, count, z, row):
            place = pl.ds(pl.multiple_of(z * layer + row * width, 8), count * width)
            rim_ref[first * width : (first + count) * width, :] = u_ref[place, :]

        near, second = (depth - 1) * top, 1 + (depth - 3) * top
        put(0, 2, near, 0)
        put(2, 2, near, rows - 2)
        put(4, 1, second, 0)
        put(5, 1, second, rows - 1)
        layers_ref[...] = u_ref[pl.ds(pl.multiple_of(top * layer, 8), SWEEPS * layer), :]


def gram_kernel(steps_ref, changes_ref, passive_ref, sums_ref, keep_ref):
    depth, rows, cols = steps_ref.shape[1:]

    def doubling(shape, dim):
        place = lax.broadcasted_iota(jnp.int32, shape, dim) // 2
        matches = place == lax.broadcasted_iota(jnp.int32, shape, 1 - dim)
        return matches.astype(F32).astype(jnp.bfloat16)

    half_rows = passive_ref.shape[1]
    twice_rows = doubling((2 * half_rows, half_rows), 0)
    twice_cols = doubling((LANES, 2 * LANES), 1)
    for z in range(passive_ref.shape[0]):
        blocks = passive_ref[z].astype(F32).astype(jnp.bfloat16)
        blocks = jnp.dot(twice_rows, blocks, preferred_element_type=F32).astype(jnp.bfloat16)
        for col in range(0, passive_ref.shape[2], LANES):
            wide = jnp.dot(
                blocks[:, col : col + LANES], twice_cols, preferred_element_type=F32
            )
            keep_ref[z, :, 2 * col : 2 * col + 2 * LANES] = 1.0 - wide

    sums = (jnp.zeros((8, LANES), F32),) * (2 * len(PAIRS))
    for z in range(depth):

        def step(block, sums):
            row = pl.ds(pl.multiple_of(block * 8, 8), 8)
            sums = list(sums)
            for col in range(0, cols, LANES):
                lane = pl.ds(col, LANES)
                s = [steps_ref[i, z, row, lane] for i in range(MEM)]
                y = [changes_ref[i, z, row, lane] for i in range(MEM)]
                for i, j in PAIRS:
                    sums[SY[i, j]] += s[i] * y[j]
                    sums[YY[i, j]] += y[i] * y[j]
            return tuple(sums)

        sums = lax.fori_loop(0, rows // 8, step, sums)
    for n, value in enumerate(sums):
        sums_ref[n : n + 1, :] = jnp.sum(value, axis=0, keepdims=True)


def pack_kernel(u_ref, odd_ref, even_ref, row_odd_ref, row_even_ref):
    depth, rows = u_ref.shape[:2]
    slab_odd = lax.rem(lax.axis_index("slab"), 2)
    tile_odd = lax.rem(lax.axis_index("tile"), 2)

    def pack(low_ref, high_ref, out_ref, top):
        start = rows - 3 if top else 0
        for z in range(depth):
            out_ref[3 * z : 3 * z + 3] = u_ref[z, start : start + 3]
        near, second = (2, 5) if top else (0, 4)
        out_ref[12:14] = low_ref[near : near + 2]
        out_ref[14:16] = high_ref[near : near + 2]
        out_ref[16] = low_ref[second]
        out_ref[17] = high_ref[second]

    for parity in range(2):
        for top in range(2):

            @pl.when((slab_odd == parity) & (tile_odd == top))
            def _():
                low_ref, high_ref = (even_ref, odd_ref) if parity else (odd_ref, even_ref)
                pack(low_ref, high_ref, row_odd_ref, top == 1)
                pack(low_ref, high_ref, row_even_ref, top == 0)


def grid_ends():
    slab, tile = lax.axis_index("slab"), lax.axis_index("tile")
    return {
        "low_z": (slab > 0).astype(F32),
        "high_z": (slab < lax.axis_size("slab") - 1).astype(F32),
        "low_y": (tile > 0).astype(F32),
        "high_y": (tile < lax.axis_size("tile") - 1).astype(F32),
    }


def line_sweep(width, depth, rows, inside):
    lane = lax.broadcasted_iota(jnp.int32, (width, LANES), 1)
    group = lax.broadcasted_iota(jnp.int32, (width, LANES), 0)
    lane_first, lane_last = lane == 0, lane == LANES - 1
    first, last = lane_first & (group == 0), lane_last & (group == width - 1)

    def relax(start, field, z, y):
        here = field(z, y)
        around = field(z - 1, y) + field(z + 1, y)
        around += field(z, y - 1) + field(z, y + 1)
        before, after = pltpu.roll(here, 1, 1), pltpu.roll(here, LANES - 1, 1)
        before = jnp.where(lane_first, pltpu.roll(before, 1, 0), before)
        after = jnp.where(lane_last, pltpu.roll(after, width - 1, 0), after)
        around += jnp.where(first, 0.0, before) + jnp.where(last, 0.0, after)
        value = start(z, y) + coupling * around
        if z < 3:
            value *= inside["low_z"]
        if z >= 3 + depth:
            value *= inside["high_z"]
        if y < 3:
            value *= inside["low_y"]
        if y >= 3 + rows:
            value *= inside["high_y"]
        return value

    return relax


def inner_kernel(u_ref, odd_ref, even_ref, start_ref, one_ref, two_ref, last_ref):
    depth, rows, width = u_ref.shape[:3]
    slab_odd = lax.rem(lax.axis_index("slab"), 2)
    inside = grid_ends()
    start_ref[3 : 3 + depth] = u_ref[...]
    for parity in range(2):

        @pl.when(slab_odd == parity)
        def _():
            low_ref, high_ref = (even_ref, odd_ref) if parity else (odd_ref, even_ref)
            start_ref[0:3] = low_ref[...] * inside["low_z"]
            start_ref[3 + depth :] = high_ref[...] * inside["high_z"]

    relax = line_sweep(width, depth, rows, inside)

    def reader(ref):
        return lambda z, y: ref[z, y - 3]

    start, one, two = reader(start_ref), reader(one_ref), reader(two_ref)
    for z in range(1, 5 + depth):
        for y in range(4, 2 + rows):
            one_ref[z, y - 3] = relax(start, start, z, y)
    for z in range(2, 4 + depth):
        for y in range(5, 1 + rows):
            two_ref[z, y - 3] = relax(start, one, z, y)
    for z in range(3, 3 + depth):
        for y in range(6, rows):
            place = ((z - 3) * rows + y - 3) * width
            last_ref[place : place + width, :] = relax(start, two, z, y)


def outer_kernel(
    row_odd_ref,
    row_even_ref,
    inner_start_ref,
    inner_one_ref,
    inner_two_ref,
    inner_last_ref,
    keep_ref,
    steps_ref,
    changes_ref,
    sums_ref,
    grad_ref,
    send_ref,
    start_ref,
    one_ref,
    two_ref,
    last_ref,
    total_ref,
):
    depth, rows = grad_ref.shape[:2]
    width = start_ref.shape[2]
    tile_odd = lax.rem(lax.axis_index("tile"), 2)
    inside = grid_ends()

    def edge(from_ref, first, count, z, factor, high):
        to = 3 + rows if high else 3 - count
        start_ref[z, to : to + count] = from_ref[first : first + count] * factor

    def beside(from_ref, high):
        factor = inside["high_y" if high else "low_y"]
        for z in range(depth):
            edge(from_ref, 3 * z, 3, 3 + z, factor, high)
        low_factor, high_factor = factor * inside["low_z"], factor * inside["high_z"]
        edge(from_ref, 12, 2, 2, low_factor, high)
        edge(from_ref, 14, 2, 3 + depth, high_factor, high)
        edge(from_ref, 16, 1, 1, low_factor, high)
        edge(from_ref, 17, 1, 4 + depth, high_factor, high)

    for parity in range(2):

        @pl.when(tile_odd == parity)
        def _():
            beside(row_odd_ref, parity == 1)
            beside(row_even_ref, parity == 0)

    relax = line_sweep(width, depth, rows, inside)

    def reader(inner_ref, outer_ref, level):
        def read(z, y):
            inner = 3 + level <= y < 3 + rows - level
            return inner_ref[z, y - 3] if inner else outer_ref[z, y]

        return read

    start = reader(inner_start_ref, start_ref, 0)
    one = reader(inner_one_ref, one_ref, 1)
    two = reader(inner_two_ref, two_ref, 2)

    def edge_lines(level):
        reach = SWEEPS - level
        for z in range(3 - reach, 3 + depth + reach):
            wide = reach - max(3 - z, z - 2 - depth, 0)
            for y in range(3 - wide, 3 + rows + wide):
                if not 3 + level <= y < 3 + rows - level:
                    yield z, y

    for z, y in edge_lines(1):
        one_ref[z, y] = relax(start, start, z, y)
    for z, y in edge_lines(2):
        two_ref[z, y] = relax(start, one, z, y)
    for z in range(depth):
        place = slice((z * rows + 3) * width, (z * rows + rows - 3) * width)
        last_ref[place, :] = inner_last_ref[place, :]
    for z, y in edge_lines(3):
        place = ((z - 3) * rows + y - 3) * width
        last_ref[place : place + width, :] = relax(start, two, z, y)

    sums = [jnp.zeros((8, LANES), F32) for _ in range(2 * MEM)]
    for z in range(depth):
        for row in range(0, rows, 8):
            for part in range(width):
                block = slice(row, row + 8), slice(part * LANES, (part + 1) * LANES)
                value = last_ref[pl.ds((z * rows + row) * width + part, 8, width), :]
                value *= keep_ref[z // 2, *block]
                grad_ref[z, *block] = value
                for i in range(MEM):
                    sums[i] += steps_ref[i, z, *block] * value
                    sums[MEM + i] += changes_ref[i, z, *block] * value
    done = 2 * len(PAIRS)
    total_ref[0:done, :] = sums_ref[0:done, :]
    for n, value in enumerate(sums):
        total_ref[done + n : done + n + 1, :] = jnp.sum(value, axis=0, keepdims=True)
    total_ref[done + 2 * MEM :, :] = jnp.zeros((SUMS - done - 2 * MEM, LANES), F32)
    totals = jnp.sum(total_ref[...], axis=1, keepdims=True)
    diagonal = lax.broadcasted_iota(jnp.int32, (SUMS, LANES), 0) == lax.broadcasted_iota(
        jnp.int32, (SUMS, LANES), 1
    )
    line = jnp.sum(jnp.where(diagonal, totals, 0.0), axis=0, keepdims=True)
    send_ref[...] = jnp.broadcast_to(line, send_ref.shape)


def combine_kernel(all_ref, grad_ref, steps_ref, changes_ref, out_hbm, out_ref, left):
    depth, rows, cols = grad_ref.shape
    line = jnp.sum(all_ref[...], axis=0, keepdims=True)

    def entry(n):
        return jnp.broadcast_to(line[:, n : n + 1], (8, LANES))

    sy = {pair: entry(n) for pair, n in SY.items()}
    yy = {pair: entry(n) for pair, n in YY.items()}
    inverse = [1.0 / sy[i, i] for i in range(MEM)]
    alphas = [None] * MEM
    for i in reversed(range(MEM)):
        product = entry(SG[i])
        for j in range(i + 1, MEM):
            product -= alphas[j] * sy[i, j]
        alphas[i] = product * inverse[i]
    scale = sy[MEM - 1, MEM - 1] / yy[MEM - 1, MEM - 1]
    weights = [None] * MEM
    for i in range(MEM):
        product = entry(YG[i])
        for j in range(MEM):
            product -= alphas[j] * yy[min(i, j), max(i, j)]
        product *= scale
        for j in range(i):
            product += weights[j] * sy[j, i]
        weights[i] = alphas[i] - product * inverse[i]
    on_changes = [scale * alphas[i] for i in range(MEM)]
    copies = [
        pltpu.make_async_copy(out_ref.at[z], out_hbm.at[z], left.at[z]) for z in range(depth)
    ]
    for z in range(depth):
        for row in range(0, rows, 8):
            for col in range(0, cols, LANES):
                lane = slice(col, col + LANES)
                value = -scale * grad_ref[z, row : row + 8, lane]
                for i in range(MEM):
                    value += on_changes[i] * changes_ref[i, z, row : row + 8, lane]
                    value -= weights[i] * steps_ref[i, z, row : row + 8, lane]
                out_ref[z, row : row + 8, lane] = value
        copies[z].start()
    for copy in copies:
        copy.wait()


def in_hbm(array):
    return pltpu.with_memory_space_constraint(array, pltpu.HBM)


def swaps():
    slabs, tiles = lax.axis_size("slab"), lax.axis_size("tile")
    places = [(slab, tile) for slab in range(slabs) for tile in range(tiles)]
    spare = max(slabs // 4, 1)

    def pairs(partner):
        targets = [partner(*place) for place in places]
        return [(i, slab * tiles + tile) for i, (slab, tile) in enumerate(targets)]

    def slab_odd(slab, tile):
        beside = slab + 1 if slab % 2 else slab - 1
        return (beside, tile) if 0 <= beside < slabs else (slab, tile ^ 1)

    def tile_odd(slab, tile):
        beside = tile + 1 if tile % 2 else tile - 1
        return (slab, beside) if 0 <= beside < tiles else (slab ^ spare, tile)

    return (
        pairs(slab_odd),
        pairs(lambda slab, tile: (slab ^ 1, tile)),
        pairs(tile_odd),
        pairs(lambda slab, tile: (slab, tile ^ 1)),
    )


def per_device(sensitivity, filtered_density, passive_blocks, history_steps, history_changes):
    shape = sensitivity.shape
    depth, rows, cols = shape
    like = jax.ShapeDtypeStruct
    width = cols // LANES
    lines, layers, rim = (
        like((count * width, LANES), F32) for count in (depth * rows, SWEEPS * rows, 6)
    )
    edges = like((3 * depth + 6, width, LANES), F32)
    devices = lax.axis_size("slab") * lax.axis_size("tile")

    u, rim_odd, rim_even, odd, even = pl.pallas_call(
        weight_kernel,
        out_shape=(lines, rim, rim, layers, layers),
        in_specs=[HBM] * 2,
        out_specs=[VMEM] * 5,
        scratch_shapes=[
            pltpu.VMEM(shape, F32),
            pltpu.VMEM(shape, F32),
            pltpu.SemaphoreType.DMA((2, depth)),
        ],
        compiler_params=kernel_params(8),
        name="weights",
    )(in_hbm(sensitivity), in_hbm(filtered_density))

    u = u.reshape(depth, rows, width, LANES)
    rim_odd, rim_even = (array.reshape(6, width, LANES) for array in (rim_odd, rim_even))
    odd, even = (array.reshape(SWEEPS, rows, width, LANES) for array in (odd, even))

    slab_odd, slab_even, tile_odd, tile_even = swaps()
    rim_odd = lax.ppermute(rim_odd, MESH_AXES, slab_odd)
    rim_even = lax.ppermute(rim_even, MESH_AXES, slab_even)
    odd = lax.ppermute(odd, MESH_AXES, slab_odd)
    even = lax.ppermute(even, MESH_AXES, slab_even)

    row_odd, row_even = pl.pallas_call(
        pack_kernel,
        out_shape=(edges, edges),
        in_specs=[VMEM] * 3,
        out_specs=[VMEM] * 2,
        compiler_params=kernel_params(8),
        cost_estimate=pl.CostEstimate(
            flops=8_000_000_000, bytes_accessed=43_000_000, transcendentals=0
        ),
        name="edges",
    )(u, rim_odd, rim_even)
    row_odd = lax.ppermute(row_odd, MESH_AXES, tile_odd)
    row_even = lax.ppermute(row_even, MESH_AXES, tile_even)

    sums, keep = pl.pallas_call(
        gram_kernel,
        out_shape=(like((SUMS, LANES), F32), like((depth // 2, rows, cols), F32)),
        in_specs=[VMEM] * 3,
        out_specs=[VMEM] * 2,
        compiler_params=kernel_params(8),
        cost_estimate=pl.CostEstimate(
            flops=8_000_000_000, bytes_accessed=43_000_000, transcendentals=0
        ),
        name="gram",
    )(history_steps, history_changes, passive_blocks)

    field = like((depth + 6, rows, width, LANES), F32)
    inner = pl.pallas_call(
        inner_kernel,
        out_shape=(field, field, field, lines),
        in_specs=[VMEM] * 3,
        out_specs=[VMEM] * 4,
        compiler_params=kernel_params(8),
        name="inner",
    )(u, odd, even)

    padded = pltpu.VMEM((depth + 6, rows + 6, width, LANES), F32)
    gradient, line = pl.pallas_call(
        outer_kernel,
        out_shape=(like(shape, F32), like((devices, LANES), F32)),
        in_specs=[VMEM] * 10,
        out_specs=[VMEM] * 2,
        scratch_shapes=[
            padded,
            padded,
            padded,
            pltpu.VMEM((depth * rows * width, LANES), F32),
            pltpu.VMEM((SUMS, LANES), F32),
        ],
        compiler_params=kernel_params(16),
        name="outer",
    )(row_odd, row_even, *inner, keep, history_steps, history_changes, sums)

    received = lax.all_to_all(line, MESH_AXES, 0, 0, tiled=True)

    return pl.pallas_call(
        combine_kernel,
        out_shape=like(shape, F32),
        in_specs=[VMEM] * 4,
        out_specs=HBM,
        scratch_shapes=[pltpu.VMEM(shape, F32), pltpu.SemaphoreType.DMA((depth,))],
        compiler_params=kernel_params(8),
        name="combine",
    )(received, gradient, history_steps, history_changes)


def solution(mesh):
    in_specs = (
        P("slab", "tile", None),
        P("slab", "tile", None),
        P("slab", "tile", None),
        P(None, "slab", "tile", None),
        P(None, "slab", "tile", None),
    )
    out_specs = P("slab", "tile", None)
    return jax.shard_map(
        per_device, mesh=mesh, in_specs=in_specs, out_specs=out_specs, check_vma=False
    )
```

```python
import jax
import jax.numpy as jnp
from jax import lax
from jax.experimental import pallas as pl
from jax.experimental.pallas import tpu as pltpu
from jax.sharding import PartitionSpec as P

SWEEPS = 3
MEM = 4

radius_square = 4.0
sharpness = 8.0
threshold = 0.5
diagonal_value = 1.0 + 6.0 * radius_square
coupling = radius_square / diagonal_value

F32 = jnp.float32
MESH_AXES = ("slab", "tile")
LANES = 128
PAIRS = [(i, j) for i in range(MEM) for j in range(i, MEM)]
SY = {pair: n for n, pair in enumerate(PAIRS)}
YY = {pair: len(PAIRS) + n for n, pair in enumerate(PAIRS)}
SG = [2 * len(PAIRS) + n for n in range(MEM)]
YG = [2 * len(PAIRS) + MEM + n for n in range(MEM)]
SUMS = 32

VMEM = pl.BlockSpec(memory_space=pltpu.VMEM)
HBM = pl.BlockSpec(memory_space=pltpu.HBM)


def kernel_params(mib):
    return pltpu.CompilerParams(vmem_limit_bytes=mib * 1024 * 1024)


def weight_kernel(
    sens_hbm,
    dens_hbm,
    u_ref,
    rim_odd_ref,
    rim_even_ref,
    far_ref,
    sens_ref,
    dens_ref,
    arrived,
):
    depth, rows, cols = sens_ref.shape
    width = cols // LANES
    layer = rows * width
    slab_odd = lax.rem(lax.axis_index("slab"), 2)
    copies = [
        [
            pltpu.make_async_copy(from_ref.at[z], to_ref.at[z], arrived.at[n, z])
            for n, (from_ref, to_ref) in enumerate(((sens_hbm, sens_ref), (dens_hbm, dens_ref)))
        ]
        for z in range(depth)
    ]
    for pair in copies:
        for copy in pair:
            copy.start()
    denominator = jnp.tanh(F32(sharpness * threshold)) + jnp.tanh(
        F32(sharpness * (1.0 - threshold))
    )
    for z in range(depth):
        for copy in copies[z]:
            copy.wait()
        bend = jnp.tanh(sharpness * (dens_ref[z] - threshold))
        slope = sharpness * (1.0 - bend * bend) / denominator
        value = sens_ref[z] * slope / diagonal_value
        for row in range(0, rows, 8):
            for part in range(width):
                place = pl.ds(z * layer + row * width + part, 8, width)
                u_ref[place, :] = value[row : row + 8, part * LANES : (part + 1) * LANES]

    for rim_ref, top in ((rim_odd_ref, slab_odd), (rim_even_ref, 1 - slab_odd)):

        def put(first, count, z, row):
            place = pl.ds(pl.multiple_of(z * layer + row * width, 8), count * width)
            rim_ref[first * width : (first + count) * width, :] = u_ref[place, :]

        near, second = (depth - 1) * top, 1 + (depth - 3) * top
        put(0, rows, near, 0)
        put(rows, 1, second, 0)
        put(rows + 1, 1, second, rows - 1)
    far_ref[...] = u_ref[layer : (depth - 1) * layer, :]


def gram_kernel(steps_ref, changes_ref, passive_ref, sums_ref, keep_ref):
    depth, rows, cols = steps_ref.shape[1:]

    def doubling(shape, dim):
        place = lax.broadcasted_iota(jnp.int32, shape, dim) // 2
        matches = place == lax.broadcasted_iota(jnp.int32, shape, 1 - dim)
        return matches.astype(F32).astype(jnp.bfloat16)

    half_rows = passive_ref.shape[1]
    twice_rows = doubling((2 * half_rows, half_rows), 0)
    twice_cols = doubling((LANES, 2 * LANES), 1)
    for z in range(passive_ref.shape[0]):
        blocks = passive_ref[z].astype(F32).astype(jnp.bfloat16)
        blocks = jnp.dot(twice_rows, blocks, preferred_element_type=F32).astype(jnp.bfloat16)
        for col in range(0, passive_ref.shape[2], LANES):
            wide = jnp.dot(
                blocks[:, col : col + LANES], twice_cols, preferred_element_type=F32
            )
            keep_ref[z, :, 2 * col : 2 * col + 2 * LANES] = 1.0 - wide

    sums = (jnp.zeros((8, LANES), F32),) * (2 * len(PAIRS))
    for z in range(depth):

        def step(block, sums):
            row = pl.ds(pl.multiple_of(block * 8, 8), 8)
            sums = list(sums)
            for col in range(0, cols, LANES):
                lane = pl.ds(col, LANES)
                s = [steps_ref[i, z, row, lane] for i in range(MEM)]
                y = [changes_ref[i, z, row, lane] for i in range(MEM)]
                for i, j in PAIRS:
                    sums[SY[i, j]] += s[i] * y[j]
                    sums[YY[i, j]] += y[i] * y[j]
            return tuple(sums)

        sums = lax.fori_loop(0, rows // 8, step, sums)
    for n, value in enumerate(sums):
        sums_ref[n : n + 1, :] = jnp.sum(value, axis=0, keepdims=True)


def pack_kernel(u_ref, odd_ref, even_ref, row_odd_ref, row_even_ref):
    depth, rows = u_ref.shape[:2]
    slab_odd = lax.rem(lax.axis_index("slab"), 2)
    tile_odd = lax.rem(lax.axis_index("tile"), 2)

    def pack(low_ref, high_ref, out_ref, top):
        start = rows - 3 if top else 0
        for z in range(depth):
            out_ref[3 * z : 3 * z + 3] = u_ref[z, start : start + 3]
        near, second = (rows - 2, rows + 1) if top else (0, rows)
        out_ref[12:14] = low_ref[near : near + 2]
        out_ref[14:16] = high_ref[near : near + 2]
        out_ref[16] = low_ref[second]
        out_ref[17] = high_ref[second]

    for parity in range(2):
        for top in range(2):

            @pl.when((slab_odd == parity) & (tile_odd == top))
            def _():
                low_ref, high_ref = (even_ref, odd_ref) if parity else (odd_ref, even_ref)
                pack(low_ref, high_ref, row_odd_ref, top == 1)
                pack(low_ref, high_ref, row_even_ref, top == 0)


def grid_ends():
    slab, tile = lax.axis_index("slab"), lax.axis_index("tile")
    return {
        "low_z": (slab > 0).astype(F32),
        "high_z": (slab < lax.axis_size("slab") - 1).astype(F32),
        "low_y": (tile > 0).astype(F32),
        "high_y": (tile < lax.axis_size("tile") - 1).astype(F32),
    }


def line_sweep(width, depth, rows, inside):
    lane = lax.broadcasted_iota(jnp.int32, (width, LANES), 1)
    group = lax.broadcasted_iota(jnp.int32, (width, LANES), 0)
    lane_first, lane_last = lane == 0, lane == LANES - 1
    first, last = lane_first & (group == 0), lane_last & (group == width - 1)

    def relax(start, field, z, y):
        here = field(z, y)
        around = field(z - 1, y) + field(z + 1, y)
        around += field(z, y - 1) + field(z, y + 1)
        before, after = pltpu.roll(here, 1, 1), pltpu.roll(here, LANES - 1, 1)
        before = jnp.where(lane_first, pltpu.roll(before, 1, 0), before)
        after = jnp.where(lane_last, pltpu.roll(after, width - 1, 0), after)
        around += jnp.where(first, 0.0, before) + jnp.where(last, 0.0, after)
        value = start(z, y) + coupling * around
        if z < 3:
            value *= inside["low_z"]
        if z >= 3 + depth:
            value *= inside["high_z"]
        if y < 3:
            value *= inside["low_y"]
        if y >= 3 + rows:
            value *= inside["high_y"]
        return value

    return relax


def inner_kernel(
    u_ref, rim_odd_ref, rim_even_ref, odd_ref, even_ref, start_ref, one_ref, two_ref, last_ref
):
    depth, rows, width = u_ref.shape[:3]
    slab_odd = lax.rem(lax.axis_index("slab"), 2)
    inside = grid_ends()
    start_ref[3 : 3 + depth] = u_ref[...]
    for parity in range(2):

        @pl.when(slab_odd == parity)
        def _():
            pairs = (rim_odd_ref, odd_ref), (rim_even_ref, even_ref)
            (low_rim, low_far), (high_rim, high_far) = pairs[::-1] if parity else pairs
            start_ref[0:2] = low_far[...] * inside["low_z"]
            start_ref[2] = low_rim[0:rows] * inside["low_z"]
            start_ref[3 + depth] = high_rim[0:rows] * inside["high_z"]
            start_ref[4 + depth :] = high_far[...] * inside["high_z"]

    relax = line_sweep(width, depth, rows, inside)

    def reader(ref):
        return lambda z, y: ref[z, y - 3]

    start, one, two = reader(start_ref), reader(one_ref), reader(two_ref)
    for z in range(1, 5 + depth):
        for y in range(4, 2 + rows):
            one_ref[z, y - 3] = relax(start, start, z, y)
    for z in range(2, 4 + depth):
        for y in range(5, 1 + rows):
            two_ref[z, y - 3] = relax(start, one, z, y)
    for z in range(3, 3 + depth):
        for y in range(6, rows):
            place = ((z - 3) * rows + y - 3) * width
            last_ref[place : place + width, :] = relax(start, two, z, y)


def outer_kernel(
    row_odd_ref,
    row_even_ref,
    inner_start_ref,
    inner_one_ref,
    inner_two_ref,
    inner_last_ref,
    keep_ref,
    steps_ref,
    changes_ref,
    sums_ref,
    grad_ref,
    send_ref,
    start_ref,
    one_ref,
    two_ref,
    last_ref,
    total_ref,
):
    depth, rows = grad_ref.shape[:2]
    width = start_ref.shape[2]
    tile_odd = lax.rem(lax.axis_index("tile"), 2)
    inside = grid_ends()

    def edge(from_ref, first, count, z, factor, high):
        to = 3 + rows if high else 3 - count
        start_ref[z, to : to + count] = from_ref[first : first + count] * factor

    def beside(from_ref, high):
        factor = inside["high_y" if high else "low_y"]
        for z in range(depth):
            edge(from_ref, 3 * z, 3, 3 + z, factor, high)
        low_factor, high_factor = factor * inside["low_z"], factor * inside["high_z"]
        edge(from_ref, 12, 2, 2, low_factor, high)
        edge(from_ref, 14, 2, 3 + depth, high_factor, high)
        edge(from_ref, 16, 1, 1, low_factor, high)
        edge(from_ref, 17, 1, 4 + depth, high_factor, high)

    for parity in range(2):

        @pl.when(tile_odd == parity)
        def _():
            beside(row_odd_ref, parity == 1)
            beside(row_even_ref, parity == 0)

    relax = line_sweep(width, depth, rows, inside)

    def reader(inner_ref, outer_ref, level):
        def read(z, y):
            inner = 3 + level <= y < 3 + rows - level
            return inner_ref[z, y - 3] if inner else outer_ref[z, y]

        return read

    start = reader(inner_start_ref, start_ref, 0)
    one = reader(inner_one_ref, one_ref, 1)
    two = reader(inner_two_ref, two_ref, 2)

    def edge_lines(level):
        reach = SWEEPS - level
        for z in range(3 - reach, 3 + depth + reach):
            wide = reach - max(3 - z, z - 2 - depth, 0)
            for y in range(3 - wide, 3 + rows + wide):
                if not 3 + level <= y < 3 + rows - level:
                    yield z, y

    for z, y in edge_lines(1):
        one_ref[z, y] = relax(start, start, z, y)
    for z, y in edge_lines(2):
        two_ref[z, y] = relax(start, one, z, y)
    for z in range(depth):
        place = slice((z * rows + 3) * width, (z * rows + rows - 3) * width)
        last_ref[place, :] = inner_last_ref[place, :]
    for z, y in edge_lines(3):
        place = ((z - 3) * rows + y - 3) * width
        last_ref[place : place + width, :] = relax(start, two, z, y)

    sums = [jnp.zeros((8, LANES), F32) for _ in range(2 * MEM)]
    for z in range(depth):
        for row in range(0, rows, 8):
            for part in range(width):
                block = slice(row, row + 8), slice(part * LANES, (part + 1) * LANES)
                value = last_ref[pl.ds((z * rows + row) * width + part, 8, width), :]
                value *= keep_ref[z // 2, *block]
                grad_ref[z, *block] = value
                for i in range(MEM):
                    sums[i] += steps_ref[i, z, *block] * value
                    sums[MEM + i] += changes_ref[i, z, *block] * value
    done = 2 * len(PAIRS)
    total_ref[0:done, :] = sums_ref[0:done, :]
    for n, value in enumerate(sums):
        total_ref[done + n : done + n + 1, :] = jnp.sum(value, axis=0, keepdims=True)
    total_ref[done + 2 * MEM :, :] = jnp.zeros((SUMS - done - 2 * MEM, LANES), F32)
    totals = jnp.sum(total_ref[...], axis=1, keepdims=True)
    diagonal = lax.broadcasted_iota(jnp.int32, (SUMS, LANES), 0) == lax.broadcasted_iota(
        jnp.int32, (SUMS, LANES), 1
    )
    line = jnp.sum(jnp.where(diagonal, totals, 0.0), axis=0, keepdims=True)
    send_ref[...] = jnp.broadcast_to(line, send_ref.shape)


def combine_kernel(all_ref, grad_ref, steps_ref, changes_ref, out_hbm, out_ref, left):
    depth, rows, cols = grad_ref.shape
    line = jnp.sum(all_ref[...], axis=0, keepdims=True)

    def entry(n):
        return jnp.broadcast_to(line[:, n : n + 1], (8, LANES))

    sy = {pair: entry(n) for pair, n in SY.items()}
    yy = {pair: entry(n) for pair, n in YY.items()}
    inverse = [1.0 / sy[i, i] for i in range(MEM)]
    alphas = [None] * MEM
    for i in reversed(range(MEM)):
        product = entry(SG[i])
        for j in range(i + 1, MEM):
            product -= alphas[j] * sy[i, j]
        alphas[i] = product * inverse[i]
    scale = sy[MEM - 1, MEM - 1] / yy[MEM - 1, MEM - 1]
    weights = [None] * MEM
    for i in range(MEM):
        product = entry(YG[i])
        for j in range(MEM):
            product -= alphas[j] * yy[min(i, j), max(i, j)]
        product *= scale
        for j in range(i):
            product += weights[j] * sy[j, i]
        weights[i] = alphas[i] - product * inverse[i]
    on_changes = [scale * alphas[i] for i in range(MEM)]
    copies = [
        pltpu.make_async_copy(out_ref.at[z], out_hbm.at[z], left.at[z]) for z in range(depth)
    ]
    for z in range(depth):
        for row in range(0, rows, 8):
            for col in range(0, cols, LANES):
                lane = slice(col, col + LANES)
                value = -scale * grad_ref[z, row : row + 8, lane]
                for i in range(MEM):
                    value += on_changes[i] * changes_ref[i, z, row : row + 8, lane]
                    value -= weights[i] * steps_ref[i, z, row : row + 8, lane]
                out_ref[z, row : row + 8, lane] = value
        copies[z].start()
    for copy in copies:
        copy.wait()


def in_hbm(array):
    return pltpu.with_memory_space_constraint(array, pltpu.HBM)


def swaps():
    slabs, tiles = lax.axis_size("slab"), lax.axis_size("tile")
    places = [(slab, tile) for slab in range(slabs) for tile in range(tiles)]
    spare = max(slabs // 4, 1)

    def pairs(partner):
        targets = [partner(*place) for place in places]
        return [(i, slab * tiles + tile) for i, (slab, tile) in enumerate(targets)]

    def slab_odd(slab, tile):
        beside = slab + 1 if slab % 2 else slab - 1
        return (beside, tile) if 0 <= beside < slabs else (slab, tile ^ 1)

    def tile_odd(slab, tile):
        beside = tile + 1 if tile % 2 else tile - 1
        return (slab, beside) if 0 <= beside < tiles else (slab ^ spare, tile)

    return (
        pairs(slab_odd),
        pairs(lambda slab, tile: (slab ^ 1, tile)),
        pairs(tile_odd),
        pairs(lambda slab, tile: (slab, tile ^ 1)),
    )


def per_device(sensitivity, filtered_density, passive_blocks, history_steps, history_changes):
    shape = sensitivity.shape
    depth, rows, cols = shape
    like = jax.ShapeDtypeStruct
    width = cols // LANES
    lines, far, rim = (
        like((count * width, LANES), F32) for count in (depth * rows, 2 * rows, rows + 2)
    )
    edges = like((3 * depth + 6, width, LANES), F32)
    devices = lax.axis_size("slab") * lax.axis_size("tile")

    u, rim_odd, rim_even, far = pl.pallas_call(
        weight_kernel,
        out_shape=(lines, rim, rim, far),
        in_specs=[HBM] * 2,
        out_specs=[VMEM] * 4,
        scratch_shapes=[
            pltpu.VMEM(shape, F32),
            pltpu.VMEM(shape, F32),
            pltpu.SemaphoreType.DMA((2, depth)),
        ],
        compiler_params=kernel_params(8),
        name="weights",
    )(in_hbm(sensitivity), in_hbm(filtered_density))

    u = u.reshape(depth, rows, width, LANES)
    rim_odd, rim_even = (
        array.reshape(rows + 2, width, LANES) for array in (rim_odd, rim_even)
    )
    far = far.reshape(2, rows, width, LANES)

    slab_odd, slab_even, tile_odd, tile_even = swaps()
    rim_odd = lax.ppermute(rim_odd, MESH_AXES, slab_odd)
    rim_even = lax.ppermute(rim_even, MESH_AXES, slab_even)
    odd = lax.ppermute(far, MESH_AXES, slab_odd)
    even = lax.ppermute(far, MESH_AXES, slab_even)

    row_odd, row_even = pl.pallas_call(
        pack_kernel,
        out_shape=(edges, edges),
        in_specs=[VMEM] * 3,
        out_specs=[VMEM] * 2,
        compiler_params=kernel_params(8),
        cost_estimate=pl.CostEstimate(
            flops=8_000_000_000, bytes_accessed=43_000_000, transcendentals=0
        ),
        name="edges",
    )(u, rim_odd, rim_even)
    row_odd = lax.ppermute(row_odd, MESH_AXES, tile_odd)
    row_even = lax.ppermute(row_even, MESH_AXES, tile_even)

    sums, keep = pl.pallas_call(
        gram_kernel,
        out_shape=(like((SUMS, LANES), F32), like((depth // 2, rows, cols), F32)),
        in_specs=[VMEM] * 3,
        out_specs=[VMEM] * 2,
        compiler_params=kernel_params(8),
        cost_estimate=pl.CostEstimate(
            flops=8_000_000_000, bytes_accessed=43_000_000, transcendentals=0
        ),
        name="gram",
    )(history_steps, history_changes, passive_blocks)

    field = like((depth + 6, rows, width, LANES), F32)
    inner = pl.pallas_call(
        inner_kernel,
        out_shape=(field, field, field, lines),
        in_specs=[VMEM] * 5,
        out_specs=[VMEM] * 4,
        compiler_params=kernel_params(8),
        name="inner",
    )(u, rim_odd, rim_even, odd, even)

    padded = pltpu.VMEM((depth + 6, rows + 6, width, LANES), F32)
    gradient, line = pl.pallas_call(
        outer_kernel,
        out_shape=(like(shape, F32), like((devices, LANES), F32)),
        in_specs=[VMEM] * 10,
        out_specs=[VMEM] * 2,
        scratch_shapes=[
            padded,
            padded,
            padded,
            pltpu.VMEM((depth * rows * width, LANES), F32),
            pltpu.VMEM((SUMS, LANES), F32),
        ],
        compiler_params=kernel_params(16),
        name="outer",
    )(row_odd, row_even, *inner, keep, history_steps, history_changes, sums)

    received = lax.all_to_all(line, MESH_AXES, 0, 0, tiled=True)

    return pl.pallas_call(
        combine_kernel,
        out_shape=like(shape, F32),
        in_specs=[VMEM] * 4,
        out_specs=HBM,
        scratch_shapes=[pltpu.VMEM(shape, F32), pltpu.SemaphoreType.DMA((depth,))],
        compiler_params=kernel_params(8),
        name="combine",
    )(received, gradient, history_steps, history_changes)


def solution(mesh):
    in_specs = (
        P("slab", "tile", None),
        P("slab", "tile", None),
        P("slab", "tile", None),
        P(None, "slab", "tile", None),
        P(None, "slab", "tile", None),
    )
    out_specs = P("slab", "tile", None)
    return jax.shard_map(
        per_device, mesh=mesh, in_specs=in_specs, out_specs=out_specs, check_vma=False
    )
```
